128 devices in a mesh: tm: 4 (over z), space: 32 (over y, x, core).
Axes of the slice: x: 4, y: 4, z: 4, core: 2. Of those that a mesh axis runs over, the one named last changes fastest.
Arguments:
- latents: bfloat16 [8, 32, 120, 512], P('tm', 'space'), may hold values from -8 to 8
- spatial_weight: bfloat16 [4608, 512], replicated, may hold values from -0.09375 to 0.09375
- temporal_weight: bfloat16 [1536, 512], replicated, may hold values from -0.15625 to 0.15625
- qkv_weight: bfloat16 [512, 1536], replicated, may hold values from -0.25 to 0.25
- out_weight: bfloat16 [512, 512], replicated, may hold values from -0.25 to 0.25
- cotangent: bfloat16 [8, 32, 120, 512], P('tm', 'space'), may hold values from -6 to 6
Outputs:
- mixed: bfloat16 [8, 32, 120, 512], P('tm', 'space')
- grad_latents: bfloat16 [8, 32, 120, 512], P('tm', 'space')
- grad_weights: float32 [8192, 512], P(('tm', 'space'))
The draws below stay inside these ranges and needn't reach their ends.
All inputs are finite; a program needn't handle non-finite values.
Results may differ from the reference program's by a relative error of at most 0.012.
The reference program's roundings to bfloat16 on the way count: a program that leaves them out, or rounds other values in their place, can miss the bound.
Values may be sent and summed in bfloat16 or wider, within the bound.
No kernel may reach another device: no remote copies, remote signals or barrier semaphores. Data moves between devices by JAX's collectives and lax.ppermute only.
A program may use at most 128 MiB of HBM per device.

```python
import math
import jax
import jax.numpy as jnp
from jax import lax

C = 512
HEADS = 16
W = 120
FRAMES = 8
ROWS = 32


def draw_latents(key, part):
    key = jax.random.fold_in(key, 11)
    key_base = jax.random.fold_in(key, 0)
    shape = (FRAMES, ROWS, W, C)
    values = jnp.clip(jax.random.normal(key_base, shape, jnp.float32), -6.0, 6.0)
    return values.astype(jnp.bfloat16)


def draw_qkv_weight(key, part):
    key = jax.random.fold_in(key, 23)
    key_base = jax.random.fold_in(key, 0)
    spread = 1.0 / math.sqrt(C)
    values = jnp.clip(jnp.clip(jax.random.normal(key_base, (C, 3 * C), jnp.float32), -5.0, 5.0) * spread, -0.25, 0.25)
    return values.astype(jnp.bfloat16)


def block_scale(stream_key, dims, cuts, low, top_value):
    def one(axis_at, blocks):
        heights = jax.random.uniform(jax.random.fold_in(jax.random.fold_in(stream_key, 6), axis_at), (blocks,), jnp.float32, low / len(cuts), top_value / len(cuts))
        return jnp.repeat(jnp.exp(heights), dims[axis_at] // blocks).reshape((-1,) + (1,) * (len(dims) - axis_at - 1))

    level = one(*cuts[0])
    for cut in cuts[1:]:
        level = level * one(*cut)
    return level


def scatter_about(stream_key, dims, scale, most, cuts=(), kind=jnp.bfloat16):
    drawn = jax.random.normal(stream_key, dims, jnp.float32) * scale
    if len(cuts) > 0:
        drawn = block_scale(stream_key, dims, cuts, -0.22, 0.18) * drawn
    return jnp.clip(drawn, min=-most, max=most).astype(kind)


def setup_inputs(seed: int = 0) -> dict:
    key_of = jax.random.split(jax.random.key(seed), 7)
    latents = draw_latents(jax.random.fold_in(key_of[6], 71), 0)
    spatial_weight = scatter_about(key_of[1], (9 * C, C), (9 * C) ** -0.5, 0.09375)
    temporal_weight = scatter_about(key_of[2], (3 * C, C), (3 * C) ** -0.5, 0.15625)
    qkv_weight = draw_qkv_weight(jax.random.fold_in(key_of[6], 71), 0)
    out_weight = scatter_about(key_of[4], (C, C), C ** -0.5, 0.25)
    cotangent = scatter_about(key_of[5], (FRAMES, ROWS, W, C), 1.0, 6.0, ((0, 4), (1, 32)))
    return {"latents": latents, "spatial_weight": spatial_weight, "temporal_weight": temporal_weight, "qkv_weight": qkv_weight, "out_weight": out_weight, "cotangent": cotangent}


def block_size(total):
    best = 1
    for cand in range(1, min(total, 1024) + 1):
        if total % cand == 0:
            best = cand
    return best

def silu_slope(value):
    sigma = jax.nn.sigmoid(value)
    return sigma * (1.0 + value * (1.0 - sigma))

def matmul(left, right):
    return jnp.dot(left.astype(jnp.float32), right.astype(jnp.float32))

def inner_rows(left, right):
    return lax.dot_general(left.astype(jnp.float32), right.astype(jnp.float32), (((0,), (0,)), ((), ())))

def transposed(left, right):
    return lax.dot_general(left.astype(jnp.float32), right.astype(jnp.float32), (((1,), (1,)), ((), ())))

def tap_back(patches, weight, taps):
    chans = weight.shape[1]
    return jnp.einsum('tpc,pdc->td', patches.reshape(-1, taps, chans).astype(jnp.float32), weight.reshape(taps, chans, chans).astype(jnp.float32))

def taps_of(padded, rows, width, flip):
    pieces = []
    for first in range(3):
        for second in range(3):
            top = 2 - first if flip else first
            left = 2 - second if flip else second
            pieces.append(padded[:, top:top + rows, left:left + width, :])
    return jnp.concatenate(pieces, axis=-1)

def softmax_rows(queries, keys, scale):
    scores = inner_rows(queries, keys) * scale
    peak = lax.optimization_barrier(jnp.max(scores, axis=1, keepdims=True))
    expo = jnp.exp(scores - peak)
    return expo / lax.optimization_barrier(jnp.sum(expo, axis=1, keepdims=True))

def attend(item, width_head, scale, qblock):
    tokf = item.shape[1]
    keys = item[width_head:2 * width_head]
    values = item[2 * width_head:]
    nblk = tokf // qblock
    qparts = item[:width_head].reshape(width_head, nblk, qblock).transpose(1, 0, 2)

    def one_block(qpart):
        probs = softmax_rows(qpart, keys, scale).astype(jnp.bfloat16)
        return transposed(values, probs)
    outs = lax.map(one_block, qparts)
    return outs.transpose(1, 0, 2).reshape(width_head, tokf).astype(jnp.bfloat16)

def attend_back(item, grad_out, width_head, scale, qblock):
    tokf = item.shape[1]
    keys = item[width_head:2 * width_head]
    values = item[2 * width_head:]
    nblk = tokf // qblock
    qparts = item[:width_head].reshape(width_head, nblk, qblock).transpose(1, 0, 2)
    gparts = grad_out.reshape(width_head, nblk, qblock).transpose(1, 0, 2)

    def one_block(carry, pair):
        qpart, gpart = pair
        probs = softmax_rows(qpart, keys, scale)
        rounded = probs.astype(jnp.bfloat16)
        dprobs = inner_rows(gpart, values)
        delta = lax.optimization_barrier(jnp.sum(probs * dprobs, axis=1, keepdims=True))
        dscores = (probs * (dprobs - delta)).astype(jnp.bfloat16)
        dquery = transposed(keys, dscores) * scale
        dkeys = carry[0] + matmul(qpart, dscores) * scale
        dvalues = carry[1] + matmul(gpart, rounded)
        return ((dkeys, dvalues), dquery)
    zero = jnp.zeros((width_head, tokf), jnp.float32)
    (dkeys, dvalues), dqs = lax.scan(one_block, (zero, zero), (qparts, gparts))
    dquery = dqs.transpose(1, 0, 2).reshape(width_head, tokf)
    return jnp.concatenate([dquery, dkeys, dvalues], axis=0).astype(jnp.bfloat16)

def reference(latents, spatial_weight, temporal_weight, qkv_weight, out_weight, cotangent):
    frames, rows, width, chans = latents.shape
    shape = latents.shape
    width_head = chans // HEADS
    tokf = rows * width
    scale = 1.0 / math.sqrt(width_head)
    norm = 1.0 / math.sqrt(frames * rows * width)
    qblock = block_size(tokf)
    xfull = latents.astype(jnp.float32)
    act = jax.nn.silu(xfull).astype(jnp.bfloat16)
    apad = jnp.pad(act, ((0, 0), (1, 1), (1, 1), (0, 0)))
    apatch = taps_of(apad, rows, width, False).reshape(-1, 9 * chans)
    pre = matmul(apatch, spatial_weight).reshape(shape)
    bact = jax.nn.silu(pre).astype(jnp.bfloat16)
    bext = jnp.concatenate([jnp.zeros((2, rows, width, chans), jnp.bfloat16), bact], axis=0)
    bpatch = jnp.concatenate([bext[k:k + frames] for k in range(3)], axis=-1).reshape(-1, 3 * chans)
    resid = xfull + matmul(bpatch, temporal_weight).reshape(shape)
    rflat = resid.astype(jnp.bfloat16).reshape(-1, chans)
    qkv = matmul(rflat, qkv_weight).astype(jnp.bfloat16)
    items = qkv.reshape(frames, tokf, 3, HEADS, width_head).transpose(0, 3, 2, 4, 1).reshape(frames * HEADS, 3 * width_head, tokf)
    outs = lax.map(lambda item: attend(item, width_head, scale, qblock), items)
    attn = outs.reshape(frames, HEADS, width_head, tokf).transpose(0, 3, 1, 2).reshape(-1, chans)
    mixed = (resid + matmul(attn, out_weight).reshape(shape)).astype(jnp.bfloat16)
    gflat = cotangent.reshape(-1, chans)
    grad_out = inner_rows(attn, gflat) * norm
    dattn = transposed(gflat, out_weight).astype(jnp.bfloat16)
    ditems = dattn.reshape(frames, tokf, HEADS, width_head).transpose(0, 2, 3, 1).reshape(frames * HEADS, width_head, tokf)
    dqkv_items = lax.map(lambda pair: attend_back(pair[0], pair[1], width_head, scale, qblock), (items, ditems))
    dqkv = dqkv_items.reshape(frames, HEADS, 3, width_head, tokf).transpose(0, 4, 2, 1, 3).reshape(-1, 3 * chans)
    grad_qkv = inner_rows(rflat, dqkv) * norm
    dres = cotangent.astype(jnp.float32) + transposed(dqkv, qkv_weight).reshape(shape)
    dresb = dres.astype(jnp.bfloat16)
    grad_temporal = inner_rows(bpatch, dresb.reshape(-1, chans)) * norm
    dext = jnp.concatenate([dresb, jnp.zeros((2, rows, width, chans), jnp.bfloat16)], axis=0)
    dpatch = jnp.concatenate([dext[2 - k:2 - k + frames] for k in range(3)], axis=-1)
    dpre = (tap_back(dpatch, temporal_weight, 3).reshape(shape) * silu_slope(pre)).astype(jnp.bfloat16)
    grad_spatial = inner_rows(apatch, dpre.reshape(-1, chans)) * norm
    dpad = jnp.pad(dpre, ((0, 0), (1, 1), (1, 1), (0, 0)))
    spatch = taps_of(dpad, rows, width, True)
    dact = tap_back(spatch, spatial_weight, 9).reshape(shape)
    grad_latents = (dres + dact * silu_slope(xfull)).astype(jnp.bfloat16)
    grad_weights = jnp.concatenate([grad_spatial, grad_temporal, grad_qkv.reshape(3 * chans, chans), grad_out], axis=0)
    return (mixed, grad_latents, grad_weights)
```

```python
import functools
import math

import jax
import jax.numpy as jnp
from jax import lax
from jax.experimental import pallas as pl
from jax.experimental.pallas import tpu as pltpu
from jax.sharding import PartitionSpec as P

HEADS = 16
F32 = jnp.float32
BF = jnp.bfloat16
NT = (((1,), (1,)), ((), ()))

def attn_kernel(scale, tq, ck, un, x_ref, o_ref, a_ref, kt_ref, vt_ref, s_ref, e_ref, acc_ref):
    tok = x_ref.shape[0]
    step = pl.program_id(0)
    nck = tok // ck
    d = 32
    @pl.when(step == 0)
    def _():
        k = x_ref[:, d:2*d]
        v = x_ref[:, 2*d:3*d]
        lane = lax.broadcasted_iota(jnp.int32, (tok, d), 1)
        ones = jnp.where(lane < 3, 1.0, 0.0).astype(BF)
        a_ref[...] = jnp.concatenate([k, k, v, ones], axis=1)
        kt_ref[...] = k.astype(F32).T.astype(BF)
        vt_ref[...] = jnp.concatenate([v, ones], axis=1).astype(F32).T.astype(BF)
        acc_ref[...] = jnp.zeros_like(acc_ref)
    rows = pl.ds(pl.multiple_of(step * tq, tq), tq)
    xb = x_ref[rows, :]
    q = xb[:, 0:d].astype(F32)
    do = xb[:, 3*d:4*d].astype(F32)
    zeros = jnp.zeros((tq, 2*d), BF)
    def split(z):
        hi = z.astype(BF)
        lo = (z - hi.astype(F32)).astype(BF)
        return hi, lo
    qh, ql = split(q * (scale * math.log2(math.e)))
    wq = jnp.concatenate([qh, ql, zeros], axis=1)
    def p1(i, m):
        r = pl.ds(pl.multiple_of(i * ck, ck), ck)
        s = lax.dot_general(a_ref[r, :], wq, NT, preferred_element_type=F32)
        s_ref[r, :] = s
        return jnp.maximum(m, jnp.max(s.reshape(ck // 8, 8, tq), axis=0))
    m = lax.fori_loop(0, nck, p1, jnp.full((8, tq), -jnp.inf, F32), unroll=un)
    m = jnp.max(m, axis=0, keepdims=True)
    def p2(i, o):
        r = pl.ds(pl.multiple_of(i * ck, ck), ck)
        e = jnp.exp2(s_ref[r, :] - m)
        s_ref[r, :] = e
        eb = e.astype(BF)
        e_ref[r, :] = eb
        return o + jnp.dot(vt_ref[:, r], eb, preferred_element_type=F32)
    o = lax.fori_loop(0, nck, p2, jnp.zeros((2*d, tq), F32), unroll=un)
    inv = 1.0 / o[d:d+1, :]
    ot = o[:d] * inv
    ob = ot.T
    delta = jnp.sum(ob * do, axis=1, keepdims=True)
    invc = jnp.broadcast_to(inv, (8, tq)).T[:, 0:1]
    dh = (-delta).astype(BF); dr = -delta - dh.astype(F32)
    dm = dr.astype(BF); dl = (dr - dm.astype(F32)).astype(BF)
    lane = lax.broadcasted_iota(jnp.int32, (tq, d), 1)
    dd = jnp.where(lane == 0, dh.astype(F32), jnp.where(lane == 1, dm.astype(F32), jnp.where(lane == 2, dl.astype(F32), 0.0))).astype(BF)
    wd = jnp.concatenate([zeros, xb[:, 3*d:], dd], axis=1)
    gh, gl = split(do * invc)
    rh, rl = split(q * (invc * scale))
    we = jnp.concatenate([zeros, gh, gl], axis=1)
    ws = jnp.concatenate([rh, rl, zeros], axis=1)
    def p3(i, dq):
        r = pl.ds(pl.multiple_of(i * ck, ck), ck)
        dp = lax.dot_general(a_ref[r, :], wd, NT, preferred_element_type=F32)
        ds = (s_ref[r, :] * dp).astype(BF)
        acc_ref[r, :] += (jnp.dot(ds, ws, preferred_element_type=F32)
                          + jnp.dot(e_ref[r, :], we, preferred_element_type=F32))
        return dq + jnp.dot(kt_ref[:, r], ds, preferred_element_type=F32)
    dq = lax.fori_loop(0, nck, p3, jnp.zeros((d, tq), F32), unroll=un)
    dq = dq * (inv * scale)
    o_ref[rows, 0:2*d] = jnp.concatenate([ot, dq], axis=0).T.astype(BF)
    @pl.when(step == pl.num_programs(0) - 1)
    def _():
        acc = acc_ref[...]
        dk = acc[:, :d] + acc[:, d:2*d]
        dv = acc[:, 2*d:3*d] + acc[:, 3*d:]
        o_ref[:, 2*d:] = jnp.concatenate([dk, dv], axis=1).astype(BF)

def attn(x, tq=256, ck=256, un=15):
    tok = x.shape[0]
    return pl.pallas_call(
        functools.partial(attn_kernel, 1.0/math.sqrt(32), tq, ck, un),
        grid=(tok // tq,),
        in_specs=[pl.BlockSpec((tok, 128), lambda i: (0, 0))],
        out_specs=pl.BlockSpec((tok, 128), lambda i: (0, 0)),
        out_shape=jax.ShapeDtypeStruct((tok, 128), BF),
        scratch_shapes=[pltpu.VMEM((tok, 128), BF), pltpu.VMEM((32, tok), BF), pltpu.VMEM((64, tok), BF),
                        pltpu.VMEM((tok, tq), F32), pltpu.VMEM((tok, tq), BF), pltpu.VMEM((tok, 128), F32)],
        compiler_params=pltpu.CompilerParams(vmem_limit_bytes=48 << 20),
        cost_estimate=pl.CostEstimate(flops=6*2*tok*tok*128, bytes_accessed=4*tok*128, transcendentals=tok*tok),
    )(x)


def silu_slope(value):
    sigma = jax.nn.sigmoid(value)
    return sigma * (1.0 + value * (1.0 - sigma))


def matmul(left, right):
    return jnp.dot(left, right, preferred_element_type=F32)


def inner_rows(left, right):
    return lax.dot_general(left, right, (((0,), (0,)), ((), ())), preferred_element_type=F32)


def transposed(left, right):
    return lax.dot_general(left, right, NT, preferred_element_type=F32)


def shift(x, axis, by):
    count = lax.axis_size(axis)
    pairs = [(i, i + by) for i in range(count) if 0 <= i + by < count]
    return lax.ppermute(x, axis, pairs)


def swap(x):
    count = lax.axis_size("space")
    return lax.ppermute(x, "space", [(i, i ^ 1) for i in range(count)])


def with_halo(field):
    return jnp.stack([shift(field, "space", 1), field, shift(field, "space", -1)], axis=1)


def side_pad(field):
    return jnp.pad(field, ((0, 0), (0, 0), (1, 1), (0, 0)))


def taps_of(padded, width):
    pieces = [padded[:, i, j : j + width] for i in range(3) for j in range(3)]
    return jnp.concatenate(pieces, axis=-1).reshape(-1, 9 * padded.shape[-1])


def per_device(latents, spatial_weight, temporal_weight, qkv_weight, out_weight, cotangent):
    frames, rows, width, chans = latents.shape
    ntok = frames * width
    n_space = lax.axis_size("space")
    n_time = lax.axis_size("tm")
    depth = chans // HEADS
    norm = 1.0 / math.sqrt(ntok * n_space * n_time)
    core = lax.axis_index("space") % 2
    half = chans // 2

    def halves(field):
        parts = field.reshape(field.shape[0], -1, 2, half)
        own = lax.dynamic_index_in_dim(parts, core, 2, keepdims=False)
        other = lax.dynamic_index_in_dim(parts, 1 - core, 2, keepdims=False)
        both = jnp.concatenate([own, swap(other)], axis=0)
        return both.reshape(both.shape[0], -1)

    def pair(field):
        return jnp.concatenate([field, swap(field)], axis=0)

    x = latents.reshape(frames, width, chans)
    xf = x.astype(F32)
    cot = cotangent.reshape(ntok, chans)
    act = jax.nn.silu(xf).astype(BF)
    ahalo = side_pad(with_halo(act))
    pre = matmul(taps_of(ahalo, width), spatial_weight)
    bact = jax.nn.silu(pre).astype(BF).reshape(frames, width, chans)
    bext = jnp.concatenate([shift(bact, "tm", 1), bact], axis=0)
    bpatch = jnp.concatenate([bext[k : k + frames] for k in range(3)], axis=-1).reshape(ntok, 3 * chans)
    resid = xf.reshape(ntok, chans) + matmul(bpatch, temporal_weight)
    rflat = resid.astype(BF)
    qkv = matmul(rflat, qkv_weight).astype(BF)
    dattn = transposed(cot, out_weight).astype(BF)
    items = jnp.concatenate([qkv, dattn], axis=1).reshape(frames, width, 4, HEADS, depth)
    items = items.transpose(0, 3, 1, 2, 4).reshape(frames * HEADS, width, 4 * depth)
    items = lax.all_to_all(items, "space", 0, 0, tiled=True)
    outs = attn(items.reshape(n_space * width, 4 * depth)).reshape(n_space, width, 4 * depth)
    outs = lax.all_to_all(outs, "space", 0, 0, tiled=True)
    outs = outs.reshape(frames, HEADS, width, 4, depth).transpose(0, 2, 3, 1, 4).reshape(ntok, 4 * chans)
    atted = outs[:, :chans]
    dqkv = outs[:, chans:]
    mixed = (resid + matmul(atted, out_weight)).astype(BF).reshape(latents.shape)

    dres = cot.astype(F32) + transposed(dqkv, qkv_weight)
    dresb = dres.astype(BF)
    dthree = dresb.reshape(frames, width, chans)
    dext = jnp.concatenate([dthree, shift(dthree, "tm", -1)], axis=0)
    tw = temporal_weight.reshape(3, chans, chans)
    dbact = sum(transposed(dext[2 - k : 2 - k + frames].reshape(ntok, chans), tw[k]) for k in range(3))
    dpre = (dbact * silu_slope(pre)).astype(BF)
    dhalo = side_pad(with_halo(dpre.reshape(frames, width, chans)))
    sw = spatial_weight.reshape(3, 3, chans, chans)
    dact = sum(
        transposed(dhalo[:, 2 - i, 2 - j : 2 - j + width].reshape(ntok, chans), sw[i, j])
        for i in range(3)
        for j in range(3)
    )
    grad_latents = (dres + dact * silu_slope(xf.reshape(ntok, chans))).astype(BF).reshape(latents.shape)

    apair = taps_of(pair(ahalo), width)
    bpair = pair(bext).reshape(2, 2 * frames, width, chans)
    bpair = jnp.concatenate([bpair[:, k : k + frames] for k in range(3)], axis=-1).reshape(2 * ntok, 3 * chans)
    terms = [
        inner_rows(apair, halves(dpre)),
        inner_rows(bpair, halves(dresb)),
        inner_rows(pair(rflat), halves(dqkv)).reshape(3 * chans, half),
        inner_rows(pair(atted), halves(cot)),
    ]
    terms = jnp.concatenate([term.astype(BF) for term in terms], axis=0)
    owners = n_space * n_time
    terms = lax.all_to_all(terms.reshape(owners, -1, half), ("tm", "space"), 0, 0, tiled=True)
    summed = jnp.sum(terms.reshape(owners // 2, 2, -1, half).astype(F32), axis=0)
    grad_weights = summed.transpose(1, 0, 2).reshape(-1, chans) * norm
    return (mixed, grad_latents, grad_weights)


def solution(mesh):
    placed = (P("tm", "space", None, None), P(), P(), P(), P(), P("tm", "space", None, None))
    return jax.shard_map(
        per_device,
        mesh=mesh,
        in_specs=placed,
        out_specs=(
            P("tm", "space", None, None),
            P("tm", "space", None, None),
            P(("tm", "space"), None),
        ),
        check_vma=False,
    )
```

```python
import functools
import math

import jax
import jax.numpy as jnp
from jax import lax
from jax.experimental import pallas as pl
from jax.experimental.pallas import tpu as pltpu
from jax.sharding import PartitionSpec as P

HEADS = 16
F32 = jnp.float32
BF = jnp.bfloat16
NT = (((1,), (1,)), ((), ()))

def dot_nt(left, right):
    return lax.dot_general(left, right, NT, preferred_element_type=F32)


def proj_kernel(x_ref, bext_ref, cot_ref, tw_ref, qw_ref, ow_ref, resid_ref, rres_ref, items_ref):
    frames, width, chans = x_ref.shape
    d = chans // HEADS
    for f in range(frames):
        acc = x_ref[f].astype(F32)
        for k in range(3):
            tap = tw_ref[k * chans : (k + 1) * chans, :]
            acc = acc + jnp.dot(bext_ref[f + k], tap, preferred_element_type=F32)
        resid_ref[f] = acc
        rounded = acc.astype(BF)
        rres_ref[f] = rounded
        qkv = jnp.dot(rounded, qw_ref[...], preferred_element_type=F32)
        dattn = dot_nt(cot_ref[f], ow_ref[...])
        for h in range(HEADS):
            parts = [qkv[:, p * chans + h * d : p * chans + (h + 1) * d] for p in range(3)]
            parts.append(dattn[:, h * d : (h + 1) * d])
            items_ref[f, h] = jnp.concatenate(parts, axis=1).astype(BF)


def proj(x, bext, cot, tw, qw, ow):
    frames, width, chans = x.shape
    return pl.pallas_call(
        proj_kernel,
        out_shape=(
            jax.ShapeDtypeStruct((frames, width, chans), F32),
            jax.ShapeDtypeStruct((frames, width, chans), BF),
            jax.ShapeDtypeStruct((frames, HEADS, width, 4 * chans // HEADS), BF),
        ),
        compiler_params=pltpu.CompilerParams(vmem_limit_bytes=32 << 20),
        cost_estimate=pl.CostEstimate(flops=10**9 * 2, bytes_accessed=6 << 20, transcendentals=0),
    )(x, bext, cot, tw, qw, ow)


def post_kernel(z_ref, cot_ref, qw_ref, attn_ref, dqkv_ref, dres_ref, dresb_ref):
    frames, width, chans = cot_ref.shape
    d = chans // HEADS
    for f in range(frames):
        heads = [z_ref[f, h].astype(F32) for h in range(HEADS)]
        for p in range(4):
            part = jnp.concatenate([z[:, p * d : (p + 1) * d] for z in heads], axis=1).astype(BF)
            if p == 0:
                attn_ref[f] = part
            else:
                dqkv_ref[f, :, (p - 1) * chans : p * chans] = part
        dres = cot_ref[f].astype(F32) + dot_nt(dqkv_ref[f], qw_ref[...])
        dres_ref[f] = dres
        dresb_ref[f] = dres.astype(BF)


def post(z, cot, qw):
    frames, width, chans = cot.shape
    return pl.pallas_call(
        post_kernel,
        out_shape=(
            jax.ShapeDtypeStruct((frames, width, chans), BF),
            jax.ShapeDtypeStruct((frames, width, 3 * chans), BF),
            jax.ShapeDtypeStruct((frames, width, chans), F32),
            jax.ShapeDtypeStruct((frames, width, chans), BF),
        ),
        compiler_params=pltpu.CompilerParams(vmem_limit_bytes=32 << 20),
        cost_estimate=pl.CostEstimate(flops=10**9, bytes_accessed=6 << 20, transcendentals=0),
    )(z, cot, qw)


def attn_kernel(scale, tq, ck, un, x_ref, o_ref, a_ref, kt_ref, vt_ref, s_ref, e_ref, acc_ref):
    tok = x_ref.shape[0]
    step = pl.program_id(0)
    nck = tok // ck
    d = 32
    @pl.when(step == 0)
    def _():
        k = x_ref[:, d:2*d]
        v = x_ref[:, 2*d:3*d]
        lane = lax.broadcasted_iota(jnp.int32, (tok, d), 1)
        ones = jnp.where(lane < 3, 1.0, 0.0).astype(BF)
        a_ref[...] = jnp.concatenate([k, k, v, ones], axis=1)
        kt_ref[...] = k.astype(F32).T.astype(BF)
        vt_ref[...] = jnp.concatenate([v, ones], axis=1).astype(F32).T.astype(BF)
        acc_ref[...] = jnp.zeros_like(acc_ref)
    rows = pl.ds(pl.multiple_of(step * tq, tq), tq)
    xb = x_ref[rows, :]
    q = xb[:, 0:d].astype(F32)
    do = xb[:, 3*d:4*d].astype(F32)
    zeros = jnp.zeros((tq, 2*d), BF)
    def split(z):
        hi = z.astype(BF)
        lo = (z - hi.astype(F32)).astype(BF)
        return hi, lo
    qh, ql = split(q * (scale * math.log2(math.e)))
    wq = jnp.concatenate([qh, ql, zeros], axis=1)
    def p1(i, m):
        r = pl.ds(pl.multiple_of(i * ck, ck), ck)
        s = lax.dot_general(a_ref[r, :], wq, NT, preferred_element_type=F32)
        s_ref[r, :] = s
        return jnp.maximum(m, jnp.max(s.reshape(ck // 8, 8, tq), axis=0))
    m = lax.fori_loop(0, nck, p1, jnp.full((8, tq), -jnp.inf, F32), unroll=un)
    m = jnp.max(m, axis=0, keepdims=True)
    def p2(i, o):
        r = pl.ds(pl.multiple_of(i * ck, ck), ck)
        e = jnp.exp2(s_ref[r, :] - m)
        s_ref[r, :] = e
        eb = e.astype(BF)
        e_ref[r, :] = eb
        return o + jnp.dot(vt_ref[:, r], eb, preferred_element_type=F32)
    o = lax.fori_loop(0, nck, p2, jnp.zeros((2*d, tq), F32), unroll=un)
    inv = 1.0 / o[d:d+1, :]
    ot = o[:d] * inv
    ob = ot.T
    delta = jnp.sum(ob * do, axis=1, keepdims=True)
    invc = jnp.broadcast_to(inv, (8, tq)).T[:, 0:1]
    dh = (-delta).astype(BF); dr = -delta - dh.astype(F32)
    dm = dr.astype(BF); dl = (dr - dm.astype(F32)).astype(BF)
    lane = lax.broadcasted_iota(jnp.int32, (tq, d), 1)
    dd = jnp.where(lane == 0, dh.astype(F32), jnp.where(lane == 1, dm.astype(F32), jnp.where(lane == 2, dl.astype(F32), 0.0))).astype(BF)
    wd = jnp.concatenate([zeros, xb[:, 3*d:], dd], axis=1)
    gh, gl = split(do * invc)
    rh, rl = split(q * (invc * scale))
    we = jnp.concatenate([zeros, gh, gl], axis=1)
    ws = jnp.concatenate([rh, rl, zeros], axis=1)
    def p3(i, dq):
        r = pl.ds(pl.multiple_of(i * ck, ck), ck)
        dp = lax.dot_general(a_ref[r, :], wd, NT, preferred_element_type=F32)
        ds = (s_ref[r, :] * dp).astype(BF)
        acc_ref[r, :] += (jnp.dot(ds, ws, preferred_element_type=F32)
                          + jnp.dot(e_ref[r, :], we, preferred_element_type=F32))
        return dq + jnp.dot(kt_ref[:, r], ds, preferred_element_type=F32)
    dq = lax.fori_loop(0, nck, p3, jnp.zeros((d, tq), F32), unroll=un)
    dq = dq * (inv * scale)
    o_ref[rows, 0:2*d] = jnp.concatenate([ot, dq], axis=0).T.astype(BF)
    @pl.when(step == pl.num_programs(0) - 1)
    def _():
        acc = acc_ref[...]
        dk = acc[:, :d] + acc[:, d:2*d]
        dv = acc[:, 2*d:3*d] + acc[:, 3*d:]
        o_ref[:, 2*d:] = jnp.concatenate([dk, dv], axis=1).astype(BF)

def attn(x, tq=768, ck=256, un=15):
    tok = x.shape[0]
    return pl.pallas_call(
        functools.partial(attn_kernel, 1.0/math.sqrt(32), tq, ck, un),
        grid=(tok // tq,),
        in_specs=[pl.BlockSpec((tok, 128), lambda i: (0, 0))],
        out_specs=pl.BlockSpec((tok, 128), lambda i: (0, 0)),
        out_shape=jax.ShapeDtypeStruct((tok, 128), BF),
        scratch_shapes=[pltpu.VMEM((tok, 128), BF), pltpu.VMEM((32, tok), BF), pltpu.VMEM((64, tok), BF),
                        pltpu.VMEM((tok, tq), F32), pltpu.VMEM((tok, tq), BF), pltpu.VMEM((tok, 128), F32)],
        compiler_params=pltpu.CompilerParams(vmem_limit_bytes=48 << 20),
        cost_estimate=pl.CostEstimate(flops=6*2*tok*tok*128, bytes_accessed=4*tok*128, transcendentals=tok*tok),
    )(x)


LANES = 128


def lanes_of(plane):
    width, chans = plane.shape
    pad = jnp.zeros((LANES - width, chans), F32)
    return jnp.concatenate([plane.astype(F32), pad], axis=0).T


def turn_kernel(r_ref, at_ref, bt_ref):
    group = r_ref.shape[0]
    frames = at_ref.shape[1]
    for f in range(frames):
        for row in range(group + 2):
            if row == 0:
                plane = r_ref[0, frames + f]
            elif row == group + 1:
                plane = r_ref[group - 1, frames + f]
            else:
                plane = r_ref[row - 1, f]
            tile = lanes_of(plane)
            cols = slice(row * LANES, (row + 1) * LANES)
            at_ref[0, f, :, cols] = pltpu.roll(tile, 1, 1).astype(BF)
            at_ref[1, f, :, cols] = tile.astype(BF)
            at_ref[2, f, :, cols] = pltpu.roll(tile, LANES - 1, 1).astype(BF)
    for f in range(2 * frames):
        for row in range(group):
            tile = lanes_of(r_ref[row, 2 * frames + f])
            bt_ref[f, :, row * LANES : (row + 1) * LANES] = tile.astype(BF)


def turn(r, frames):
    group, _, _, chans = r.shape
    return pl.pallas_call(
        turn_kernel,
        out_shape=(
            jax.ShapeDtypeStruct((3, frames, chans, (group + 2) * LANES), BF),
            jax.ShapeDtypeStruct((2 * frames, chans, group * LANES), BF),
        ),
        compiler_params=pltpu.CompilerParams(vmem_limit_bytes=40 << 20),
        cost_estimate=pl.CostEstimate(flops=10**9, bytes_accessed=10 << 20, transcendentals=0),
    )(r)


def terms_kernel(at_ref, bt_ref, dres_ref, dpre_ref, out_ref, dt_ref, dp_ref):
    group, frames, width, cols = dres_ref.shape
    chans = bt_ref.shape[1]
    blocks, rows = chans // out_ref.shape[1], out_ref.shape[1]
    pad = jnp.zeros((LANES - width, cols), F32)
    for src, dst in ((dres_ref, dt_ref), (dpre_ref, dp_ref)):
        for f in range(frames):
            for row in range(group):
                full = jnp.concatenate([src[row, f].astype(F32), pad], axis=0)
                dst[f, row * LANES : (row + 1) * LANES, :] = full.astype(BF)
    span = group * LANES

    def put(tap, value):
        value = value.astype(BF)
        for b in range(blocks):
            out_ref[tap * blocks + b] = value[b * rows : (b + 1) * rows]

    for i in range(3):
        for j in range(3):
            acc = jnp.zeros((chans, cols), F32)
            for f in range(frames):
                left = at_ref[j, f, :, i * LANES : i * LANES + span]
                acc = acc + jnp.dot(left, dp_ref[f], preferred_element_type=F32)
            put(3 * i + j, acc)
    for k in range(3):
        acc = jnp.zeros((chans, cols), F32)
        for f in range(frames):
            acc = acc + jnp.dot(bt_ref[f + k], dt_ref[f], preferred_element_type=F32)
        put(9 + k, acc)
    rest = out_ref.shape[0] - 12 * blocks
    out_ref[12 * blocks :] = jnp.zeros((rest, rows, cols), BF)


def conv_terms(at, bt, dres, dpre, owners, rows):
    group, frames, width, cols = dres.shape
    return pl.pallas_call(
        terms_kernel,
        out_shape=jax.ShapeDtypeStruct((owners, rows, cols), BF),
        scratch_shapes=[
            pltpu.VMEM((frames, group * LANES, cols), BF),
            pltpu.VMEM((frames, group * LANES, cols), BF),
        ],
        compiler_params=pltpu.CompilerParams(vmem_limit_bytes=40 << 20),
        cost_estimate=pl.CostEstimate(flops=2 * 10**9, bytes_accessed=10 << 20, transcendentals=0),
    )(at, bt, dres, dpre)


def silu_slope(value):
    sigma = jax.nn.sigmoid(value)
    return sigma * (1.0 + value * (1.0 - sigma))


def matmul(left, right):
    return jnp.dot(left, right, preferred_element_type=F32)


def inner_rows(left, right):
    return lax.dot_general(left, right, (((0,), (0,)), ((), ())), preferred_element_type=F32)


def transposed(left, right):
    return lax.dot_general(left, right, NT, preferred_element_type=F32)


def shift(x, axis, by):
    count = lax.axis_size(axis)
    pairs = [(i, i + by) for i in range(count) if 0 <= i + by < count]
    return lax.ppermute(x, axis, pairs)


def swap(x):
    count = lax.axis_size("space")
    return lax.ppermute(x, "space", [(i, i ^ 1) for i in range(count)])


def neighbours(field):
    return shift(field, "space", 1), shift(field, "space", -1)


GROUP = 8


def exchange(x):
    count = lax.axis_size("space")
    groups = [list(range(at, at + GROUP)) for at in range(0, count, GROUP)]
    return lax.all_to_all(x, "space", 0, 0, axis_index_groups=groups, tiled=True)


def by_chip(field):
    frames, width, chans = field.shape
    parts = field.reshape(frames, width, GROUP // 2, -1).transpose(2, 0, 1, 3)
    return jnp.repeat(parts, 2, axis=0)


def by_core(field, rows):
    planes, width, chans = field.shape
    parts = field.reshape(planes, width, -1, 2, rows).transpose(3, 0, 1, 2, 4)
    parts = parts.reshape(2, planes, width, chans // 2)
    return jnp.tile(parts, (GROUP // 2, 1, 1, 1))


def side_pad(field):
    return jnp.pad(field, ((0, 0), (0, 0), (1, 1), (0, 0)))


def taps_of(padded, width):
    pieces = [padded[:, i, j : j + width] for i in range(3) for j in range(3)]
    return jnp.concatenate(pieces, axis=-1).reshape(-1, 9 * padded.shape[-1])


def per_device(latents, spatial_weight, temporal_weight, qkv_weight, out_weight, cotangent):
    frames, rows, width, chans = latents.shape
    ntok = frames * width
    n_space = lax.axis_size("space")
    n_time = lax.axis_size("tm")
    depth = chans // HEADS
    norm = 1.0 / math.sqrt(ntok * n_space * n_time)
    core = lax.axis_index("space") % 2
    half = chans // 2
    share = 16 * chans // (n_space * n_time * 2)

    def halves(field):
        parts = field.reshape(field.shape[0], -1, 2, half)
        own = lax.dynamic_index_in_dim(parts, core, 2, keepdims=False)
        other = lax.dynamic_index_in_dim(parts, 1 - core, 2, keepdims=False)
        both = jnp.concatenate([own, swap(other)], axis=0)
        return both.reshape(both.shape[0], -1)

    def pair(field):
        return jnp.concatenate([field, swap(field)], axis=0)

    x = latents.reshape(frames, width, chans)
    xf = x.astype(F32)
    cot = cotangent.reshape(ntok, chans)
    act = jax.nn.silu(xf).astype(BF)
    above, below = neighbours(act)
    ahalo = side_pad(jnp.stack([above, act, below], axis=1))
    pre = matmul(taps_of(ahalo, width), spatial_weight)
    bact = jax.nn.silu(pre).astype(BF).reshape(frames, width, chans)
    bext = jnp.concatenate([shift(bact, "tm", 1), bact], axis=0)
    cot3 = cotangent.reshape(frames, width, chans)
    resid, rres, items = proj(x, bext, cot3, temporal_weight, qkv_weight, out_weight)
    rflat = rres.reshape(ntok, chans)
    items = items.reshape(frames * HEADS, width, 4 * depth)
    items = lax.all_to_all(items, "space", 0, 0, tiled=True)
    first = lax.axis_index("space") % GROUP == 0
    early = by_core(jnp.concatenate([act, jnp.where(first, above, below), bext], axis=0), share)
    rpair, cpair = pair(rflat), halves(cot)
    early, rpair, cpair, items = lax.optimization_barrier((early, rpair, cpair, items))
    early = exchange(early)
    outs = attn(items.reshape(n_space * width, 4 * depth)).reshape(n_space, width, 4 * depth)
    outs, early = lax.optimization_barrier((outs, early))
    outs = lax.all_to_all(outs, "space", 0, 0, tiled=True)
    aturn, bturn = turn(early, frames)
    outs = outs.reshape(frames, HEADS, width, 4 * depth)
    atted, dqkv, dres, dthree = post(outs, cot3, qkv_weight)
    atted = atted.reshape(ntok, chans)
    dqkv = dqkv.reshape(ntok, 3 * chans)
    dres = dres.reshape(ntok, chans)
    dresb = dthree.reshape(ntok, chans)
    mixed = (resid.reshape(ntok, chans) + matmul(atted, out_weight)).astype(BF).reshape(latents.shape)

    dext = jnp.concatenate([dthree, shift(dthree, "tm", -1)], axis=0)
    tw = temporal_weight.reshape(3, chans, chans)
    dbact = sum(transposed(dext[2 - k : 2 - k + frames].reshape(ntok, chans), tw[k]) for k in range(3))
    dpre = (dbact * silu_slope(pre)).astype(BF)
    dpre = dpre.reshape(frames, width, chans)
    last = [
        inner_rows(rpair, halves(dqkv)).reshape(3 * chans, half),
        inner_rows(pair(atted), cpair),
    ]
    last = jnp.concatenate([term.astype(BF) for term in last], axis=0)
    last, dpre = lax.optimization_barrier((last, dpre))
    dnear = exchange(by_chip(dpre))
    dabove, dbelow = neighbours(dpre)
    dhalo = side_pad(jnp.stack([dabove, dpre, dbelow], axis=1))
    last = lax.all_to_all(last.reshape(n_space, -1, half), "space", 0, 0, tiled=True)
    owners = n_space * n_time
    terms = conv_terms(aturn, bturn, exchange(by_chip(dthree)), dnear, owners, share)
    terms, dhalo = lax.optimization_barrier((terms, dhalo))
    terms = lax.all_to_all(terms, ("tm", "space"), 0, 0, tiled=True)
    sw = spatial_weight.reshape(3, 3, chans, chans)
    last = jnp.sum(last.reshape(n_space // 2, 2, -1, half).astype(F32), axis=0)
    last = last.transpose(1, 0, 2).reshape(-1, chans)
    others = [lax.ppermute(last, "tm", [(t, n_time - 1)]) for t in range(n_time - 1)]
    last = last + sum(others)
    dact = sum(
        transposed(dhalo[:, 2 - i, 2 - j : 2 - j + width].reshape(ntok, chans), sw[i, j])
        for i in range(3)
        for j in range(3)
    )
    grad_latents = (dres + dact * silu_slope(xf.reshape(ntok, chans))).astype(BF).reshape(latents.shape)
    summed = jnp.sum(terms.reshape(owners // GROUP, GROUP // 2, 2, share, -1).astype(F32), axis=0)
    summed = summed.transpose(1, 2, 0, 3).reshape(-1, chans)
    grad_weights = jnp.where(lax.axis_index("tm") == n_time - 1, last, summed) * norm
    return (mixed, grad_latents, grad_weights)


def solution(mesh):
    placed = (P("tm", "space", None, None), P(), P(), P(), P(), P("tm", "space", None, None))
    return jax.shard_map(
        per_device,
        mesh=mesh,
        in_specs=placed,
        out_specs=(
            P("tm", "space", None, None),
            P("tm", "space", None, None),
            P(("tm", "space"), None),
        ),
        check_vma=False,
    )
```

```python
import functools
import math

import jax
import jax.numpy as jnp
from jax import lax
from jax.experimental import pallas as pl
from jax.experimental.pallas import tpu as pltpu
from jax.sharding import PartitionSpec as P

HEADS = 16
GROUP = 8
F32 = jnp.float32
BF = jnp.bfloat16
NT = (((1,), (1,)), ((), ()))

def dot_nt(left, right):
    return lax.dot_general(left, right, NT, preferred_element_type=F32)


def proj_kernel(x_ref, bext_ref, cot_ref, tw_ref, qw_ref, ow_ref, resid_ref, rres_ref, items_ref):
    frames, width, chans = x_ref.shape
    d = chans // HEADS
    for f in range(frames):
        acc = x_ref[f].astype(F32)
        for k in range(3):
            tap = tw_ref[k * chans : (k + 1) * chans, :]
            acc = acc + jnp.dot(bext_ref[f + k], tap, preferred_element_type=F32)
        resid_ref[f] = acc
        rounded = acc.astype(BF)
        rres_ref[f] = rounded
        qkv = jnp.dot(rounded, qw_ref[...], preferred_element_type=F32)
        dattn = dot_nt(cot_ref[f], ow_ref[...])
        for h in range(HEADS):
            parts = [qkv[:, p * chans + h * d : p * chans + (h + 1) * d] for p in range(3)]
            parts.append(dattn[:, h * d : (h + 1) * d])
            items_ref[f, h] = jnp.concatenate(parts, axis=1).astype(BF)


def proj(x, bext, cot, tw, qw, ow):
    frames, width, chans = x.shape
    return pl.pallas_call(
        proj_kernel,
        out_shape=(
            jax.ShapeDtypeStruct((frames, width, chans), F32),
            jax.ShapeDtypeStruct((frames, width, chans), BF),
            jax.ShapeDtypeStruct((frames, HEADS, width, 4 * chans // HEADS), BF),
        ),
        compiler_params=pltpu.CompilerParams(vmem_limit_bytes=32 << 20),
        cost_estimate=pl.CostEstimate(flops=10**9 * 2, bytes_accessed=6 << 20, transcendentals=0),
    )(x, bext, cot, tw, qw, ow)


def post_kernel(z_ref, cot_ref, qw_ref, attn_ref, dres_ref, dresb_ref, pay_ref):
    frames, width, chans = cot_ref.shape
    d = chans // HEADS
    half = chans // 2
    for f in range(frames):
        heads = [z_ref[f, h].astype(F32) for h in range(HEADS)]
        dres = cot_ref[f].astype(F32)
        for p in range(4):
            part = jnp.concatenate([z[:, p * d : (p + 1) * d] for z in heads], axis=1).astype(BF)
            if p == 0:
                attn_ref[f] = part
                continue
            dres = dres + dot_nt(part, qw_ref[:, (p - 1) * chans : p * chans])
            for c in range(2):
                pay_ref[c, f, :, (p - 1) * half : p * half] = part[:, c * half : (c + 1) * half]
        dres_ref[f] = dres
        dresb = dres.astype(BF)
        dresb_ref[f] = dresb
        for c in range(2):
            pay_ref[c, f, :, 3 * half :] = dresb[:, c * half : (c + 1) * half]


def post(z, cot, qw):
    frames, width, chans = cot.shape
    return pl.pallas_call(
        post_kernel,
        out_shape=(
            jax.ShapeDtypeStruct((frames, width, chans), BF),
            jax.ShapeDtypeStruct((frames, width, chans), F32),
            jax.ShapeDtypeStruct((frames, width, chans), BF),
            jax.ShapeDtypeStruct((2, frames, width, 2 * chans), BF),
        ),
        compiler_params=pltpu.CompilerParams(vmem_limit_bytes=32 << 20),
        cost_estimate=pl.CostEstimate(flops=10**9, bytes_accessed=6 << 20, transcendentals=0),
    )(z, cot, qw)


def attn_kernel(scale, tq, ck, un, x_ref, o_ref, a_ref, kt_ref, vt_ref, s_ref, e_ref, acc_ref):
    tok = x_ref.shape[0]
    step = pl.program_id(0)
    nck = tok // ck
    d = 32
    @pl.when(step == 0)
    def _():
        k = x_ref[:, d:2*d]
        v = x_ref[:, 2*d:3*d]
        lane = lax.broadcasted_iota(jnp.int32, (tok, d), 1)
        ones = jnp.where(lane < 3, 1.0, 0.0).astype(BF)
        a_ref[...] = jnp.concatenate([k, k, v, ones], axis=1)
        kt_ref[...] = k.astype(F32).T.astype(BF)
        vt_ref[...] = jnp.concatenate([v, ones], axis=1).astype(F32).T.astype(BF)
        acc_ref[...] = jnp.zeros_like(acc_ref)
    rows = pl.ds(pl.multiple_of(step * tq, tq), tq)
    xb = x_ref[rows, :]
    q = xb[:, 0:d].astype(F32)
    do = xb[:, 3*d:4*d].astype(F32)
    zeros = jnp.zeros((tq, 2*d), BF)
    def split(z):
        hi = z.astype(BF)
        lo = (z - hi.astype(F32)).astype(BF)
        return hi, lo
    qh, ql = split(q * (scale * math.log2(math.e)))
    wq = jnp.concatenate([qh, ql, zeros], axis=1)
    def p1(i, m):
        r = pl.ds(pl.multiple_of(i * ck, ck), ck)
        s = lax.dot_general(a_ref[r, :], wq, NT, preferred_element_type=F32)
        s_ref[r, :] = s
        return jnp.maximum(m, jnp.max(s.reshape(ck // 8, 8, tq), axis=0))
    m = lax.fori_loop(0, nck, p1, jnp.full((8, tq), -jnp.inf, F32), unroll=un)
    m = jnp.max(m, axis=0, keepdims=True)
    def p2(i, o):
        r = pl.ds(pl.multiple_of(i * ck, ck), ck)
        e = jnp.exp2(s_ref[r, :] - m)
        s_ref[r, :] = e
        eb = e.astype(BF)
        e_ref[r, :] = eb
        return o + jnp.dot(vt_ref[:, r], eb, preferred_element_type=F32)
    o = lax.fori_loop(0, nck, p2, jnp.zeros((2*d, tq), F32), unroll=un)
    inv = 1.0 / o[d:d+1, :]
    ot = o[:d] * inv
    ob = ot.T
    delta = jnp.sum(ob * do, axis=1, keepdims=True)
    invc = jnp.broadcast_to(inv, (8, tq)).T[:, 0:1]
    dh = (-delta).astype(BF); dr = -delta - dh.astype(F32)
    dm = dr.astype(BF); dl = (dr - dm.astype(F32)).astype(BF)
    lane = lax.broadcasted_iota(jnp.int32, (tq, d), 1)
    dd = jnp.where(lane == 0, dh.astype(F32), jnp.where(lane == 1, dm.astype(F32), jnp.where(lane == 2, dl.astype(F32), 0.0))).astype(BF)
    wd = jnp.concatenate([zeros, xb[:, 3*d:], dd], axis=1)
    gh, gl = split(do * invc)
    rh, rl = split(q * (invc * scale))
    we = jnp.concatenate([zeros, gh, gl], axis=1)
    ws = jnp.concatenate([rh, rl, zeros], axis=1)
    def p3(i, dq):
        r = pl.ds(pl.multiple_of(i * ck, ck), ck)
        dp = lax.dot_general(a_ref[r, :], wd, NT, preferred_element_type=F32)
        ds = (s_ref[r, :] * dp).astype(BF)
        acc_ref[r, :] += (jnp.dot(ds, ws, preferred_element_type=F32)
                          + jnp.dot(e_ref[r, :], we, preferred_element_type=F32))
        return dq + jnp.dot(kt_ref[:, r], ds, preferred_element_type=F32)
    dq = lax.fori_loop(0, nck, p3, jnp.zeros((d, tq), F32), unroll=un)
    dq = dq * (inv * scale)
    o_ref[rows, 0:2*d] = jnp.concatenate([ot, dq], axis=0).T.astype(BF)
    @pl.when(step == pl.num_programs(0) - 1)
    def _():
        acc = acc_ref[...]
        dk = acc[:, :d] + acc[:, d:2*d]
        dv = acc[:, 2*d:3*d] + acc[:, 3*d:]
        o_ref[:, 2*d:] = jnp.concatenate([dk, dv], axis=1).astype(BF)

def attn(x, tq=768, ck=256, un=15):
    tok = x.shape[0]
    return pl.pallas_call(
        functools.partial(attn_kernel, 1.0/math.sqrt(32), tq, ck, un),
        grid=(tok // tq,),
        in_specs=[pl.BlockSpec((tok, 128), lambda i: (0, 0))],
        out_specs=pl.BlockSpec((tok, 128), lambda i: (0, 0)),
        out_shape=jax.ShapeDtypeStruct((tok, 128), BF),
        scratch_shapes=[pltpu.VMEM((tok, 128), BF), pltpu.VMEM((32, tok), BF), pltpu.VMEM((64, tok), BF),
                        pltpu.VMEM((tok, tq), F32), pltpu.VMEM((tok, tq), BF), pltpu.VMEM((tok, 128), F32)],
        compiler_params=pltpu.CompilerParams(vmem_limit_bytes=48 << 20),
        cost_estimate=pl.CostEstimate(flops=6*2*tok*tok*128, bytes_accessed=4*tok*128, transcendentals=tok*tok),
    )(x)


LANES = 128
CALL = functools.partial(pltpu.CompilerParams, vmem_limit_bytes=40 << 20)


def cost(flops, moved):
    return pl.CostEstimate(flops=int(flops), bytes_accessed=int(moved), transcendentals=0)


def padded(plane):
    width, chans = plane.shape
    return jnp.concatenate([plane.astype(F32), jnp.zeros((LANES - width, chans), F32)], axis=0)


def pick_kernel(rows, act_ref, outer_ref, out_ref):
    group = out_ref.shape[0]
    frames, width, chans = act_ref.shape
    for f in range(frames):
        for at, src in ((f, act_ref), (frames + f, outer_ref)):
            plane = src[f].astype(F32)
            for c in range(2):
                parts = [plane[:, b + c * rows : b + (c + 1) * rows] for b in range(0, chans, 2 * rows)]
                part = jnp.concatenate(parts, axis=1).astype(BF)
                for x in range(group // 2):
                    out_ref[2 * x + c, at] = part


def pick(act, outer, rows):
    frames, width, chans = act.shape
    return pl.pallas_call(
        functools.partial(pick_kernel, rows),
        out_shape=jax.ShapeDtypeStruct((GROUP, 2 * frames, width, chans // 2), BF),
        compiler_params=CALL(),
        cost_estimate=cost(1e8, 3 << 20),
    )(act, outer)


def turn_kernel(r_ref, at_ref):
    group = r_ref.shape[0]
    frames = at_ref.shape[1]
    for f in range(frames):
        for row in range(group + 2):
            if row == 0:
                plane = r_ref[0, frames + f]
            elif row == group + 1:
                plane = r_ref[group - 1, frames + f]
            else:
                plane = r_ref[row - 1, f]
            tile = padded(plane).T
            cols = slice(row * LANES, (row + 1) * LANES)
            at_ref[0, f, :, cols] = pltpu.roll(tile, 1, 1).astype(BF)
            at_ref[1, f, :, cols] = tile.astype(BF)
            at_ref[2, f, :, cols] = pltpu.roll(tile, LANES - 1, 1).astype(BF)


def turn(r, frames):
    group, _, _, chans = r.shape
    return pl.pallas_call(
        turn_kernel,
        out_shape=jax.ShapeDtypeStruct((3, frames, chans, (group + 2) * LANES), BF),
        compiler_params=CALL(),
        cost_estimate=cost(1e9, 6 << 20),
    )(r)


def turn_pair_kernel(*refs):
    ins, outs = refs[:4], refs[4:]
    for own, other, out in ((ins[0], ins[1], outs[0]), (ins[2], ins[3], outs[1])):
        count = own.shape[0]
        for d, src in enumerate((own, other)):
            for f in range(count):
                at = (d * count + f) * LANES
                out[:, at : at + LANES] = padded(src[f]).T.astype(BF)


def turn_pair(own_r, other_r, own_b, other_b):
    chans = own_r.shape[-1]
    return pl.pallas_call(
        turn_pair_kernel,
        out_shape=tuple(
            jax.ShapeDtypeStruct((chans, 2 * x.shape[0] * LANES), BF) for x in (own_r, own_b)
        ),
        compiler_params=CALL(),
        cost_estimate=cost(1e9, 4 << 20),
    )(own_r, other_r, own_b, other_b)


def local_terms_kernel(rt_ref, bt_ref, a0_ref, a1_ref, p0_ref, p1_ref, c0_ref, c1_ref, out_ref, at_ref, pay_ref, cot_ref, mix_ref):
    frames, width, chans = a0_ref.shape
    half = chans // 2
    for d, (a, p, c) in enumerate(((a0_ref, p0_ref, c0_ref), (a1_ref, p1_ref, c1_ref))):
        for f in range(frames):
            at = (d * frames + f) * LANES
            at_ref[:, at : at + LANES] = padded(a[f]).T.astype(BF)
            pay_ref[at : at + LANES, :] = padded(p[f]).astype(BF)
            cot_ref[at : at + LANES, :] = padded(c[f]).astype(BF)
    parts, _, rows, _ = out_ref.shape
    block = parts * rows

    def put(first, value, lane=0):
        for n in range(value.shape[0] // block):
            for y in range(parts):
                at = n * block + y * rows
                out_ref[y, first + n, :, lane : lane + value.shape[1]] = value[at : at + rows].astype(BF)

    for k in range(3):
        acc = jnp.zeros((chans, half), F32)
        for d in range(2):
            left = bt_ref[:, (2 * d * frames + k) * LANES : (2 * d * frames + k + frames) * LANES]
            right = pay_ref[d * frames * LANES : (d + 1) * frames * LANES, 3 * half :]
            acc = acc + jnp.dot(left, right, preferred_element_type=F32)
        put(k * chans // block, acc)
    for p in range(3):
        right = pay_ref[:, p * half : (p + 1) * half]
        for lane in range(0, half, LANES):
            value = jnp.dot(rt_ref[...], right[:, lane : lane + LANES], preferred_element_type=F32)
            mix_ref[lane // LANES, pl.ds(p, chans, stride=3), :] = value
    for lane in range(0, half, LANES):
        put(3 * chans // block, mix_ref[lane // LANES], lane)
    put(6 * chans // block, jnp.dot(at_ref[...], cot_ref[...], preferred_element_type=F32))


def local_terms(rt, bt, atted, pay, cot):
    frames, width, chans = atted[0].shape
    half = chans // 2
    span = 2 * frames * LANES
    return pl.pallas_call(
        local_terms_kernel,
        out_shape=jax.ShapeDtypeStruct((4, 7 * chans // 64, 16, half), BF),
        scratch_shapes=[
            pltpu.VMEM((chans, span), BF),
            pltpu.VMEM((span, 4 * half), BF),
            pltpu.VMEM((span, half), BF),
            pltpu.VMEM((half // LANES, 3 * chans, LANES), F32),
        ],
        compiler_params=CALL(),
        cost_estimate=cost(2e9, 10 << 20),
    )(rt, bt, *atted, *pay, *cot)


def conv_terms_kernel(at_ref, dpre_ref, s0_ref, s1_ref, s2_ref, s3_ref, out_ref, dp_ref):
    group, frames, width, cols = dpre_ref.shape
    chans = at_ref.shape[2]
    rows = out_ref.shape[1]
    blocks = chans // rows
    for f in range(frames):
        for row in range(group):
            dp_ref[f, row * LANES : (row + 1) * LANES, :] = padded(dpre_ref[row, f]).astype(BF)
    span = group * LANES
    for i in range(3):
        for j in range(3):
            acc = jnp.zeros((chans, cols), F32)
            for f in range(frames):
                left = at_ref[j, f, :, i * LANES : i * LANES + span]
                acc = acc + jnp.dot(left, dp_ref[f], preferred_element_type=F32)
            value = acc.astype(BF)
            for b in range(blocks):
                out_ref[(3 * i + j) * blocks + b] = value[b * rows : (b + 1) * rows]
    for n in range(s0_ref.shape[0]):
        value = s0_ref[n].astype(F32) + s1_ref[n].astype(F32) + s2_ref[n].astype(F32) + s3_ref[n].astype(F32)
        value = value.astype(BF)
        out_ref[9 * blocks + n] = jnp.concatenate([value[:, :cols], value[:, cols:]], axis=0)


def conv_terms(at, dpre, parts, owners, rows):
    group, frames, width, cols = dpre.shape
    return pl.pallas_call(
        conv_terms_kernel,
        out_shape=jax.ShapeDtypeStruct((owners, rows, cols), BF),
        scratch_shapes=[pltpu.VMEM((frames, group * LANES, cols), BF)],
        compiler_params=CALL(),
        cost_estimate=cost(2e9, 10 << 20),
    )(at, dpre, *parts)


def sum_kernel(norm, dims, which_ref, terms_ref, out_ref):
    times, ys, xs = dims
    rows, cols = terms_ref.shape[1:]

    @pl.when(which_ref[0] == 1)
    def _():
        for x in range(xs):
            for c in range(2):
                acc = jnp.zeros((rows, cols), F32)
                for t in range(times):
                    for y in range(ys):
                        acc = acc + terms_ref[((t * ys + y) * xs + x) * 2 + c].astype(F32)
                out_ref[c * rows : (c + 1) * rows, x * cols : (x + 1) * cols] = acc * norm

    @pl.when(which_ref[0] == 0)
    def _():
        part = rows // 2
        for y in range(ys):
            for c in range(2):
                acc = jnp.zeros((rows, cols), F32)
                for t in range(times):
                    for x in range(xs):
                        acc = acc + terms_ref[((t * ys + y) * xs + x) * 2 + c].astype(F32)
                acc = acc * norm
                for h in range(2):
                    at = (2 * c + h) * cols
                    out_ref[y * part : (y + 1) * part, at : at + cols] = acc[h * part : (h + 1) * part]


def sum_terms(which, terms, norm, dims):
    owners, rows, cols = terms.shape
    return pl.pallas_call(
        functools.partial(sum_kernel, norm, dims),
        out_shape=jax.ShapeDtypeStruct((2 * rows, 4 * cols), F32),
        in_specs=[pl.BlockSpec(memory_space=pltpu.SMEM), pl.BlockSpec(memory_space=pltpu.VMEM)],
        compiler_params=CALL(),
        cost_estimate=cost(1e7, 1 << 20),
    )(which, terms)


def dpre_kernel(own_ref, next_ref, slope_ref, tw_ref, dpre_ref, near_ref):
    frames, width, chans = own_ref.shape
    group, _, _, cols = near_ref.shape
    ext = [own_ref[f] for f in range(frames)] + [next_ref[f] for f in range(frames)]
    for f in range(frames):
        acc = jnp.zeros((width, chans), F32)
        for k in range(3):
            acc = acc + dot_nt(ext[f + 2 - k], tw_ref[k * chans : (k + 1) * chans, :])
        value = (acc * slope_ref[f]).astype(BF)
        dpre_ref[f] = value
        for e in range(group):
            near_ref[e, f] = value[:, (e // 2) * cols : (e // 2 + 1) * cols]


def make_dpre(own, nxt, slope, tw):
    frames, width, chans = own.shape
    return pl.pallas_call(
        dpre_kernel,
        out_shape=(
            jax.ShapeDtypeStruct((frames, width, chans), BF),
            jax.ShapeDtypeStruct((GROUP, frames, width, 2 * chans // GROUP), BF),
        ),
        compiler_params=CALL(),
        cost_estimate=cost(5e8, 3 << 20),
    )(own, nxt, slope, tw)


def dact_kernel(mid_ref, above_ref, below_ref, dres_ref, x_ref, sw_ref, out_ref):
    frames, width, chans = mid_ref.shape
    line = lax.broadcasted_iota(jnp.int32, (width, chans), 0)
    for f in range(frames):
        acc = jnp.zeros((width, chans), F32)
        for i, src in enumerate((below_ref, mid_ref, above_ref)):
            plane = src[f]
            wide = plane.astype(F32)
            right = jnp.where(line == width - 1, 0.0, pltpu.roll(wide, width - 1, 0)).astype(BF)
            left = jnp.where(line == 0, 0.0, pltpu.roll(wide, 1, 0)).astype(BF)
            for j, value in enumerate((right, plane, left)):
                tap = 3 * i + j
                acc = acc + dot_nt(value, sw_ref[tap * chans : (tap + 1) * chans, :])
        x = x_ref[f].astype(F32)
        sigma = 1.0 / (1.0 + jnp.exp(-x))
        slope = sigma * (1.0 + x * (1.0 - sigma))
        out_ref[f] = (dres_ref[f] + acc * slope).astype(BF)


def make_grad_latents(mid, above, below, dres, x, sw):
    return pl.pallas_call(
        dact_kernel,
        out_shape=jax.ShapeDtypeStruct(mid.shape, BF),
        compiler_params=CALL(),
        cost_estimate=cost(2e9, 8 << 20),
    )(mid, above, below, dres, x, sw)


def silu_slope(value):
    sigma = jax.nn.sigmoid(value)
    return sigma * (1.0 + value * (1.0 - sigma))


def matmul(left, right):
    return jnp.dot(left, right, preferred_element_type=F32)


def shift(x, axis, by):
    count = lax.axis_size(axis)
    pairs = [(i, i + by) for i in range(count) if 0 <= i + by < count]
    return lax.ppermute(x, axis, pairs)


def swap(x):
    count = lax.axis_size("space")
    return lax.ppermute(x, "space", [(i, i ^ 1) for i in range(count)])


def neighbours(field):
    return shift(field, "space", 1), shift(field, "space", -1)


def exchange(x):
    count = lax.axis_size("space")
    groups = [list(range(at, at + GROUP)) for at in range(0, count, GROUP)]
    return lax.all_to_all(x, "space", 0, 0, axis_index_groups=groups, tiled=True)


def along_y(x, by):
    count = lax.axis_size("space")
    return lax.ppermute(x, "space", [(i, (i + by * GROUP) % count) for i in range(count)])


def pick_one(x, index):
    return lax.dynamic_index_in_dim(x, index, 0, keepdims=False)


def side_pad(field):
    return jnp.pad(field, ((0, 0), (0, 0), (1, 1), (0, 0)))


def taps_of(padded, width):
    pieces = [padded[:, i, j : j + width] for i in range(3) for j in range(3)]
    return jnp.concatenate(pieces, axis=-1).reshape(-1, 9 * padded.shape[-1])


def per_device(latents, spatial_weight, temporal_weight, qkv_weight, out_weight, cotangent):
    frames, rows, width, chans = latents.shape
    ntok = frames * width
    n_space = lax.axis_size("space")
    n_time = lax.axis_size("tm")
    owners = n_space * n_time
    depth = chans // HEADS
    norm = 1.0 / math.sqrt(ntok * n_space * n_time)
    here = lax.axis_index("space")
    core, line = here % 2, here // GROUP
    half = chans // 2
    share = 16 * chans // (2 * owners)

    x = latents.reshape(frames, width, chans)
    cot = cotangent.reshape(frames, width, chans)
    act = jax.nn.silu(x.astype(F32)).astype(BF)
    above, below = neighbours(act)
    pre = matmul(taps_of(side_pad(jnp.stack([above, act, below], axis=1)), width), spatial_weight)
    pre = pre.reshape(frames, width, chans)
    bact = jax.nn.silu(pre).astype(BF)
    bext = jnp.concatenate([shift(bact, "tm", 1), bact], axis=0)
    resid, rres, items = proj(x, bext, cot, temporal_weight, qkv_weight, out_weight)
    items = items.reshape(frames * HEADS, width, 4 * depth)
    items = lax.all_to_all(items, "space", 0, 0, tiled=True)

    early = pick(act, jnp.where(here % GROUP == 0, above, below), share)
    chalf = cot.reshape(frames, width, 2, half).transpose(2, 0, 1, 3)
    cpair = (pick_one(chalf, core), swap(pick_one(chalf, 1 - core)))
    rother, bother = swap(rres), swap(bext)
    early, cpair, rother, bother, items = lax.optimization_barrier((early, cpair, rother, bother, items))
    early = exchange(early)
    outs = attn(items.reshape(n_space * width, 4 * depth)).reshape(n_space, width, 4 * depth)
    outs, early, rother, bother = lax.optimization_barrier((outs, early, rother, bother))
    outs = lax.all_to_all(outs, "space", 0, 0, tiled=True)
    aturn = turn(early, frames)
    rturn, bturn = turn_pair(rres, rother, bext, bother)
    slope = silu_slope(pre)
    outs, aturn, rturn, bturn, slope = lax.optimization_barrier((outs, aturn, rturn, bturn, slope))

    atted, dres, dresb, pay = post(outs.reshape(frames, HEADS, width, 4 * depth), cot, qkv_weight)
    dnext = shift(dresb, "tm", -1)
    apair = (atted, swap(atted))
    ppair = (pick_one(pay, core), swap(pick_one(pay, 1 - core)))
    local = local_terms(rturn, bturn, apair, ppair, cpair)
    local, dnext = lax.optimization_barrier((local, dnext))
    dpre, near = make_dpre(dresb, dnext, slope, temporal_weight)
    near = exchange(near)
    dabove, dbelow = neighbours(dpre)
    parts = [pick_one(local, line)]
    for by in range(1, 4):
        parts.append(along_y(pick_one(local, (line + by) % 4), by))
    mixed = resid.reshape(ntok, chans) + matmul(atted.reshape(ntok, chans), out_weight)
    mixed = mixed.astype(BF).reshape(latents.shape)
    mixed, dabove, dbelow, near = lax.optimization_barrier((mixed, dabove, dbelow, near))
    terms = conv_terms(aturn, near, parts, owners, share)
    terms, dpre = lax.optimization_barrier((terms, dpre))
    terms = lax.all_to_all(terms, ("tm", "space"), 0, 0, tiled=True)
    grad_latents = make_grad_latents(dpre, dabove, dbelow, dres, x, spatial_weight).reshape(latents.shape)
    index = lax.axis_index("tm") * n_space + here
    which = (index < 9 * chans // (2 * share)).astype(jnp.int32).reshape(1)
    grad_weights = sum_terms(which, terms, norm, (n_time, n_space // GROUP, GROUP // 2))
    return (mixed, grad_latents, grad_weights)


def solution(mesh):
    placed = (P("tm", "space", None, None), P(), P(), P(), P(), P("tm", "space", None, None))
    return jax.shard_map(
        per_device,
        mesh=mesh,
        in_specs=placed,
        out_specs=(
            P("tm", "space", None, None),
            P("tm", "space", None, None),
            P(("tm", "space"), None),
        ),
        check_vma=False,
    )
```

```python
import functools
import math

import jax
import jax.numpy as jnp
from jax import lax
from jax.experimental import pallas as pl
from jax.experimental.pallas import tpu as pltpu
from jax.sharding import PartitionSpec as P

HEADS = 16
GROUP = 8
F32 = jnp.float32
BF = jnp.bfloat16
NT = (((1,), (1,)), ((), ()))

def dot_nt(left, right):
    return lax.dot_general(left, right, NT, preferred_element_type=F32)


def proj_kernel(x_ref, bext_ref, cot_ref, tw_ref, qw_ref, ow_ref, resid_ref, rres_ref, items_ref):
    frames, width, chans = x_ref.shape
    d = chans // HEADS
    for f in range(frames):
        acc = x_ref[f].astype(F32)
        for k in range(3):
            tap = tw_ref[k * chans : (k + 1) * chans, :]
            acc = acc + jnp.dot(bext_ref[f + k], tap, preferred_element_type=F32)
        resid_ref[f] = acc
        rounded = acc.astype(BF)
        rres_ref[f] = rounded
        qkv = jnp.dot(rounded, qw_ref[...], preferred_element_type=F32)
        dattn = dot_nt(cot_ref[f], ow_ref[...])
        for h in range(HEADS):
            parts = [qkv[:, p * chans + h * d : p * chans + (h + 1) * d] for p in range(3)]
            parts.append(dattn[:, h * d : (h + 1) * d])
            items_ref[f, h] = jnp.concatenate(parts, axis=1).astype(BF)


def proj(x, bext, cot, tw, qw, ow):
    frames, width, chans = x.shape
    return pl.pallas_call(
        proj_kernel,
        out_shape=(
            jax.ShapeDtypeStruct((frames, width, chans), F32),
            jax.ShapeDtypeStruct((frames, width, chans), BF),
            jax.ShapeDtypeStruct((frames, HEADS, width, 4 * chans // HEADS), BF),
        ),
        compiler_params=pltpu.CompilerParams(vmem_limit_bytes=20 << 20),
        cost_estimate=pl.CostEstimate(flops=10**9 * 2, bytes_accessed=6 << 20, transcendentals=0),
    )(x, bext, cot, tw, qw, ow)


def columns(z_ref, f, part, d):
    return jnp.concatenate([z_ref[f, h].astype(F32)[:, part * d : (part + 1) * d] for h in range(HEADS)], axis=1)


def dres_kernel(z_ref, cot_ref, qw_ref, dres_ref, dresb_ref):
    frames, width, chans = cot_ref.shape
    d = chans // HEADS
    for f in range(frames):
        dres = cot_ref[f].astype(F32)
        for p in range(3):
            part = columns(z_ref, f, p + 1, d).astype(BF)
            dres = dres + dot_nt(part, qw_ref[:, p * chans : (p + 1) * chans])
        dres_ref[f] = dres
        dresb_ref[f] = dres.astype(BF)


def make_dres(z, cot, qw):
    return pl.pallas_call(
        dres_kernel,
        out_shape=(jax.ShapeDtypeStruct(cot.shape, F32), jax.ShapeDtypeStruct(cot.shape, BF)),
        compiler_params=pltpu.CompilerParams(vmem_limit_bytes=20 << 20),
        cost_estimate=pl.CostEstimate(flops=10**9, bytes_accessed=6 << 20, transcendentals=0),
    )(z, cot, qw)


def pack_kernel(z_ref, dresb_ref, attn_ref, pay_ref):
    frames, width, chans = dresb_ref.shape
    half = chans // 2
    for f in range(frames):
        parts = [columns(z_ref, f, p, chans // HEADS).astype(BF) for p in range(4)]
        attn_ref[f] = parts[0]
        for at, part in enumerate(parts[1:] + [dresb_ref[f]]):
            for c in range(2):
                pay_ref[c, f, :, at * half : (at + 1) * half] = part[:, c * half : (c + 1) * half]


def pack(z, dresb):
    frames, width, chans = dresb.shape
    return pl.pallas_call(
        pack_kernel,
        out_shape=(
            jax.ShapeDtypeStruct((frames, width, chans), BF),
            jax.ShapeDtypeStruct((2, frames, width, 2 * chans), BF),
        ),
        compiler_params=pltpu.CompilerParams(vmem_limit_bytes=20 << 20),
        cost_estimate=pl.CostEstimate(flops=10**8, bytes_accessed=4 << 20, transcendentals=0),
    )(z, dresb)


def attn_kernel(scale, tq, ck, un, x_ref, o_ref, a_ref, kt_ref, vt_ref, s_ref, e_ref, acc_ref):
    tok = x_ref.shape[0]
    step = pl.program_id(0)
    nck = tok // ck
    d = 32
    @pl.when(step == 0)
    def _():
        k = x_ref[:, d:2*d]
        v = x_ref[:, 2*d:3*d]
        lane = lax.broadcasted_iota(jnp.int32, (tok, d), 1)
        ones = jnp.where(lane < 3, 1.0, 0.0).astype(BF)
        a_ref[...] = jnp.concatenate([k, k, v, ones], axis=1)
        kt_ref[...] = k.astype(F32).T.astype(BF)
        vt_ref[...] = jnp.concatenate([v, ones], axis=1).astype(F32).T.astype(BF)
        acc_ref[...] = jnp.zeros_like(acc_ref)
    rows = pl.ds(pl.multiple_of(step * tq, tq), tq)
    xb = x_ref[rows, :]
    q = xb[:, 0:d].astype(F32)
    do = xb[:, 3*d:4*d].astype(F32)
    zeros = jnp.zeros((tq, 2*d), BF)
    def split(z):
        hi = z.astype(BF)
        lo = (z - hi.astype(F32)).astype(BF)
        return hi, lo
    qh, ql = split(q * (scale * math.log2(math.e)))
    wq = jnp.concatenate([qh, ql, zeros], axis=1)
    def p1(i, m):
        r = pl.ds(pl.multiple_of(i * ck, ck), ck)
        s = lax.dot_general(a_ref[r, :], wq, NT, preferred_element_type=F32)
        s_ref[r, :] = s
        return jnp.maximum(m, jnp.max(s.reshape(ck // 8, 8, tq), axis=0))
    m = lax.fori_loop(0, nck, p1, jnp.full((8, tq), -jnp.inf, F32), unroll=un)
    m = jnp.max(m, axis=0, keepdims=True)
    def p2(i, o):
        r = pl.ds(pl.multiple_of(i * ck, ck), ck)
        e = jnp.exp2(s_ref[r, :] - m)
        s_ref[r, :] = e
        eb = e.astype(BF)
        e_ref[r, :] = eb
        return o + jnp.dot(vt_ref[:, r], eb, preferred_element_type=F32)
    o = lax.fori_loop(0, nck, p2, jnp.zeros((2*d, tq), F32), unroll=un)
    inv = 1.0 / o[d:d+1, :]
    ot = o[:d] * inv
    ob = ot.T
    delta = jnp.sum(ob * do, axis=1, keepdims=True)
    invc = jnp.broadcast_to(inv, (8, tq)).T[:, 0:1]
    dh = (-delta).astype(BF); dr = -delta - dh.astype(F32)
    dm = dr.astype(BF); dl = (dr - dm.astype(F32)).astype(BF)
    lane = lax.broadcasted_iota(jnp.int32, (tq, d), 1)
    dd = jnp.where(lane == 0, dh.astype(F32), jnp.where(lane == 1, dm.astype(F32), jnp.where(lane == 2, dl.astype(F32), 0.0))).astype(BF)
    wd = jnp.concatenate([zeros, xb[:, 3*d:], dd], axis=1)
    gh, gl = split(do * invc)
    rh, rl = split(q * (invc * scale))
    we = jnp.concatenate([zeros, gh, gl], axis=1)
    ws = jnp.concatenate([rh, rl, zeros], axis=1)
    def p3(i, dq):
        r = pl.ds(pl.multiple_of(i * ck, ck), ck)
        dp = lax.dot_general(a_ref[r, :], wd, NT, preferred_element_type=F32)
        ds = (s_ref[r, :] * dp).astype(BF)
        acc_ref[r, :] += (jnp.dot(ds, ws, preferred_element_type=F32)
                          + jnp.dot(e_ref[r, :], we, preferred_element_type=F32))
        return dq + jnp.dot(kt_ref[:, r], ds, preferred_element_type=F32)
    dq = lax.fori_loop(0, nck, p3, jnp.zeros((d, tq), F32), unroll=un)
    dq = dq * (inv * scale)
    o_ref[rows, 0:2*d] = jnp.concatenate([ot, dq], axis=0).T.astype(BF)
    @pl.when(step == pl.num_programs(0) - 1)
    def _():
        acc = acc_ref[...]
        dk = acc[:, :d] + acc[:, d:2*d]
        dv = acc[:, 2*d:3*d] + acc[:, 3*d:]
        o_ref[:, 2*d:] = jnp.concatenate([dk, dv], axis=1).astype(BF)

def attn(x, tq=768, ck=256, un=15):
    tok = x.shape[0]
    return pl.pallas_call(
        functools.partial(attn_kernel, 1.0/math.sqrt(32), tq, ck, un),
        grid=(tok // tq,),
        in_specs=[pl.BlockSpec((tok, 128), lambda i: (0, 0))],
        out_specs=pl.BlockSpec((tok, 128), lambda i: (0, 0)),
        out_shape=jax.ShapeDtypeStruct((tok, 128), BF),
        scratch_shapes=[pltpu.VMEM((tok, 128), BF), pltpu.VMEM((32, tok), BF), pltpu.VMEM((64, tok), BF),
                        pltpu.VMEM((tok, tq), F32), pltpu.VMEM((tok, tq), BF), pltpu.VMEM((tok, 128), F32)],
        compiler_params=pltpu.CompilerParams(vmem_limit_bytes=34 << 20),
        cost_estimate=pl.CostEstimate(flops=6*2*tok*tok*128, bytes_accessed=4*tok*128, transcendentals=tok*tok),
    )(x)


LANES = 128
CALL = functools.partial(pltpu.CompilerParams, vmem_limit_bytes=20 << 20)


def cost(flops, moved):
    return pl.CostEstimate(flops=int(flops), bytes_accessed=int(moved), transcendentals=0)


def padded(plane):
    width, chans = plane.shape
    return jnp.concatenate([plane.astype(F32), jnp.zeros((LANES - width, chans), F32)], axis=0)


def turn_kernel(rows, core_ref, r_ref, at_ref, all_ref):
    group = r_ref.shape[0]
    frames, chans = at_ref.shape[1:3]
    first = pl.multiple_of(core_ref[0] * rows, rows)
    for f in range(frames):
        for row in range(group + 2):
            if row == 0:
                plane = r_ref[0, frames + f]
            elif row == group + 1:
                plane = r_ref[group - 1, frames + f]
            else:
                plane = r_ref[row - 1, f]
            all_ref[...] = padded(plane).T
            mine = [all_ref[pl.ds(b + first, rows), :] for b in range(0, 2 * chans, 2 * rows)]
            tile = jnp.concatenate(mine, axis=0)
            cols = slice(row * LANES, (row + 1) * LANES)
            at_ref[0, f, :, cols] = pltpu.roll(tile, 1, 1).astype(BF)
            at_ref[1, f, :, cols] = tile.astype(BF)
            at_ref[2, f, :, cols] = pltpu.roll(tile, LANES - 1, 1).astype(BF)


def turn(core, r, frames, rows):
    group, _, _, chans = r.shape
    return pl.pallas_call(
        functools.partial(turn_kernel, rows),
        out_shape=jax.ShapeDtypeStruct((3, frames, chans // 2, (group + 2) * LANES), BF),
        in_specs=[pl.BlockSpec(memory_space=pltpu.SMEM), pl.BlockSpec(memory_space=pltpu.VMEM)],
        scratch_shapes=[pltpu.VMEM((chans, LANES), F32)],
        compiler_params=CALL(),
        cost_estimate=cost(1e9, 6 << 20),
    )(core, r)


def turn_pair_kernel(*refs):
    ins, outs = refs[:4], refs[4:]
    for own, other, out in ((ins[0], ins[1], outs[0]), (ins[2], ins[3], outs[1])):
        count = own.shape[0]
        for d, src in enumerate((own, other)):
            for f in range(count):
                at = (d * count + f) * LANES
                out[:, at : at + LANES] = padded(src[f]).T.astype(BF)


def turn_pair(own_r, other_r, own_b, other_b):
    chans = own_r.shape[-1]
    return pl.pallas_call(
        turn_pair_kernel,
        out_shape=tuple(
            jax.ShapeDtypeStruct((chans, 2 * x.shape[0] * LANES), BF) for x in (own_r, own_b)
        ),
        compiler_params=CALL(),
        cost_estimate=cost(1e9, 4 << 20),
    )(own_r, other_r, own_b, other_b)


def local_terms_kernel(rt_ref, bt_ref, a0_ref, a1_ref, p0_ref, p1_ref, c0_ref, c1_ref, out_ref, at_ref, pay_ref, cot_ref, mix_ref):
    frames, width, chans = a0_ref.shape
    half = chans // 2
    for d, (a, p, c) in enumerate(((a0_ref, p0_ref, c0_ref), (a1_ref, p1_ref, c1_ref))):
        for f in range(frames):
            at = (d * frames + f) * LANES
            at_ref[:, at : at + LANES] = padded(a[f]).T.astype(BF)
            pay_ref[at : at + LANES, :] = padded(p[f]).astype(BF)
            cot_ref[at : at + LANES, :] = padded(c[f]).astype(BF)
    parts, _, rows, _ = out_ref.shape
    block = parts * rows

    def put(first, value, lane=0):
        for n in range(value.shape[0] // block):
            for y in range(parts):
                at = n * block + y * rows
                out_ref[y, first + n, :, lane : lane + value.shape[1]] = value[at : at + rows].astype(BF)

    for k in range(3):
        acc = jnp.zeros((chans, half), F32)
        for d in range(2):
            left = bt_ref[:, (2 * d * frames + k) * LANES : (2 * d * frames + k + frames) * LANES]
            right = pay_ref[d * frames * LANES : (d + 1) * frames * LANES, 3 * half :]
            acc = acc + jnp.dot(left, right, preferred_element_type=F32)
        put(k * chans // block, acc)
    for p in range(3):
        right = pay_ref[:, p * half : (p + 1) * half]
        for lane in range(0, half, LANES):
            value = jnp.dot(rt_ref[...], right[:, lane : lane + LANES], preferred_element_type=F32)
            mix_ref[lane // LANES, pl.ds(p, chans, stride=3), :] = value
    for lane in range(0, half, LANES):
        put(3 * chans // block, mix_ref[lane // LANES], lane)
    put(6 * chans // block, jnp.dot(at_ref[...], cot_ref[...], preferred_element_type=F32))


def local_terms(rt, bt, atted, pay, cot):
    frames, width, chans = atted[0].shape
    half = chans // 2
    span = 2 * frames * LANES
    return pl.pallas_call(
        local_terms_kernel,
        out_shape=jax.ShapeDtypeStruct((4, 7 * chans // 64, 16, half), BF),
        scratch_shapes=[
            pltpu.VMEM((chans, span), BF),
            pltpu.VMEM((span, 4 * half), BF),
            pltpu.VMEM((span, half), BF),
            pltpu.VMEM((half // LANES, 3 * chans, LANES), F32),
        ],
        compiler_params=CALL(),
        cost_estimate=cost(2e9, 10 << 20),
    )(rt, bt, *atted, *pay, *cot)


def conv_terms_kernel(at_ref, dpre_ref, s0_ref, s1_ref, s2_ref, s3_ref, out_ref, dp_ref):
    group, frames, width, cols = dpre_ref.shape
    chans = at_ref.shape[2]
    rows = out_ref.shape[1]
    blocks = chans // rows
    for f in range(frames):
        for row in range(group):
            dp_ref[f, row * LANES : (row + 1) * LANES, :] = padded(dpre_ref[row, f]).astype(BF)
    span = group * LANES
    for i in range(3):
        for j in range(3):
            acc = jnp.zeros((chans, cols), F32)
            for f in range(frames):
                left = at_ref[j, f, :, i * LANES : i * LANES + span]
                acc = acc + jnp.dot(left, dp_ref[f], preferred_element_type=F32)
            value = acc.astype(BF)
            for b in range(blocks):
                out_ref[(3 * i + j) * blocks + b] = value[b * rows : (b + 1) * rows]
    for n in range(s0_ref.shape[0]):
        value = s0_ref[n].astype(F32) + s1_ref[n].astype(F32) + s2_ref[n].astype(F32) + s3_ref[n].astype(F32)
        value = value.astype(BF)
        out_ref[9 * blocks + n] = jnp.concatenate([value[:, :cols], value[:, cols:]], axis=0)


def conv_terms(at, dpre, parts, owners, rows):
    group, frames, width, cols = dpre.shape
    return pl.pallas_call(
        conv_terms_kernel,
        out_shape=jax.ShapeDtypeStruct((owners, rows, cols), BF),
        scratch_shapes=[pltpu.VMEM((frames, group * LANES, cols), BF)],
        compiler_params=CALL(),
        cost_estimate=cost(2e9, 10 << 20),
    )(at, dpre, *parts)


def sum_kernel(norm, dims, which_ref, terms_ref, out_ref):
    times, ys, xs = dims
    rows, cols = terms_ref.shape[1:]

    @pl.when(which_ref[0] == 1)
    def _():
        for x in range(xs):
            for c in range(2):
                acc = jnp.zeros((rows, cols), F32)
                for t in range(times):
                    for y in range(ys):
                        acc = acc + terms_ref[((t * ys + y) * xs + x) * 2 + c].astype(F32)
                out_ref[c * rows : (c + 1) * rows, x * cols : (x + 1) * cols] = acc * norm

    @pl.when(which_ref[0] == 0)
    def _():
        part = rows // 2
        for y in range(ys):
            for c in range(2):
                acc = jnp.zeros((rows, cols), F32)
                for t in range(times):
                    for x in range(xs):
                        acc = acc + terms_ref[((t * ys + y) * xs + x) * 2 + c].astype(F32)
                acc = acc * norm
                for h in range(2):
                    at = (2 * c + h) * cols
                    out_ref[y * part : (y + 1) * part, at : at + cols] = acc[h * part : (h + 1) * part]


def sum_terms(which, terms, norm, dims):
    owners, rows, cols = terms.shape
    return pl.pallas_call(
        functools.partial(sum_kernel, norm, dims),
        out_shape=jax.ShapeDtypeStruct((2 * rows, 4 * cols), F32),
        in_specs=[pl.BlockSpec(memory_space=pltpu.SMEM), pl.BlockSpec(memory_space=pltpu.VMEM)],
        compiler_params=CALL(),
        cost_estimate=cost(1e7, 1 << 20),
    )(which, terms)


def dpre_kernel(own_ref, next_ref, slope_ref, tw_ref, dpre_ref, near_ref):
    frames, width, chans = own_ref.shape
    group, _, _, cols = near_ref.shape
    ext = [own_ref[f] for f in range(frames)] + [next_ref[f] for f in range(frames)]
    for f in range(frames):
        acc = jnp.zeros((width, chans), F32)
        for k in range(3):
            acc = acc + dot_nt(ext[f + 2 - k], tw_ref[k * chans : (k + 1) * chans, :])
        value = (acc * slope_ref[f]).astype(BF)
        dpre_ref[f] = value
        for e in range(group):
            near_ref[e, f] = value[:, (e // 2) * cols : (e // 2 + 1) * cols]


def make_dpre(own, nxt, slope, tw):
    frames, width, chans = own.shape
    return pl.pallas_call(
        dpre_kernel,
        out_shape=(
            jax.ShapeDtypeStruct((frames, width, chans), BF),
            jax.ShapeDtypeStruct((GROUP, frames, width, 2 * chans // GROUP), BF),
        ),
        compiler_params=CALL(),
        cost_estimate=cost(5e8, 3 << 20),
    )(own, nxt, slope, tw)


def dact_kernel(mid_ref, above_ref, below_ref, dres_ref, x_ref, sw_ref, out_ref):
    frames, width, chans = mid_ref.shape
    line = lax.broadcasted_iota(jnp.int32, (width, chans), 0)
    for f in range(frames):
        acc = jnp.zeros((width, chans), F32)
        for i, src in enumerate((below_ref, mid_ref, above_ref)):
            plane = src[f]
            wide = plane.astype(F32)
            right = jnp.where(line == width - 1, 0.0, pltpu.roll(wide, width - 1, 0)).astype(BF)
            left = jnp.where(line == 0, 0.0, pltpu.roll(wide, 1, 0)).astype(BF)
            for j, value in enumerate((right, plane, left)):
                tap = 3 * i + j
                acc = acc + dot_nt(value, sw_ref[tap * chans : (tap + 1) * chans, :])
        x = x_ref[f].astype(F32)
        sigma = 1.0 / (1.0 + jnp.exp(-x))
        slope = sigma * (1.0 + x * (1.0 - sigma))
        out_ref[f] = (dres_ref[f] + acc * slope).astype(BF)


def make_grad_latents(mid, above, below, dres, x, sw):
    return pl.pallas_call(
        dact_kernel,
        out_shape=jax.ShapeDtypeStruct(mid.shape, BF),
        compiler_params=CALL(),
        cost_estimate=cost(2e9, 8 << 20),
    )(mid, above, below, dres, x, sw)


def conv_kernel(mid_ref, above_ref, below_ref, first_ref, sw_ref, bact_ref, slope_ref, rows_ref, taps_ref, acc_ref):
    step = pl.program_id(0)
    frames, width, chans = mid_ref.shape
    line = lax.broadcasted_iota(jnp.int32, (width, chans), 0)

    def silu(value):
        return value / (1.0 + jnp.exp(-value))

    @pl.when(step == 0)
    def _():
        pad = jnp.zeros((LANES - width, chans), F32)
        outer = jnp.where(first_ref[0] == 1, 1.0, 0.0)
        for f in range(frames):
            planes = [silu(src[f].astype(F32)) for src in (above_ref, mid_ref, below_ref)]
            rows_ref[f] = planes[1].astype(BF)
            rows_ref[frames + f] = (outer * planes[0] + (1.0 - outer) * planes[2]).astype(BF)
            at = slice(f * LANES, (f + 1) * LANES)
            for i, plane in enumerate(planes):
                left = jnp.where(line == 0, 0.0, pltpu.roll(plane, 1, 0))
                right = jnp.where(line == width - 1, 0.0, pltpu.roll(plane, width - 1, 0))
                for j, value in enumerate((left, plane, right)):
                    taps_ref[3 * i + j, at, :] = jnp.concatenate([value, pad], axis=0).astype(BF)

    total = jnp.zeros(acc_ref.shape, F32)
    for j in range(3):
        total = total + jnp.dot(
            taps_ref[3 * step + j], sw_ref[j * chans : (j + 1) * chans, :], preferred_element_type=F32
        )

    @pl.when(step == 0)
    def _():
        acc_ref[...] = total

    @pl.when(step > 0)
    def _():
        acc_ref[...] += total

    @pl.when(step == 2)
    def _():
        for f in range(frames):
            pre = acc_ref[f * LANES : f * LANES + width, :]
            sigma = 1.0 / (1.0 + jnp.exp(-pre))
            bact_ref[f] = (pre * sigma).astype(BF)
            slope_ref[f] = sigma * (1.0 + pre * (1.0 - sigma))


def conv(mid, above, below, first, sw):
    frames, width, chans = mid.shape
    whole = pl.BlockSpec((frames, width, chans), lambda i: (0, 0, 0))
    return pl.pallas_call(
        conv_kernel,
        grid=(3,),
        in_specs=[whole, whole, whole, pl.BlockSpec(memory_space=pltpu.SMEM), pl.BlockSpec((3 * chans, chans), lambda i: (i, 0))],
        out_specs=(whole, whole, pl.BlockSpec((2 * frames, width, chans), lambda i: (0, 0, 0))),
        out_shape=(
            jax.ShapeDtypeStruct((frames, width, chans), BF),
            jax.ShapeDtypeStruct((frames, width, chans), F32),
            jax.ShapeDtypeStruct((2 * frames, width, chans), BF),
        ),
        scratch_shapes=[pltpu.VMEM((9, frames * LANES, chans), BF), pltpu.VMEM((frames * LANES, chans), F32)],
        compiler_params=CALL(),
        cost_estimate=cost(1.2e9, 6 << 20),
    )(mid, above, below, first, sw)


def matmul(left, right):
    return jnp.dot(left, right, preferred_element_type=F32)


def shift(x, axis, by):
    count = lax.axis_size(axis)
    pairs = [(i, i + by) for i in range(count) if 0 <= i + by < count]
    return lax.ppermute(x, axis, pairs)


def swap(x):
    count = lax.axis_size("space")
    return lax.ppermute(x, "space", [(i, i ^ 1) for i in range(count)])


def neighbours(field):
    return shift(field, "space", 1), shift(field, "space", -1)


def groups_of(count):
    return [list(range(at, at + GROUP)) for at in range(0, count, GROUP)]


def exchange(x):
    groups = groups_of(lax.axis_size("space"))
    return lax.all_to_all(x, "space", 0, 0, axis_index_groups=groups, tiled=True)


def along_y(x, by):
    count = lax.axis_size("space")
    return lax.ppermute(x, "space", [(i, (i + by * GROUP) % count) for i in range(count)])


def pick_one(x, index):
    return lax.dynamic_index_in_dim(x, index, 0, keepdims=False)


def per_device(latents, spatial_weight, temporal_weight, qkv_weight, out_weight, cotangent):
    frames, rows, width, chans = latents.shape
    ntok = frames * width
    n_space = lax.axis_size("space")
    n_time = lax.axis_size("tm")
    owners = n_space * n_time
    depth = chans // HEADS
    norm = 1.0 / math.sqrt(ntok * n_space * n_time)
    here = lax.axis_index("space")
    core, line = here % 2, here // GROUP
    half = chans // 2
    share = 16 * chans // (2 * owners)

    x = latents.reshape(frames, width, chans)
    cot = cotangent.reshape(frames, width, chans)
    above, below = neighbours(x)
    first = (here % GROUP == 0).astype(jnp.int32).reshape(1)
    bact, slope, planes = conv(x, above, below, first, spatial_weight)
    bext = jnp.concatenate([shift(bact, "tm", 1), bact], axis=0)
    groups = groups_of(n_space)
    early = lax.all_gather(planes, "space", axis=0, axis_index_groups=groups, tiled=True)
    resid, rres, items = proj(x, bext, cot, temporal_weight, qkv_weight, out_weight)
    items = items.reshape(frames * HEADS, width, 4 * depth)
    items = lax.all_to_all(items, "space", 0, 0, tiled=True)

    chalf = cot.reshape(frames, width, 2, half).transpose(2, 0, 1, 3)
    cpair = (pick_one(chalf, core), swap(pick_one(chalf, 1 - core)))
    rother, bother = swap(rres), swap(bext)
    cpair, rother, bother, items = lax.optimization_barrier((cpair, rother, bother, items))
    outs = attn(items.reshape(n_space * width, 4 * depth)).reshape(n_space, width, 4 * depth)
    outs = lax.all_to_all(outs, "space", 0, 0, tiled=True)
    aturn = turn(core.astype(jnp.int32).reshape(1), early.reshape(GROUP, 2 * frames, width, chans), frames, share)
    rturn, bturn = turn_pair(rres, rother, bext, bother)
    outs, aturn, rturn, bturn = lax.optimization_barrier((outs, aturn, rturn, bturn))

    outs = outs.reshape(frames, HEADS, width, 4 * depth)
    dres, dresb = make_dres(outs, cot, qkv_weight)
    dnext = shift(dresb, "tm", -1)
    atted, pay = pack(outs, dresb)
    apair = (atted, swap(atted))
    ppair = (pick_one(pay, core), swap(pick_one(pay, 1 - core)))
    local = local_terms(rturn, bturn, apair, ppair, cpair)
    local, dnext = lax.optimization_barrier((local, dnext))
    dpre, near = make_dpre(dresb, dnext, slope, temporal_weight)
    near, local = lax.optimization_barrier((near, local))
    near = exchange(near)
    dabove, dbelow = neighbours(dpre)
    parts = [pick_one(local, line)]
    for by in range(1, 4):
        parts.append(along_y(pick_one(local, (line + by) % 4), by))
    mixed = resid.reshape(ntok, chans) + matmul(atted.reshape(ntok, chans), out_weight)
    mixed = mixed.astype(BF).reshape(latents.shape)
    mixed, dabove, dbelow, near = lax.optimization_barrier((mixed, dabove, dbelow, near))
    terms = conv_terms(aturn, near, parts, owners, share)
    terms, dpre = lax.optimization_barrier((terms, dpre))
    terms = lax.all_to_all(terms, ("tm", "space"), 0, 0, tiled=True)
    grad_latents = make_grad_latents(dpre, dabove, dbelow, dres, x, spatial_weight).reshape(latents.shape)
    index = lax.axis_index("tm") * n_space + here
    which = (index < 9 * chans // (2 * share)).astype(jnp.int32).reshape(1)
    grad_weights = sum_terms(which, terms, norm, (n_time, n_space // GROUP, GROUP // 2))
    return (mixed, grad_latents, grad_weights)


def solution(mesh):
    placed = (P("tm", "space", None, None), P(), P(), P(), P(), P("tm", "space", None, None))
    return jax.shard_map(
        per_device,
        mesh=mesh,
        in_specs=placed,
        out_specs=(
            P("tm", "space", None, None),
            P("tm", "space", None, None),
            P(("tm", "space"), None),
        ),
        check_vma=False,
    )
```

```python
import functools
import math

import jax
import jax.numpy as jnp
from jax import lax
from jax.experimental import pallas as pl
from jax.experimental.pallas import tpu as pltpu
from jax.sharding import PartitionSpec as P

HEADS = 16
GROUP = 8
F32 = jnp.float32
BF = jnp.bfloat16
NT = (((1,), (1,)), ((), ()))

LANES = 128
CALL = functools.partial(pltpu.CompilerParams, vmem_limit_bytes=20 << 20)
SMALL = pl.CostEstimate(flops=10**6, bytes_accessed=1 << 16, transcendentals=0)


def dot_nt(left, right):
    return lax.dot_general(left, right, NT, preferred_element_type=F32)


def proj_kernel(x_ref, bext_ref, cot_ref, tw_ref, qw_ref, ow_ref, resid_ref, rres_ref, items_ref):
    frames, width, chans = x_ref.shape
    d = chans // HEADS
    for f in range(frames):
        acc = x_ref[f].astype(F32)
        for k in range(3):
            tap = tw_ref[k * chans : (k + 1) * chans, :]
            acc = acc + jnp.dot(bext_ref[f + k], tap, preferred_element_type=F32)
        resid_ref[f] = acc
        rounded = acc.astype(BF)
        rres_ref[f] = rounded
        qkv = jnp.dot(rounded, qw_ref[...], preferred_element_type=F32)
        dattn = dot_nt(cot_ref[f], ow_ref[...])
        for h in range(HEADS):
            parts = [qkv[:, p * chans + h * d : p * chans + (h + 1) * d] for p in range(3)]
            parts.append(dattn[:, h * d : (h + 1) * d])
            items_ref[f, h] = jnp.concatenate(parts, axis=1).astype(BF)


def proj(x, bext, cot, tw, qw, ow):
    frames, width, chans = x.shape
    return pl.pallas_call(
        proj_kernel,
        out_shape=(
            jax.ShapeDtypeStruct((frames, width, chans), F32),
            jax.ShapeDtypeStruct((frames, width, chans), BF),
            jax.ShapeDtypeStruct((frames, HEADS, width, 4 * chans // HEADS), BF),
        ),
        compiler_params=CALL(),
        cost_estimate=SMALL,
    )(x, bext, cot, tw, qw, ow)


def columns(z_ref, f, part, d):
    return jnp.concatenate([z_ref[f, h].astype(F32)[:, part * d : (part + 1) * d] for h in range(HEADS)], axis=1)


def dres_kernel(z_ref, cot_ref, qw_ref, dres_ref, dresb_ref):
    frames, width, chans = cot_ref.shape
    d = chans // HEADS
    for f in range(frames):
        dres = cot_ref[f].astype(F32)
        for p in range(3):
            part = columns(z_ref, f, p + 1, d).astype(BF)
            dres = dres + dot_nt(part, qw_ref[:, p * chans : (p + 1) * chans])
        dres_ref[f] = dres
        dresb_ref[f] = dres.astype(BF)


def make_dres(z, cot, qw):
    return pl.pallas_call(
        dres_kernel,
        out_shape=(jax.ShapeDtypeStruct(cot.shape, F32), jax.ShapeDtypeStruct(cot.shape, BF)),
        compiler_params=CALL(),
        cost_estimate=SMALL,
    )(z, cot, qw)


def pack_kernel(core_ref, z_ref, dresb_ref, attn_ref, mine_ref, other_ref):
    frames, width, chans = dresb_ref.shape
    half = chans // 2

    def halves(f, first, second):
        parts = [columns(z_ref, f, p, chans // HEADS).astype(BF) for p in range(1, 4)]
        for at, part in enumerate(parts + [dresb_ref[f]]):
            for out, c in ((first, 0), (second, 1)):
                out[f, :, at * half : (at + 1) * half] = part[:, c * half : (c + 1) * half]

    for f in range(frames):
        attn_ref[f] = columns(z_ref, f, 0, chans // HEADS).astype(BF)

    @pl.when(core_ref[0] == 0)
    def _():
        for f in range(frames):
            halves(f, mine_ref, other_ref)

    @pl.when(core_ref[0] == 1)
    def _():
        for f in range(frames):
            halves(f, other_ref, mine_ref)


def pack(core, z, dresb):
    frames, width, chans = dresb.shape
    return pl.pallas_call(
        pack_kernel,
        out_shape=(
            jax.ShapeDtypeStruct((frames, width, chans), BF),
            jax.ShapeDtypeStruct((frames, width, 2 * chans), BF),
            jax.ShapeDtypeStruct((frames, width, 2 * chans), BF),
        ),
        in_specs=[pl.BlockSpec(memory_space=pltpu.SMEM)] + [pl.BlockSpec(memory_space=pltpu.VMEM)] * 2,
        compiler_params=CALL(),
        cost_estimate=SMALL,
    )(core, z, dresb)


def attn_kernel(scale, tq, ck, un, x_ref, o_ref, a_ref, kt_ref, vt_ref, s_ref, e_ref, acc_ref):
    tok = x_ref.shape[0]
    step = pl.program_id(0)
    nck = tok // ck
    d = 32
    @pl.when(step == 0)
    def _():
        k = x_ref[:, d:2*d]
        v = x_ref[:, 2*d:3*d]
        lane = lax.broadcasted_iota(jnp.int32, (tok, d), 1)
        ones = jnp.where(lane < 3, 1.0, 0.0).astype(BF)
        a_ref[...] = jnp.concatenate([k, k, v, ones], axis=1)
        kt_ref[...] = k.astype(F32).T.astype(BF)
        vt_ref[...] = jnp.concatenate([v, ones], axis=1).astype(F32).T.astype(BF)
        acc_ref[...] = jnp.zeros_like(acc_ref)
    rows = pl.ds(pl.multiple_of(step * tq, tq), tq)
    xb = x_ref[rows, :]
    q = xb[:, 0:d].astype(F32)
    do = xb[:, 3*d:4*d].astype(F32)
    zeros = jnp.zeros((tq, 2*d), BF)
    def split(z):
        hi = z.astype(BF)
        lo = (z - hi.astype(F32)).astype(BF)
        return hi, lo
    qh, ql = split(q * (scale * math.log2(math.e)))
    wq = jnp.concatenate([qh, ql, zeros], axis=1)
    def p1(i, m):
        r = pl.ds(pl.multiple_of(i * ck, ck), ck)
        s = lax.dot_general(a_ref[r, :], wq, NT, preferred_element_type=F32)
        s_ref[r, :] = s
        return jnp.maximum(m, jnp.max(s.reshape(ck // 8, 8, tq), axis=0))
    m = lax.fori_loop(0, nck, p1, jnp.full((8, tq), -jnp.inf, F32), unroll=un)
    m = jnp.max(m, axis=0, keepdims=True)
    def p2(i, o):
        r = pl.ds(pl.multiple_of(i * ck, ck), ck)
        e = jnp.exp2(s_ref[r, :] - m)
        s_ref[r, :] = e
        eb = e.astype(BF)
        e_ref[r, :] = eb
        return o + jnp.dot(vt_ref[:, r], eb, preferred_element_type=F32)
    o = lax.fori_loop(0, nck, p2, jnp.zeros((2*d, tq), F32), unroll=un)
    inv = 1.0 / o[d:d+1, :]
    ot = o[:d] * inv
    ob = ot.T
    delta = jnp.sum(ob * do, axis=1, keepdims=True)
    invc = jnp.broadcast_to(inv, (8, tq)).T[:, 0:1]
    dh = (-delta).astype(BF); dr = -delta - dh.astype(F32)
    dm = dr.astype(BF); dl = (dr - dm.astype(F32)).astype(BF)
    lane = lax.broadcasted_iota(jnp.int32, (tq, d), 1)
    dd = jnp.where(lane == 0, dh.astype(F32), jnp.where(lane == 1, dm.astype(F32), jnp.where(lane == 2, dl.astype(F32), 0.0))).astype(BF)
    wd = jnp.concatenate([zeros, xb[:, 3*d:], dd], axis=1)
    gh, gl = split(do * invc)
    rh, rl = split(q * (invc * scale))
    we = jnp.concatenate([zeros, gh, gl], axis=1)
    ws = jnp.concatenate([rh, rl, zeros], axis=1)
    def p3(i, dq):
        r = pl.ds(pl.multiple_of(i * ck, ck), ck)
        dp = lax.dot_general(a_ref[r, :], wd, NT, preferred_element_type=F32)
        ds = (s_ref[r, :] * dp).astype(BF)
        acc_ref[r, :] += (jnp.dot(ds, ws, preferred_element_type=F32)
                          + jnp.dot(e_ref[r, :], we, preferred_element_type=F32))
        return dq + jnp.dot(kt_ref[:, r], ds, preferred_element_type=F32)
    dq = lax.fori_loop(0, nck, p3, jnp.zeros((d, tq), F32), unroll=un)
    dq = dq * (inv * scale)
    o_ref[rows, 0:2*d] = jnp.concatenate([ot, dq], axis=0).T.astype(BF)
    @pl.when(step == pl.num_programs(0) - 1)
    def _():
        acc = acc_ref[...]
        dk = acc[:, :d] + acc[:, d:2*d]
        dv = acc[:, 2*d:3*d] + acc[:, 3*d:]
        o_ref[:, 2*d:] = jnp.concatenate([dk, dv], axis=1).astype(BF)

def attn(x, tq=768, ck=256, un=15):
    tok = x.shape[0]
    return pl.pallas_call(
        functools.partial(attn_kernel, 1.0/math.sqrt(32), tq, ck, un),
        grid=(tok // tq,),
        in_specs=[pl.BlockSpec((tok, 128), lambda i: (0, 0))],
        out_specs=pl.BlockSpec((tok, 128), lambda i: (0, 0)),
        out_shape=jax.ShapeDtypeStruct((tok, 128), BF),
        scratch_shapes=[pltpu.VMEM((tok, 128), BF), pltpu.VMEM((32, tok), BF), pltpu.VMEM((64, tok), BF),
                        pltpu.VMEM((tok, tq), F32), pltpu.VMEM((tok, tq), BF), pltpu.VMEM((tok, 128), F32)],
        compiler_params=pltpu.CompilerParams(vmem_limit_bytes=34 << 20),
        cost_estimate=pl.CostEstimate(flops=6*2*tok*tok*128, bytes_accessed=4*tok*128, transcendentals=tok*tok),
    )(x)


def padded(plane):
    width, chans = plane.shape
    return jnp.concatenate([plane.astype(F32), jnp.zeros((LANES - width, chans), F32)], axis=0)


def pick_kernel(rows, act_ref, outer_ref, out_ref):
    group = out_ref.shape[0]
    frames, width, chans = act_ref.shape
    for f in range(frames):
        for at, src in ((f, act_ref), (frames + f, outer_ref)):
            plane = src[f].astype(F32)
            for c in range(2):
                parts = [plane[:, b + c * rows : b + (c + 1) * rows] for b in range(0, chans, 2 * rows)]
                part = jnp.concatenate(parts, axis=1).astype(BF)
                for x in range(group // 2):
                    out_ref[2 * x + c, at] = part


def pick(act, outer, rows):
    frames, width, chans = act.shape
    return pl.pallas_call(
        functools.partial(pick_kernel, rows),
        out_shape=jax.ShapeDtypeStruct((GROUP, 2 * frames, width, chans // 2), BF),
        compiler_params=CALL(),
        cost_estimate=SMALL,
    )(act, outer)


def turn_kernel(r_ref, at_ref):
    group = r_ref.shape[0]
    frames = at_ref.shape[1]
    for f in range(frames):
        for row in range(group + 2):
            if row == 0:
                plane = r_ref[0, frames + f]
            elif row == group + 1:
                plane = r_ref[group - 1, frames + f]
            else:
                plane = r_ref[row - 1, f]
            tile = padded(plane).T
            cols = slice(row * LANES, (row + 1) * LANES)
            at_ref[0, f, :, cols] = pltpu.roll(tile, 1, 1).astype(BF)
            at_ref[1, f, :, cols] = tile.astype(BF)
            at_ref[2, f, :, cols] = pltpu.roll(tile, LANES - 1, 1).astype(BF)


def turn(r, frames):
    group, _, _, chans = r.shape
    return pl.pallas_call(
        turn_kernel,
        out_shape=jax.ShapeDtypeStruct((3, frames, chans, (group + 2) * LANES), BF),
        compiler_params=CALL(),
        cost_estimate=SMALL,
    )(r)


def turn_pair_kernel(*refs):
    ins, outs = refs[:4], refs[4:]
    for own, other, out in ((ins[0], ins[1], outs[0]), (ins[2], ins[3], outs[1])):
        count = own.shape[0]
        for d, src in enumerate((own, other)):
            for f in range(count):
                at = (d * count + f) * LANES
                out[:, at : at + LANES] = padded(src[f]).T.astype(BF)


def turn_pair(own_r, other_r, own_b, other_b):
    chans = own_r.shape[-1]
    return pl.pallas_call(
        turn_pair_kernel,
        out_shape=tuple(
            jax.ShapeDtypeStruct((chans, 2 * x.shape[0] * LANES), BF) for x in (own_r, own_b)
        ),
        compiler_params=CALL(),
        cost_estimate=SMALL,
    )(own_r, other_r, own_b, other_b)


def local_terms_kernel(
    line_ref, rt_ref, bt_ref, a0_ref, a1_ref, p0_ref, p1_ref, c0_ref, c1_ref, *refs
):
    outs, (at_ref, pay_ref, cot_ref, mix_ref) = refs[:4], refs[4:]
    frames, width, chans = a0_ref.shape
    half = chans // 2
    for d, (a, p, c) in enumerate(((a0_ref, p0_ref, c0_ref), (a1_ref, p1_ref, c1_ref))):
        for f in range(frames):
            at = (d * frames + f) * LANES
            at_ref[:, at : at + LANES] = padded(a[f]).T.astype(BF)
            pay_ref[at : at + LANES, :] = padded(p[f]).astype(BF)
            cot_ref[at : at + LANES, :] = padded(c[f]).astype(BF)
    _, rows, _ = outs[0].shape
    block = rows * len(outs)
    starts = [pl.multiple_of(lax.rem(line_ref[0] + k, len(outs)) * rows, rows) for k in range(len(outs))]

    def put(first, count, lane):
        for n in range(count // block):
            for start, out in zip(starts, outs):
                value = mix_ref[lane // LANES, pl.ds(n * block + start, rows), :]
                out[first + n, :, lane : lane + LANES] = value.astype(BF)

    def put_whole(first, value):
        for lane in range(0, half, LANES):
            mix_ref[lane // LANES, 0 : value.shape[0], :] = value[:, lane : lane + LANES]
            put(first, value.shape[0], lane)

    for k in range(3):
        acc = jnp.zeros((chans, half), F32)
        for d in range(2):
            left = bt_ref[:, (2 * d * frames + k) * LANES : (2 * d * frames + k + frames) * LANES]
            right = pay_ref[d * frames * LANES : (d + 1) * frames * LANES, 3 * half :]
            acc = acc + jnp.dot(left, right, preferred_element_type=F32)
        put_whole(k * chans // block, acc)
    for p in range(3):
        right = pay_ref[:, p * half : (p + 1) * half]
        for lane in range(0, half, LANES):
            value = jnp.dot(rt_ref[...], right[:, lane : lane + LANES], preferred_element_type=F32)
            mix_ref[lane // LANES, pl.ds(p, chans, stride=3), :] = value
    for lane in range(0, half, LANES):
        put(3 * chans // block, 3 * chans, lane)
    put_whole(6 * chans // block, jnp.dot(at_ref[...], cot_ref[...], preferred_element_type=F32))


def local_terms(line, rt, bt, atted, pay, cot):
    frames, width, chans = atted[0].shape
    half = chans // 2
    span = 2 * frames * LANES
    return pl.pallas_call(
        local_terms_kernel,
        out_shape=(jax.ShapeDtypeStruct((7 * chans // 64, 16, half), BF),) * 4,
        in_specs=[pl.BlockSpec(memory_space=pltpu.SMEM)] + [pl.BlockSpec(memory_space=pltpu.VMEM)] * 8,
        scratch_shapes=[
            pltpu.VMEM((chans, span), BF),
            pltpu.VMEM((span, 4 * half), BF),
            pltpu.VMEM((span, half), BF),
            pltpu.VMEM((half // LANES, 3 * chans, LANES), F32),
        ],
        compiler_params=CALL(),
        cost_estimate=SMALL,
    )(line, rt, bt, *atted, *pay, *cot)


def conv_terms_kernel(at_ref, dpre_ref, s0_ref, s1_ref, s2_ref, s3_ref, out_ref, dp_ref):
    group, frames, width, cols = dpre_ref.shape
    chans = at_ref.shape[2]
    rows = out_ref.shape[1]
    blocks = chans // rows
    for f in range(frames):
        for row in range(group):
            dp_ref[f, row * LANES : (row + 1) * LANES, :] = padded(dpre_ref[row, f]).astype(BF)
    span = group * LANES
    for i in range(3):
        for j in range(3):
            acc = jnp.zeros((chans, cols), F32)
            for f in range(frames):
                left = at_ref[j, f, :, i * LANES : i * LANES + span]
                acc = acc + jnp.dot(left, dp_ref[f], preferred_element_type=F32)
            value = acc.astype(BF)
            for b in range(blocks):
                out_ref[(3 * i + j) * blocks + b] = value[b * rows : (b + 1) * rows]
    for n in range(s0_ref.shape[0]):
        value = s0_ref[n].astype(F32) + s1_ref[n].astype(F32) + s2_ref[n].astype(F32) + s3_ref[n].astype(F32)
        value = value.astype(BF)
        out_ref[9 * blocks + n] = jnp.concatenate([value[:, :cols], value[:, cols:]], axis=0)


def conv_terms(at, dpre, parts, owners, rows):
    group, frames, width, cols = dpre.shape
    return pl.pallas_call(
        conv_terms_kernel,
        out_shape=jax.ShapeDtypeStruct((owners, rows, cols), BF),
        scratch_shapes=[pltpu.VMEM((frames, group * LANES, cols), BF)],
        compiler_params=CALL(),
        cost_estimate=SMALL,
    )(at, dpre, *parts)


def sum_kernel(norm, dims, which_ref, terms_ref, out_ref):
    times, ys, xs = dims
    rows, cols = terms_ref.shape[1:]

    @pl.when(which_ref[0] == 1)
    def _():
        for x in range(xs):
            for c in range(2):
                acc = jnp.zeros((rows, cols), F32)
                for t in range(times):
                    for y in range(ys):
                        acc = acc + terms_ref[((t * ys + y) * xs + x) * 2 + c].astype(F32)
                out_ref[c * rows : (c + 1) * rows, x * cols : (x + 1) * cols] = acc * norm

    @pl.when(which_ref[0] == 0)
    def _():
        part = rows // 2
        for y in range(ys):
            for c in range(2):
                acc = jnp.zeros((rows, cols), F32)
                for t in range(times):
                    for x in range(xs):
                        acc = acc + terms_ref[((t * ys + y) * xs + x) * 2 + c].astype(F32)
                acc = acc * norm
                for h in range(2):
                    at = (2 * c + h) * cols
                    out_ref[y * part : (y + 1) * part, at : at + cols] = acc[h * part : (h + 1) * part]


def sum_terms(which, terms, norm, dims):
    owners, rows, cols = terms.shape
    return pl.pallas_call(
        functools.partial(sum_kernel, norm, dims),
        out_shape=jax.ShapeDtypeStruct((2 * rows, 4 * cols), F32),
        in_specs=[pl.BlockSpec(memory_space=pltpu.SMEM), pl.BlockSpec(memory_space=pltpu.VMEM)],
        compiler_params=CALL(),
        cost_estimate=SMALL,
    )(which, terms)


def dpre_kernel(own_ref, next_ref, slope_ref, tw_ref, dpre_ref, near_ref):
    frames, width, chans = own_ref.shape
    group, _, _, cols = near_ref.shape
    ext = [own_ref[f] for f in range(frames)] + [next_ref[f] for f in range(frames)]
    for f in range(frames):
        acc = jnp.zeros((width, chans), F32)
        for k in range(3):
            acc = acc + dot_nt(ext[f + 2 - k], tw_ref[k * chans : (k + 1) * chans, :])
        value = (acc * slope_ref[f]).astype(BF)
        dpre_ref[f] = value
        for e in range(group):
            near_ref[e, f] = value[:, (e // 2) * cols : (e // 2 + 1) * cols]


def make_dpre(own, nxt, slope, tw):
    frames, width, chans = own.shape
    return pl.pallas_call(
        dpre_kernel,
        out_shape=(
            jax.ShapeDtypeStruct((frames, width, chans), BF),
            jax.ShapeDtypeStruct((GROUP, frames, width, 2 * chans // GROUP), BF),
        ),
        compiler_params=CALL(),
        cost_estimate=SMALL,
    )(own, nxt, slope, tw)


def dact_kernel(mid_ref, above_ref, below_ref, dres_ref, x_ref, sw_ref, out_ref):
    frames, width, chans = mid_ref.shape
    line = lax.broadcasted_iota(jnp.int32, (width, chans), 0)
    for f in range(frames):
        acc = jnp.zeros((width, chans), F32)
        for i, src in enumerate((below_ref, mid_ref, above_ref)):
            plane = src[f]
            wide = plane.astype(F32)
            right = jnp.where(line == width - 1, 0.0, pltpu.roll(wide, width - 1, 0)).astype(BF)
            left = jnp.where(line == 0, 0.0, pltpu.roll(wide, 1, 0)).astype(BF)
            for j, value in enumerate((right, plane, left)):
                tap = 3 * i + j
                acc = acc + dot_nt(value, sw_ref[tap * chans : (tap + 1) * chans, :])
        x = x_ref[f].astype(F32)
        sigma = 1.0 / (1.0 + jnp.exp(-x))
        slope = sigma * (1.0 + x * (1.0 - sigma))
        out_ref[f] = (dres_ref[f] + acc * slope).astype(BF)


def make_grad_latents(mid, above, below, dres, x, sw):
    return pl.pallas_call(
        dact_kernel,
        out_shape=jax.ShapeDtypeStruct(mid.shape, BF),
        compiler_params=CALL(),
        cost_estimate=SMALL,
    )(mid, above, below, dres, x, sw)


def silu_slope(value):
    sigma = jax.nn.sigmoid(value)
    return sigma * (1.0 + value * (1.0 - sigma))


def matmul(left, right):
    return jnp.dot(left, right, preferred_element_type=F32)


def shift(x, axis, by):
    count = lax.axis_size(axis)
    pairs = [(i, i + by) for i in range(count) if 0 <= i + by < count]
    return lax.ppermute(x, axis, pairs)


def swap(x):
    count = lax.axis_size("space")
    return lax.ppermute(x, "space", [(i, i ^ 1) for i in range(count)])


def neighbours(field):
    return shift(field, "space", 1), shift(field, "space", -1)


def exchange(x):
    count = lax.axis_size("space")
    groups = [list(range(at, at + GROUP)) for at in range(0, count, GROUP)]
    return lax.all_to_all(x, "space", 0, 0, axis_index_groups=groups, tiled=True)


def along_y(x, by):
    count = lax.axis_size("space")
    return lax.ppermute(x, "space", [(i, (i + by * GROUP) % count) for i in range(count)])


def as_ref(scalar):
    return scalar.astype(jnp.int32).reshape(1)


def pick_one(x, index):
    return lax.dynamic_index_in_dim(x, index, 0, keepdims=False)


def side_pad(field):
    return jnp.pad(field, ((0, 0), (0, 0), (1, 1), (0, 0)))


def taps_of(padded, width):
    pieces = [padded[:, i, j : j + width] for i in range(3) for j in range(3)]
    return jnp.concatenate(pieces, axis=-1).reshape(-1, 9 * padded.shape[-1])


def per_device(latents, spatial_weight, temporal_weight, qkv_weight, out_weight, cotangent):
    frames, rows, width, chans = latents.shape
    ntok = frames * width
    n_space = lax.axis_size("space")
    n_time = lax.axis_size("tm")
    owners = n_space * n_time
    depth = chans // HEADS
    norm = 1.0 / math.sqrt(ntok * n_space * n_time)
    here = lax.axis_index("space")
    core, line = here % 2, here // GROUP
    half = chans // 2
    share = 16 * chans // (2 * owners)

    x = latents.reshape(frames, width, chans)
    cot = cotangent.reshape(frames, width, chans)
    act = jax.nn.silu(x.astype(F32)).astype(BF)
    above, below = neighbours(act)
    pre = matmul(taps_of(side_pad(jnp.stack([above, act, below], axis=1)), width), spatial_weight)
    pre = pre.reshape(frames, width, chans)
    bact = jax.nn.silu(pre).astype(BF)
    bext = jnp.concatenate([shift(bact, "tm", 1), bact], axis=0)
    resid, rres, items = proj(x, bext, cot, temporal_weight, qkv_weight, out_weight)
    items = items.reshape(frames * HEADS, width, 4 * depth)
    items = lax.all_to_all(items, "space", 0, 0, tiled=True)

    early = pick(act, jnp.where(here % GROUP == 0, above, below), share)
    chalf = cot.reshape(frames, width, 2, half).transpose(2, 0, 1, 3)
    cpair = (pick_one(chalf, core), swap(pick_one(chalf, 1 - core)))
    rother, bother = swap(rres), swap(bext)
    early, cpair, rother, bother, items = lax.optimization_barrier((early, cpair, rother, bother, items))
    early = exchange(early)
    outs = attn(items.reshape(n_space * width, 4 * depth)).reshape(n_space, width, 4 * depth)
    outs, early, rother, bother = lax.optimization_barrier((outs, early, rother, bother))
    outs = lax.all_to_all(outs, "space", 0, 0, tiled=True)
    aturn = turn(early, frames)
    rturn, bturn = turn_pair(rres, rother, bext, bother)
    slope = silu_slope(pre)
    outs, aturn, rturn, bturn, slope = lax.optimization_barrier((outs, aturn, rturn, bturn, slope))

    outs = outs.reshape(frames, HEADS, width, 4 * depth)
    dres, dresb = make_dres(outs, cot, qkv_weight)
    dnext = shift(dresb, "tm", -1)
    atted, mine, other = pack(as_ref(core), outs, dresb)
    local = local_terms(as_ref(line), rturn, bturn, (atted, swap(atted)), (mine, swap(other)), cpair)
    parts = [local[0]] + [along_y(local[by], by) for by in range(1, 4)]
    dpre, near = make_dpre(dresb, dnext, slope, temporal_weight)
    near = exchange(near)
    dabove, dbelow = neighbours(dpre)
    mixed = resid.reshape(ntok, chans) + matmul(atted.reshape(ntok, chans), out_weight)
    mixed = mixed.astype(BF).reshape(latents.shape)
    mixed, dabove, dbelow, near = lax.optimization_barrier((mixed, dabove, dbelow, near))
    terms = conv_terms(aturn, near, parts, owners, share)
    terms, dpre = lax.optimization_barrier((terms, dpre))
    terms = lax.all_to_all(terms, ("tm", "space"), 0, 0, tiled=True)
    grad_latents = make_grad_latents(dpre, dabove, dbelow, dres, x, spatial_weight).reshape(latents.shape)
    index = lax.axis_index("tm") * n_space + here
    which = (index < 9 * chans // (2 * share)).astype(jnp.int32).reshape(1)
    grad_weights = sum_terms(which, terms, norm, (n_time, n_space // GROUP, GROUP // 2))
    return (mixed, grad_latents, grad_weights)


def solution(mesh):
    placed = (P("tm", "space", None, None), P(), P(), P(), P(), P("tm", "space", None, None))
    return jax.shard_map(
        per_device,
        mesh=mesh,
        in_specs=placed,
        out_specs=(
            P("tm", "space", None, None),
            P("tm", "space", None, None),
            P(("tm", "space"), None),
        ),
        check_vma=False,
    )
```

```python
import functools
import math

import jax
import jax.numpy as jnp
from jax import lax
from jax.experimental import pallas as pl
from jax.experimental.pallas import tpu as pltpu
from jax.sharding import PartitionSpec as P

HEADS = 16
GROUP = 8
F32 = jnp.float32
BF = jnp.bfloat16
NT = (((1,), (1,)), ((), ()))

def dot_nt(left, right):
    return lax.dot_general(left, right, NT, preferred_element_type=F32)


def proj_kernel(x_ref, bext_ref, cot_ref, tw_ref, qw_ref, ow_ref, resid_ref, rres_ref, items_ref):
    frames, width, chans = x_ref.shape
    d = chans // HEADS
    for f in range(frames):
        acc = x_ref[f].astype(F32)
        for k in range(3):
            tap = tw_ref[k * chans : (k + 1) * chans, :]
            acc = acc + jnp.dot(bext_ref[f + k], tap, preferred_element_type=F32)
        resid_ref[f] = acc
        rounded = acc.astype(BF)
        rres_ref[f] = rounded
        qkv = jnp.dot(rounded, qw_ref[...], preferred_element_type=F32)
        dattn = dot_nt(cot_ref[f], ow_ref[...])
        for h in range(HEADS):
            parts = [qkv[:, p * chans + h * d : p * chans + (h + 1) * d] for p in range(3)]
            parts.append(dattn[:, h * d : (h + 1) * d])
            items_ref[f, h] = jnp.concatenate(parts, axis=1).astype(BF)


def proj(x, bext, cot, tw, qw, ow):
    frames, width, chans = x.shape
    return pl.pallas_call(
        proj_kernel,
        out_shape=(
            jax.ShapeDtypeStruct((frames, width, chans), F32),
            jax.ShapeDtypeStruct((frames, width, chans), BF),
            jax.ShapeDtypeStruct((frames, HEADS, width, 4 * chans // HEADS), BF),
        ),
        compiler_params=pltpu.CompilerParams(vmem_limit_bytes=32 << 20),
        cost_estimate=pl.CostEstimate(flops=10**9 * 2, bytes_accessed=6 << 20, transcendentals=0),
    )(x, bext, cot, tw, qw, ow)


def post_kernel(core_ref, z_ref, cot_ref, qw_ref, attn_ref, dres_ref, dresb_ref, mine_ref, other_ref):
    frames, width, chans = cot_ref.shape
    d = chans // HEADS
    half = chans // 2
    all_parts = []
    for f in range(frames):
        heads = [z_ref[f, h].astype(F32) for h in range(HEADS)]
        dres = cot_ref[f].astype(F32)
        parts = [jnp.concatenate([z[:, p * d : (p + 1) * d] for z in heads], axis=1).astype(BF) for p in range(4)]
        attn_ref[f] = parts[0]
        for p in range(3):
            dres = dres + dot_nt(parts[p + 1], qw_ref[:, p * chans : (p + 1) * chans])
        dres_ref[f] = dres
        dresb = dres.astype(BF)
        dresb_ref[f] = dresb
        all_parts.append(parts[1:] + [dresb])

    def store(first, second):
        for f in range(frames):
            for at, part in enumerate(all_parts[f]):
                for out, c in ((first, 0), (second, 1)):
                    out[f, :, at * half : (at + 1) * half] = part[:, c * half : (c + 1) * half]

    @pl.when(core_ref[0] == 0)
    def _():
        store(mine_ref, other_ref)

    @pl.when(core_ref[0] == 1)
    def _():
        store(other_ref, mine_ref)


def post(core, z, cot, qw):
    frames, width, chans = cot.shape
    return pl.pallas_call(
        post_kernel,
        out_shape=(
            jax.ShapeDtypeStruct((frames, width, chans), BF),
            jax.ShapeDtypeStruct((frames, width, chans), F32),
            jax.ShapeDtypeStruct((frames, width, chans), BF),
            jax.ShapeDtypeStruct((frames, width, 2 * chans), BF),
            jax.ShapeDtypeStruct((frames, width, 2 * chans), BF),
        ),
        in_specs=[pl.BlockSpec(memory_space=pltpu.SMEM)] + [pl.BlockSpec(memory_space=pltpu.VMEM)] * 3,
        compiler_params=pltpu.CompilerParams(vmem_limit_bytes=32 << 20),
        cost_estimate=pl.CostEstimate(flops=10**9, bytes_accessed=6 << 20, transcendentals=0),
    )(core, z, cot, qw)


def fetch_kernel(w_ref, out_ref):
    out_ref[...] = w_ref[...]


def fetch(w):
    return pl.pallas_call(
        fetch_kernel,
        out_shape=jax.ShapeDtypeStruct(w.shape, w.dtype),
        compiler_params=pltpu.CompilerParams(vmem_limit_bytes=24 << 20),
        cost_estimate=pl.CostEstimate(flops=10**6, bytes_accessed=10 << 20, transcendentals=0),
    )(w)


def attn_kernel(scale, tq, ck, un, x_ref, o_ref, a_ref, kt_ref, vt_ref, s_ref, e_ref, acc_ref):
    tok = x_ref.shape[0]
    step = pl.program_id(0)
    nck = tok // ck
    d = 32
    @pl.when(step == 0)
    def _():
        k = x_ref[:, d:2*d]
        v = x_ref[:, 2*d:3*d]
        lane = lax.broadcasted_iota(jnp.int32, (tok, d), 1)
        ones = jnp.where(lane < 3, 1.0, 0.0).astype(BF)
        a_ref[...] = jnp.concatenate([k, k, v, ones], axis=1)
        kt_ref[...] = k.astype(F32).T.astype(BF)
        vt_ref[...] = jnp.concatenate([v, ones], axis=1).astype(F32).T[: d + 16].astype(BF)
        acc_ref[...] = jnp.zeros_like(acc_ref)
    rows = pl.ds(pl.multiple_of(step * tq, tq), tq)
    xb = x_ref[rows, :]
    q = xb[:, 0:d].astype(F32)
    do = xb[:, 3*d:4*d].astype(F32)
    zeros = jnp.zeros((tq, 2*d), BF)
    def split(z):
        hi = z.astype(BF)
        lo = (z - hi.astype(F32)).astype(BF)
        return hi, lo
    qh, ql = split(q * (scale * math.log2(math.e)))
    wq = jnp.concatenate([qh, ql, zeros], axis=1)
    def p1(i, m):
        r = pl.ds(pl.multiple_of(i * ck, ck), ck)
        s = lax.dot_general(a_ref[r, :], wq, NT, preferred_element_type=F32)
        s_ref[r, :] = s
        return jnp.maximum(m, jnp.max(s.reshape(ck // 8, 8, tq), axis=0))
    m = lax.fori_loop(0, nck, p1, jnp.full((8, tq), -jnp.inf, F32), unroll=un)
    m = jnp.max(m, axis=0, keepdims=True)
    def p2(i, o):
        r = pl.ds(pl.multiple_of(i * ck, ck), ck)
        e = jnp.exp2(s_ref[r, :] - m)
        s_ref[r, :] = e
        eb = e.astype(BF)
        e_ref[r, :] = eb
        return o + jnp.dot(vt_ref[:, r], eb, preferred_element_type=F32)
    o = lax.fori_loop(0, nck, p2, jnp.zeros((d + 16, tq), F32), unroll=un)
    inv = 1.0 / o[d:d+1, :]
    ot = o[:d] * inv
    ob = ot.T
    delta = jnp.sum(ob * do, axis=1, keepdims=True)
    invc = jnp.broadcast_to(inv, (8, tq)).T[:, 0:1]
    dh = (-delta).astype(BF); dr = -delta - dh.astype(F32)
    dm = dr.astype(BF); dl = (dr - dm.astype(F32)).astype(BF)
    lane = lax.broadcasted_iota(jnp.int32, (tq, d), 1)
    dd = jnp.where(lane == 0, dh.astype(F32), jnp.where(lane == 1, dm.astype(F32), jnp.where(lane == 2, dl.astype(F32), 0.0))).astype(BF)
    wd = jnp.concatenate([zeros, xb[:, 3*d:], dd], axis=1)
    gh, gl = split(do * invc)
    rh, rl = split(q * (invc * scale))
    we = jnp.concatenate([zeros, gh, gl], axis=1)
    ws = jnp.concatenate([rh, rl, zeros], axis=1)
    def p3(i, dq):
        r = pl.ds(pl.multiple_of(i * ck, ck), ck)
        dp = lax.dot_general(a_ref[r, :], wd, NT, preferred_element_type=F32)
        ds = (s_ref[r, :] * dp).astype(BF)
        acc_ref[r, :] += (jnp.dot(ds, ws, preferred_element_type=F32)
                          + jnp.dot(e_ref[r, :], we, preferred_element_type=F32))
        return dq + jnp.dot(kt_ref[:, r], ds, preferred_element_type=F32)
    dq = lax.fori_loop(0, nck, p3, jnp.zeros((d, tq), F32), unroll=un)
    dq = dq * (inv * scale)
    o_ref[rows, 0:2*d] = jnp.concatenate([ot, dq], axis=0).T.astype(BF)
    @pl.when(step == pl.num_programs(0) - 1)
    def _():
        acc = acc_ref[...]
        dk = acc[:, :d] + acc[:, d:2*d]
        dv = acc[:, 2*d:3*d] + acc[:, 3*d:]
        o_ref[:, 2*d:] = jnp.concatenate([dk, dv], axis=1).astype(BF)

def attn(x, tq=768, ck=3840, un=1):
    tok = x.shape[0]
    return pl.pallas_call(
        functools.partial(attn_kernel, 1.0/math.sqrt(32), tq, ck, un),
        grid=(tok // tq,),
        in_specs=[pl.BlockSpec((tok, 128), lambda i: (0, 0))],
        out_specs=pl.BlockSpec((tok, 128), lambda i: (0, 0)),
        out_shape=jax.ShapeDtypeStruct((tok, 128), BF),
        scratch_shapes=[pltpu.VMEM((tok, 128), BF), pltpu.VMEM((32, tok), BF), pltpu.VMEM((48, tok), BF),
                        pltpu.VMEM((tok, tq), F32), pltpu.VMEM((tok, tq), BF), pltpu.VMEM((tok, 128), F32)],
        compiler_params=pltpu.CompilerParams(vmem_limit_bytes=48 << 20),
        cost_estimate=pl.CostEstimate(flops=6*2*tok*tok*128, bytes_accessed=4*tok*128, transcendentals=tok*tok),
    )(x)


LANES = 128
CALL = functools.partial(pltpu.CompilerParams, vmem_limit_bytes=40 << 20)


def cost(flops, moved):
    return pl.CostEstimate(flops=int(flops), bytes_accessed=int(moved), transcendentals=0)


def padded(plane):
    width, chans = plane.shape
    return jnp.concatenate([plane.astype(F32), jnp.zeros((LANES - width, chans), F32)], axis=0)


def pick_kernel(rows, act_ref, outer_ref, out_ref):
    group = out_ref.shape[0]
    frames, width, chans = act_ref.shape
    for f in range(frames):
        for at, src in ((f, act_ref), (frames + f, outer_ref)):
            plane = src[f].astype(F32)
            for c in range(2):
                parts = [plane[:, b + c * rows : b + (c + 1) * rows] for b in range(0, chans, 2 * rows)]
                part = jnp.concatenate(parts, axis=1).astype(BF)
                for x in range(group // 2):
                    out_ref[2 * x + c, at] = part


def pick(act, outer, rows):
    frames, width, chans = act.shape
    return pl.pallas_call(
        functools.partial(pick_kernel, rows),
        out_shape=jax.ShapeDtypeStruct((GROUP, 2 * frames, width, chans // 2), BF),
        compiler_params=CALL(),
        cost_estimate=cost(1e8, 3 << 20),
    )(act, outer)


def turn_kernel(r_ref, at_ref):
    group = r_ref.shape[0]
    frames = at_ref.shape[1]
    for f in range(frames):
        for row in range(group + 2):
            if row == 0:
                plane = r_ref[0, frames + f]
            elif row == group + 1:
                plane = r_ref[group - 1, frames + f]
            else:
                plane = r_ref[row - 1, f]
            tile = padded(plane).T
            cols = slice(row * LANES, (row + 1) * LANES)
            at_ref[0, f, :, cols] = pltpu.roll(tile, 1, 1).astype(BF)
            at_ref[1, f, :, cols] = tile.astype(BF)
            at_ref[2, f, :, cols] = pltpu.roll(tile, LANES - 1, 1).astype(BF)


def turn(r, frames):
    group, _, _, chans = r.shape
    return pl.pallas_call(
        turn_kernel,
        out_shape=jax.ShapeDtypeStruct((3, frames, chans, (group + 2) * LANES), BF),
        compiler_params=CALL(),
        cost_estimate=cost(1e9, 6 << 20),
    )(r)


def turn_pair_kernel(*refs):
    ins, outs = refs[:4], refs[4:]
    for own, other, out in ((ins[0], ins[1], outs[0]), (ins[2], ins[3], outs[1])):
        count = own.shape[0]
        for d, src in enumerate((own, other)):
            for f in range(count):
                at = (d * count + f) * LANES
                out[:, at : at + LANES] = padded(src[f]).T.astype(BF)


def turn_pair(own_r, other_r, own_b, other_b):
    chans = own_r.shape[-1]
    return pl.pallas_call(
        turn_pair_kernel,
        out_shape=tuple(
            jax.ShapeDtypeStruct((chans, 2 * x.shape[0] * LANES), BF) for x in (own_r, own_b)
        ),
        compiler_params=CALL(),
        cost_estimate=cost(1e9, 4 << 20),
    )(own_r, other_r, own_b, other_b)


def local_terms_kernel(rt_ref, bt_ref, a0_ref, a1_ref, p0_ref, p1_ref, c0_ref, c1_ref, out_ref, at_ref, pay_ref, cot_ref, mix_ref):
    frames, width, chans = a0_ref.shape
    half = chans // 2
    for d, (a, p, c) in enumerate(((a0_ref, p0_ref, c0_ref), (a1_ref, p1_ref, c1_ref))):
        for f in range(frames):
            at = (d * frames + f) * LANES
            at_ref[:, at : at + LANES] = padded(a[f]).T.astype(BF)
            pay_ref[at : at + LANES, :] = padded(p[f]).astype(BF)
            cot_ref[at : at + LANES, :] = padded(c[f]).astype(BF)
    parts, _, rows, _ = out_ref.shape
    block = parts * rows

    def put(first, value, lane=0):
        for n in range(value.shape[0] // block):
            for y in range(parts):
                at = n * block + y * rows
                out_ref[y, first + n, :, lane : lane + value.shape[1]] = value[at : at + rows].astype(BF)

    for k in range(3):
        acc = jnp.zeros((chans, half), F32)
        for d in range(2):
            left = bt_ref[:, (2 * d * frames + k) * LANES : (2 * d * frames + k + frames) * LANES]
            right = pay_ref[d * frames * LANES : (d + 1) * frames * LANES, 3 * half :]
            acc = acc + jnp.dot(left, right, preferred_element_type=F32)
        put(k * chans // block, acc)
    for p in range(3):
        right = pay_ref[:, p * half : (p + 1) * half]
        for lane in range(0, half, LANES):
            value = jnp.dot(rt_ref[...], right[:, lane : lane + LANES], preferred_element_type=F32)
            mix_ref[lane // LANES, pl.ds(p, chans, stride=3), :] = value
    for lane in range(0, half, LANES):
        put(3 * chans // block, mix_ref[lane // LANES], lane)
    put(6 * chans // block, jnp.dot(at_ref[...], cot_ref[...], preferred_element_type=F32))


def local_terms(rt, bt, atted, pay, cot):
    frames, width, chans = atted[0].shape
    half = chans // 2
    span = 2 * frames * LANES
    return pl.pallas_call(
        local_terms_kernel,
        out_shape=jax.ShapeDtypeStruct((4, 7 * chans // 64, 16, half), BF),
        scratch_shapes=[
            pltpu.VMEM((chans, span), BF),
            pltpu.VMEM((span, 4 * half), BF),
            pltpu.VMEM((span, half), BF),
            pltpu.VMEM((half // LANES, 3 * chans, LANES), F32),
        ],
        compiler_params=CALL(),
        cost_estimate=cost(2e9, 10 << 20),
    )(rt, bt, *atted, *pay, *cot)


def conv_terms_kernel(at_ref, dpre_ref, *refs):
    parts, (out_ref, dp_ref, part_ref, sems) = refs[:4], refs[4:]
    step = pl.program_id(0)
    group, frames, width, cols = dpre_ref.shape
    chans = at_ref.shape[2]
    rows = out_ref.shape[1]
    blocks = chans // rows
    copies = [pltpu.make_async_copy(src, part_ref.at[k], sems.at[k]) for k, src in enumerate(parts)]

    @pl.when(step == 0)
    def _():
        for copy in copies:
            copy.start()
        for f in range(frames):
            for row in range(group):
                dp_ref[f, row * LANES : (row + 1) * LANES, :] = padded(dpre_ref[row, f]).astype(BF)

    span = group * LANES
    for i in range(3):
        acc = jnp.zeros((chans, cols), F32)
        for f in range(frames):
            left = at_ref[0, f, :, i * LANES : i * LANES + span]
            acc = acc + jnp.dot(left, dp_ref[f], preferred_element_type=F32)
        value = acc.astype(BF)
        for b in range(blocks):
            out_ref[(3 * i + step) * blocks + b] = value[b * rows : (b + 1) * rows]

    @pl.when(step == 2)
    def _():
        for copy in copies:
            copy.wait()
        for n in range(part_ref.shape[1]):
            value = part_ref[0, n].astype(F32)
            for k in range(1, 4):
                value = value + part_ref[k, n].astype(F32)
            value = value.astype(BF)
            out_ref[9 * blocks + n] = jnp.concatenate([value[:, :cols], value[:, cols:]], axis=0)


def conv_terms(at, dpre, parts, owners, rows):
    group, frames, width, cols = dpre.shape
    return pl.pallas_call(
        conv_terms_kernel,
        grid=(3,),
        in_specs=[
            pl.BlockSpec((1,) + at.shape[1:], lambda j: (j, 0, 0, 0)),
            pl.BlockSpec(dpre.shape, lambda j: (0, 0, 0, 0)),
        ]
        + [pl.BlockSpec(memory_space=pl.ANY)] * 4,
        out_specs=pl.BlockSpec((owners, rows, cols), lambda j: (0, 0, 0)),
        out_shape=jax.ShapeDtypeStruct((owners, rows, cols), BF),
        scratch_shapes=[
            pltpu.VMEM((frames, group * LANES, cols), BF),
            pltpu.VMEM((4,) + parts[0].shape, BF),
            pltpu.SemaphoreType.DMA((4,)),
        ],
        compiler_params=pltpu.CompilerParams(vmem_limit_bytes=60 << 20),
        cost_estimate=cost(2e9, 10 << 20),
    )(at, dpre, *parts)


def sum_kernel(norm, dims, which_ref, terms_ref, out_ref):
    times, ys, xs = dims
    rows, cols = terms_ref.shape[1:]

    @pl.when(which_ref[0] == 1)
    def _():
        for x in range(xs):
            for c in range(2):
                acc = jnp.zeros((rows, cols), F32)
                for t in range(times):
                    for y in range(ys):
                        acc = acc + terms_ref[((t * ys + y) * xs + x) * 2 + c].astype(F32)
                out_ref[c * rows : (c + 1) * rows, x * cols : (x + 1) * cols] = acc * norm

    @pl.when(which_ref[0] == 0)
    def _():
        part = rows // 2
        for y in range(ys):
            for c in range(2):
                acc = jnp.zeros((rows, cols), F32)
                for t in range(times):
                    for x in range(xs):
                        acc = acc + terms_ref[((t * ys + y) * xs + x) * 2 + c].astype(F32)
                acc = acc * norm
                for h in range(2):
                    at = (2 * c + h) * cols
                    out_ref[y * part : (y + 1) * part, at : at + cols] = acc[h * part : (h + 1) * part]


def sum_terms(which, terms, norm, dims):
    owners, rows, cols = terms.shape
    return pl.pallas_call(
        functools.partial(sum_kernel, norm, dims),
        out_shape=jax.ShapeDtypeStruct((2 * rows, 4 * cols), F32),
        in_specs=[pl.BlockSpec(memory_space=pltpu.SMEM), pl.BlockSpec(memory_space=pltpu.VMEM)],
        compiler_params=CALL(),
        cost_estimate=cost(1e7, 1 << 20),
    )(which, terms)


def dpre_kernel(own_ref, next_ref, slope_ref, tw_ref, dpre_ref, near_ref):
    frames, width, chans = own_ref.shape
    group, _, _, cols = near_ref.shape
    ext = [own_ref[f] for f in range(frames)] + [next_ref[f] for f in range(frames)]
    for f in range(frames):
        acc = jnp.zeros((width, chans), F32)
        for k in range(3):
            acc = acc + dot_nt(ext[f + 2 - k], tw_ref[k * chans : (k + 1) * chans, :])
        value = (acc * slope_ref[f]).astype(BF)
        dpre_ref[f] = value
        for e in range(group):
            near_ref[e, f] = value[:, (e // 2) * cols : (e // 2 + 1) * cols]


def make_dpre(own, nxt, slope, tw):
    frames, width, chans = own.shape
    return pl.pallas_call(
        dpre_kernel,
        out_shape=(
            jax.ShapeDtypeStruct((frames, width, chans), BF),
            jax.ShapeDtypeStruct((GROUP, frames, width, 2 * chans // GROUP), BF),
        ),
        compiler_params=CALL(),
        cost_estimate=cost(5e8, 3 << 20),
    )(own, nxt, slope, tw)


def dact_kernel(mid_ref, above_ref, below_ref, dres_ref, x_ref, sw_ref, out_ref):
    frames, width, chans = mid_ref.shape
    line = lax.broadcasted_iota(jnp.int32, (width, chans), 0)
    for f in range(frames):
        acc = jnp.zeros((width, chans), F32)
        for i, src in enumerate((below_ref, mid_ref, above_ref)):
            plane = src[f]
            wide = plane.astype(F32)
            right = jnp.where(line == width - 1, 0.0, pltpu.roll(wide, width - 1, 0)).astype(BF)
            left = jnp.where(line == 0, 0.0, pltpu.roll(wide, 1, 0)).astype(BF)
            for j, value in enumerate((right, plane, left)):
                tap = 3 * i + j
                acc = acc + dot_nt(value, sw_ref[tap * chans : (tap + 1) * chans, :])
        x = x_ref[f].astype(F32)
        sigma = 1.0 / (1.0 + jnp.exp(-x))
        slope = sigma * (1.0 + x * (1.0 - sigma))
        out_ref[f] = (dres_ref[f] + acc * slope).astype(BF)


def make_grad_latents(mid, above, below, dres, x, sw):
    return pl.pallas_call(
        dact_kernel,
        out_shape=jax.ShapeDtypeStruct(mid.shape, BF),
        compiler_params=CALL(),
        cost_estimate=cost(2e9, 8 << 20),
    )(mid, above, below, dres, x, sw)


def silu_slope(value):
    sigma = jax.nn.sigmoid(value)
    return sigma * (1.0 + value * (1.0 - sigma))


def matmul(left, right):
    return jnp.dot(left, right, preferred_element_type=F32)


def shift(x, axis, by):
    count = lax.axis_size(axis)
    pairs = [(i, i + by) for i in range(count) if 0 <= i + by < count]
    return lax.ppermute(x, axis, pairs)


def swap(x):
    count = lax.axis_size("space")
    return lax.ppermute(x, "space", [(i, i ^ 1) for i in range(count)])


def neighbours(field):
    return shift(field, "space", 1), shift(field, "space", -1)


def exchange(x):
    count = lax.axis_size("space")
    groups = [list(range(at, at + GROUP)) for at in range(0, count, GROUP)]
    return lax.all_to_all(x, "space", 0, 0, axis_index_groups=groups, tiled=True)


def along_y(x, by):
    count = lax.axis_size("space")
    return lax.ppermute(x, "space", [(i, (i + by * GROUP) % count) for i in range(count)])


def pick_one(x, index):
    return lax.dynamic_index_in_dim(x, index, 0, keepdims=False)


def side_pad(field):
    return jnp.pad(field, ((0, 0), (0, 0), (1, 1), (0, 0)))


def taps_of(padded, width):
    pieces = [padded[:, i, j : j + width] for i in range(3) for j in range(3)]
    return jnp.concatenate(pieces, axis=-1).reshape(-1, 9 * padded.shape[-1])


def per_device(latents, spatial_weight, temporal_weight, qkv_weight, out_weight, cotangent):
    frames, rows, width, chans = latents.shape
    ntok = frames * width
    n_space = lax.axis_size("space")
    n_time = lax.axis_size("tm")
    owners = n_space * n_time
    depth = chans // HEADS
    norm = 1.0 / math.sqrt(ntok * n_space * n_time)
    here = lax.axis_index("space")
    core, line = here % 2, here // GROUP
    half = chans // 2
    share = 16 * chans // (2 * owners)

    x = latents.reshape(frames, width, chans)
    cot = cotangent.reshape(frames, width, chans)
    act = jax.nn.silu(x.astype(F32)).astype(BF)
    above, below = neighbours(act)
    pre = matmul(taps_of(side_pad(jnp.stack([above, act, below], axis=1)), width), fetch(spatial_weight))
    pre = pre.reshape(frames, width, chans)
    bact = jax.nn.silu(pre).astype(BF)
    bext = jnp.concatenate([shift(bact, "tm", 1), bact], axis=0)
    resid, rres, items = proj(x, bext, cot, temporal_weight, qkv_weight, out_weight)
    items = items.reshape(frames * HEADS, width, 4 * depth)
    items = lax.all_to_all(items, "space", 0, 0, tiled=True)

    early = pick(act, jnp.where(here % GROUP == 0, above, below), share)
    chalf = cot.reshape(frames, width, 2, half).transpose(2, 0, 1, 3)
    cpair = (pick_one(chalf, core), swap(pick_one(chalf, 1 - core)))
    rother, bother = swap(rres), swap(bext)
    early, cpair, rother, bother, items = lax.optimization_barrier((early, cpair, rother, bother, items))
    early = exchange(early)
    outs = attn(items.reshape(n_space * width, 4 * depth)).reshape(n_space, width, 4 * depth)
    outs, early, rother, bother = lax.optimization_barrier((outs, early, rother, bother))
    outs = lax.all_to_all(outs, "space", 0, 0, tiled=True)
    aturn = turn(early, frames)
    rturn, bturn = turn_pair(rres, rother, bext, bother)
    slope = silu_slope(pre)
    outs, aturn, rturn, bturn, slope = lax.optimization_barrier((outs, aturn, rturn, bturn, slope))

    core_at = core.astype(jnp.int32).reshape(1)
    outs = outs.reshape(frames, HEADS, width, 4 * depth)
    atted, dres, dresb, mine, other = post(core_at, outs, cot, qkv_weight)
    dnext = shift(dresb, "tm", -1)
    local = local_terms(rturn, bturn, (atted, swap(atted)), (mine, swap(other)), cpair)
    dpre, near = make_dpre(dresb, dnext, slope, temporal_weight)
    near = exchange(near)
    dabove, dbelow = neighbours(dpre)
    parts = [pick_one(local, line)]
    for by in range(1, 4):
        parts.append(along_y(pick_one(local, (line + by) % 4), by))
    mixed = resid.reshape(ntok, chans) + matmul(atted.reshape(ntok, chans), out_weight)
    mixed = mixed.astype(BF).reshape(latents.shape)
    mixed, dabove, dbelow, near = lax.optimization_barrier((mixed, dabove, dbelow, near))
    terms = conv_terms(aturn, near, parts, owners, share)
    terms, dpre = lax.optimization_barrier((terms, dpre))
    terms = lax.all_to_all(terms, ("tm", "space"), 0, 0, tiled=True)
    grad_latents = make_grad_latents(dpre, dabove, dbelow, dres, x, spatial_weight).reshape(latents.shape)
    index = lax.axis_index("tm") * n_space + here
    which = (index < 9 * chans // (2 * share)).astype(jnp.int32).reshape(1)
    grad_weights = sum_terms(which, terms, norm, (n_time, n_space // GROUP, GROUP // 2))
    return (mixed, grad_latents, grad_weights)


def solution(mesh):
    placed = (P("tm", "space", None, None), P(), P(), P(), P(), P("tm", "space", None, None))
    return jax.shard_map(
        per_device,
        mesh=mesh,
        in_specs=placed,
        out_specs=(
            P("tm", "space", None, None),
            P("tm", "space", None, None),
            P(("tm", "space"), None),
        ),
        check_vma=False,
    )
```

```python
import functools
import math

import jax
import jax.numpy as jnp
from jax import lax
from jax.experimental import pallas as pl
from jax.experimental.pallas import tpu as pltpu
from jax.sharding import PartitionSpec as P

HEADS = 16
GROUP = 8
F32 = jnp.float32
BF = jnp.bfloat16
NT = (((1,), (1,)), ((), ()))

def dot_nt(left, right):
    return lax.dot_general(left, right, NT, preferred_element_type=F32)


def proj_kernel(x_ref, bext_ref, cot_ref, tw_ref, qw_ref, ow_ref, resid_ref, rres_ref, items_ref):
    frames, width, chans = x_ref.shape
    d = chans // HEADS
    for f in range(frames):
        acc = x_ref[f].astype(F32)
        for k in range(3):
            tap = tw_ref[k * chans : (k + 1) * chans, :]
            acc = acc + jnp.dot(bext_ref[f + k], tap, preferred_element_type=F32)
        resid_ref[f] = acc
        rounded = acc.astype(BF)
        rres_ref[f] = rounded
        qkv = jnp.dot(rounded, qw_ref[...], preferred_element_type=F32)
        dattn = dot_nt(cot_ref[f], ow_ref[...])
        for h in range(HEADS):
            parts = [qkv[:, p * chans + h * d : p * chans + (h + 1) * d] for p in range(3)]
            parts.append(dattn[:, h * d : (h + 1) * d])
            items_ref[f, h] = jnp.concatenate(parts, axis=1).astype(BF)


def proj(x, bext, cot, tw, qw, ow):
    frames, width, chans = x.shape
    return pl.pallas_call(
        proj_kernel,
        out_shape=(
            jax.ShapeDtypeStruct((frames, width, chans), F32),
            jax.ShapeDtypeStruct((frames, width, chans), BF),
            jax.ShapeDtypeStruct((frames, HEADS, width, 4 * chans // HEADS), BF),
        ),
        compiler_params=pltpu.CompilerParams(vmem_limit_bytes=32 << 20),
        cost_estimate=pl.CostEstimate(flops=10**9 * 2, bytes_accessed=6 << 20, transcendentals=0),
    )(x, bext, cot, tw, qw, ow)


def post_kernel(core_ref, z_ref, cot_ref, qw_ref, attn_ref, dres_ref, dresb_ref, mine_ref, other_ref):
    frames, width, chans = cot_ref.shape
    d = chans // HEADS
    half = chans // 2
    all_parts = []
    for f in range(frames):
        heads = [z_ref[f, h].astype(F32) for h in range(HEADS)]
        dres = cot_ref[f].astype(F32)
        parts = [jnp.concatenate([z[:, p * d : (p + 1) * d] for z in heads], axis=1).astype(BF) for p in range(4)]
        attn_ref[f] = parts[0]
        for p in range(3):
            dres = dres + dot_nt(parts[p + 1], qw_ref[:, p * chans : (p + 1) * chans])
        dres_ref[f] = dres
        dresb = dres.astype(BF)
        dresb_ref[f] = dresb
        all_parts.append(parts[1:] + [dresb])

    def store(first, second):
        for f in range(frames):
            for at, part in enumerate(all_parts[f]):
                for out, c in ((first, 0), (second, 1)):
                    out[f, :, at * half : (at + 1) * half] = part[:, c * half : (c + 1) * half]

    @pl.when(core_ref[0] == 0)
    def _():
        store(mine_ref, other_ref)

    @pl.when(core_ref[0] == 1)
    def _():
        store(other_ref, mine_ref)


def post(core, z, cot, qw):
    frames, width, chans = cot.shape
    return pl.pallas_call(
        post_kernel,
        out_shape=(
            jax.ShapeDtypeStruct((frames, width, chans), BF),
            jax.ShapeDtypeStruct((frames, width, chans), F32),
            jax.ShapeDtypeStruct((frames, width, chans), BF),
            jax.ShapeDtypeStruct((frames, width, 2 * chans), BF),
            jax.ShapeDtypeStruct((frames, width, 2 * chans), BF),
        ),
        in_specs=[pl.BlockSpec(memory_space=pltpu.SMEM)] + [pl.BlockSpec(memory_space=pltpu.VMEM)] * 3,
        compiler_params=pltpu.CompilerParams(vmem_limit_bytes=32 << 20),
        cost_estimate=pl.CostEstimate(flops=10**9, bytes_accessed=6 << 20, transcendentals=0),
    )(core, z, cot, qw)


def fetch_kernel(w_ref, out_ref):
    out_ref[...] = w_ref[...]


def fetch(w):
    return pl.pallas_call(
        fetch_kernel,
        out_shape=jax.ShapeDtypeStruct(w.shape, w.dtype),
        compiler_params=pltpu.CompilerParams(vmem_limit_bytes=24 << 20),
        cost_estimate=pl.CostEstimate(flops=10**6, bytes_accessed=10 << 20, transcendentals=0),
    )(w)


def attn_kernel(scale, tq, ck, un, x_ref, o_ref, a_ref, kt_ref, vt_ref, s_ref, e_ref, acc_ref):
    tok = x_ref.shape[0]
    step = pl.program_id(0)
    nck = tok // ck
    d = 32
    @pl.when(step == 0)
    def _():
        k = x_ref[:, d:2*d]
        v = x_ref[:, 2*d:3*d]
        lane = lax.broadcasted_iota(jnp.int32, (tok, d), 1)
        ones = jnp.where(lane < 3, 1.0, 0.0).astype(BF)
        a_ref[...] = jnp.concatenate([k, k, v, ones], axis=1)
        kt_ref[...] = k.astype(F32).T.astype(BF)
        vt_ref[...] = jnp.concatenate([v, ones], axis=1).astype(F32).T[: d + 16].astype(BF)
        acc_ref[...] = jnp.zeros_like(acc_ref)
    rows = pl.ds(pl.multiple_of(step * tq, tq), tq)
    xb = x_ref[rows, :]
    q = xb[:, 0:d].astype(F32)
    do = xb[:, 3*d:4*d].astype(F32)
    zeros = jnp.zeros((tq, 2*d), BF)
    def split(z):
        hi = z.astype(BF)
        lo = (z - hi.astype(F32)).astype(BF)
        return hi, lo
    qh, ql = split(q * (scale * math.log2(math.e)))
    wq = jnp.concatenate([qh, ql, zeros], axis=1)
    def p1(i, m):
        r = pl.ds(pl.multiple_of(i * ck, ck), ck)
        s = lax.dot_general(a_ref[r, :], wq, NT, preferred_element_type=F32)
        s_ref[r, :] = s
        return jnp.maximum(m, jnp.max(s.reshape(ck // 8, 8, tq), axis=0))
    m = lax.fori_loop(0, nck, p1, jnp.full((8, tq), -jnp.inf, F32), unroll=un)
    m = jnp.max(m, axis=0, keepdims=True)
    def p2(i, o):
        r = pl.ds(pl.multiple_of(i * ck, ck), ck)
        e = jnp.exp2(s_ref[r, :] - m)
        s_ref[r, :] = e
        eb = e.astype(BF)
        e_ref[r, :] = eb
        return o + jnp.dot(vt_ref[:, r], eb, preferred_element_type=F32)
    o = lax.fori_loop(0, nck, p2, jnp.zeros((d + 16, tq), F32), unroll=un)
    inv = 1.0 / o[d:d+1, :]
    ot = o[:d] * inv
    ob = ot.T
    delta = jnp.sum(ob * do, axis=1, keepdims=True)
    invc = jnp.broadcast_to(inv, (8, tq)).T[:, 0:1]
    dh = (-delta).astype(BF); dr = -delta - dh.astype(F32)
    dm = dr.astype(BF); dl = (dr - dm.astype(F32)).astype(BF)
    lane = lax.broadcasted_iota(jnp.int32, (tq, d), 1)
    dd = jnp.where(lane == 0, dh.astype(F32), jnp.where(lane == 1, dm.astype(F32), jnp.where(lane == 2, dl.astype(F32), 0.0))).astype(BF)
    wd = jnp.concatenate([zeros, xb[:, 3*d:], dd], axis=1)
    gh, gl = split(do * invc)
    rh, rl = split(q * (invc * scale))
    we = jnp.concatenate([zeros, gh, gl], axis=1)
    ws = jnp.concatenate([rh, rl, zeros], axis=1)
    def p3(i, dq):
        r = pl.ds(pl.multiple_of(i * ck, ck), ck)
        dp = lax.dot_general(a_ref[r, :], wd, NT, preferred_element_type=F32)
        ds = (s_ref[r, :] * dp).astype(BF)
        acc_ref[r, :] += (jnp.dot(ds, ws, preferred_element_type=F32)
                          + jnp.dot(e_ref[r, :], we, preferred_element_type=F32))
        return dq + jnp.dot(kt_ref[:, r], ds, preferred_element_type=F32)
    dq = lax.fori_loop(0, nck, p3, jnp.zeros((d, tq), F32), unroll=un)
    dq = dq * (inv * scale)
    o_ref[rows, 0:2*d] = jnp.concatenate([ot, dq], axis=0).T.astype(BF)
    @pl.when(step == pl.num_programs(0) - 1)
    def _():
        acc = acc_ref[...]
        dk = acc[:, :d] + acc[:, d:2*d]
        dv = acc[:, 2*d:3*d] + acc[:, 3*d:]
        o_ref[:, 2*d:] = jnp.concatenate([dk, dv], axis=1).astype(BF)

def attn(x, tq=768, ck=3840, un=1):
    tok = x.shape[0]
    return pl.pallas_call(
        functools.partial(attn_kernel, 1.0/math.sqrt(32), tq, ck, un),
        grid=(tok // tq,),
        in_specs=[pl.BlockSpec((tok, 128), lambda i: (0, 0))],
        out_specs=pl.BlockSpec((tok, 128), lambda i: (0, 0)),
        out_shape=jax.ShapeDtypeStruct((tok, 128), BF),
        scratch_shapes=[pltpu.VMEM((tok, 128), BF), pltpu.VMEM((32, tok), BF), pltpu.VMEM((48, tok), BF),
                        pltpu.VMEM((tok, tq), F32), pltpu.VMEM((tok, tq), BF), pltpu.VMEM((tok, 128), F32)],
        compiler_params=pltpu.CompilerParams(vmem_limit_bytes=48 << 20),
        cost_estimate=pl.CostEstimate(flops=6*2*tok*tok*128, bytes_accessed=4*tok*128, transcendentals=tok*tok),
    )(x)


LANES = 128
CALL = functools.partial(pltpu.CompilerParams, vmem_limit_bytes=40 << 20)


def cost(flops, moved):
    return pl.CostEstimate(flops=int(flops), bytes_accessed=int(moved), transcendentals=0)


def padded(plane):
    width, chans = plane.shape
    return jnp.concatenate([plane.astype(F32), jnp.zeros((LANES - width, chans), F32)], axis=0)


def pick_kernel(rows, act_ref, outer_ref, out_ref):
    group = out_ref.shape[0]
    frames, width, chans = act_ref.shape
    for f in range(frames):
        for at, src in ((f, act_ref), (frames + f, outer_ref)):
            plane = src[f].astype(F32)
            for c in range(2):
                parts = [plane[:, b + c * rows : b + (c + 1) * rows] for b in range(0, chans, 2 * rows)]
                part = jnp.concatenate(parts, axis=1).astype(BF)
                for x in range(group // 2):
                    out_ref[2 * x + c, at] = part


def pick(act, outer, rows):
    frames, width, chans = act.shape
    return pl.pallas_call(
        functools.partial(pick_kernel, rows),
        out_shape=jax.ShapeDtypeStruct((GROUP, 2 * frames, width, chans // 2), BF),
        compiler_params=CALL(),
        cost_estimate=cost(1e8, 3 << 20),
    )(act, outer)


def turn_kernel(r_ref, at_ref):
    group = r_ref.shape[0]
    frames = at_ref.shape[1]
    for f in range(frames):
        for row in range(group + 2):
            if row == 0:
                plane = r_ref[0, frames + f]
            elif row == group + 1:
                plane = r_ref[group - 1, frames + f]
            else:
                plane = r_ref[row - 1, f]
            tile = padded(plane).T
            cols = slice(row * LANES, (row + 1) * LANES)
            at_ref[0, f, :, cols] = pltpu.roll(tile, 1, 1).astype(BF)
            at_ref[1, f, :, cols] = tile.astype(BF)
            at_ref[2, f, :, cols] = pltpu.roll(tile, LANES - 1, 1).astype(BF)


def turn(r, frames):
    group, _, _, chans = r.shape
    return pl.pallas_call(
        turn_kernel,
        out_shape=jax.ShapeDtypeStruct((3, frames, chans, (group + 2) * LANES), BF),
        compiler_params=CALL(),
        cost_estimate=cost(1e9, 6 << 20),
    )(r)


def turn_pair_kernel(*refs):
    ins, outs = refs[:4], refs[4:]
    for own, other, out in ((ins[0], ins[1], outs[0]), (ins[2], ins[3], outs[1])):
        count = own.shape[0]
        for d, src in enumerate((own, other)):
            for f in range(count):
                at = (d * count + f) * LANES
                out[:, at : at + LANES] = padded(src[f]).T.astype(BF)


def turn_pair(own_r, other_r, own_b, other_b):
    chans = own_r.shape[-1]
    return pl.pallas_call(
        turn_pair_kernel,
        out_shape=tuple(
            jax.ShapeDtypeStruct((chans, 2 * x.shape[0] * LANES), BF) for x in (own_r, own_b)
        ),
        compiler_params=CALL(),
        cost_estimate=cost(1e9, 4 << 20),
    )(own_r, other_r, own_b, other_b)


def local_terms_kernel(
    line_ref, rt_ref, bt_ref, a0_ref, a1_ref, p0_ref, p1_ref, c0_ref, c1_ref, *refs
):
    outs, (at_ref, pay_ref, cot_ref, mix_ref, out_ref) = refs[:4], refs[4:]
    frames, width, chans = a0_ref.shape
    half = chans // 2
    for d, (a, p, c) in enumerate(((a0_ref, p0_ref, c0_ref), (a1_ref, p1_ref, c1_ref))):
        for f in range(frames):
            at = (d * frames + f) * LANES
            at_ref[:, at : at + LANES] = padded(a[f]).T.astype(BF)
            pay_ref[at : at + LANES, :] = padded(p[f]).astype(BF)
            cot_ref[at : at + LANES, :] = padded(c[f]).astype(BF)
    parts, _, rows, _ = out_ref.shape
    block = parts * rows

    def put(first, value, lane=0):
        for n in range(value.shape[0] // block):
            for y in range(parts):
                at = n * block + y * rows
                out_ref[y, first + n, :, lane : lane + value.shape[1]] = value[at : at + rows].astype(BF)

    for k in range(3):
        acc = jnp.zeros((chans, half), F32)
        for d in range(2):
            left = bt_ref[:, (2 * d * frames + k) * LANES : (2 * d * frames + k + frames) * LANES]
            right = pay_ref[d * frames * LANES : (d + 1) * frames * LANES, 3 * half :]
            acc = acc + jnp.dot(left, right, preferred_element_type=F32)
        put(k * chans // block, acc)
    for p in range(3):
        right = pay_ref[:, p * half : (p + 1) * half]
        for lane in range(0, half, LANES):
            value = jnp.dot(rt_ref[...], right[:, lane : lane + LANES], preferred_element_type=F32)
            mix_ref[lane // LANES, pl.ds(p, chans, stride=3), :] = value
    for lane in range(0, half, LANES):
        put(3 * chans // block, mix_ref[lane // LANES], lane)
    put(6 * chans // block, jnp.dot(at_ref[...], cot_ref[...], preferred_element_type=F32))
    for k, out in enumerate(outs):
        out[...] = out_ref[lax.rem(line_ref[0] + k, parts)]


def local_terms(line, rt, bt, atted, pay, cot):
    frames, width, chans = atted[0].shape
    half = chans // 2
    span = 2 * frames * LANES
    piece = (7 * chans // 64, 16, half)
    return pl.pallas_call(
        local_terms_kernel,
        out_shape=(jax.ShapeDtypeStruct(piece, BF),) * 4,
        in_specs=[pl.BlockSpec(memory_space=pltpu.SMEM)] + [pl.BlockSpec(memory_space=pltpu.VMEM)] * 8,
        scratch_shapes=[
            pltpu.VMEM((chans, span), BF),
            pltpu.VMEM((span, 4 * half), BF),
            pltpu.VMEM((span, half), BF),
            pltpu.VMEM((half // LANES, 3 * chans, LANES), F32),
            pltpu.VMEM((4,) + piece, BF),
        ],
        compiler_params=pltpu.CompilerParams(vmem_limit_bytes=60 << 20),
        cost_estimate=cost(2e9, 10 << 20),
    )(line, rt, bt, *atted, *pay, *cot)


def conv_terms_kernel(at_ref, dpre_ref, out_ref, dp_ref):
    step = pl.program_id(0)
    group, frames, width, cols = dpre_ref.shape
    chans = at_ref.shape[2]
    rows = out_ref.shape[1]
    blocks = chans // rows

    @pl.when(step == 0)
    def _():
        for f in range(frames):
            for row in range(group):
                dp_ref[f, row * LANES : (row + 1) * LANES, :] = padded(dpre_ref[row, f]).astype(BF)

    span = group * LANES
    for i in range(3):
        acc = jnp.zeros((chans, cols), F32)
        for f in range(frames):
            left = at_ref[0, f, :, i * LANES : i * LANES + span]
            acc = acc + jnp.dot(left, dp_ref[f], preferred_element_type=F32)
        value = acc.astype(BF)
        for b in range(blocks):
            out_ref[(3 * i + step) * blocks + b] = value[b * rows : (b + 1) * rows]


def conv_terms(at, dpre, owners, rows):
    group, frames, width, cols = dpre.shape
    return pl.pallas_call(
        conv_terms_kernel,
        grid=(3,),
        in_specs=[
            pl.BlockSpec((1,) + at.shape[1:], lambda j: (j, 0, 0, 0)),
            pl.BlockSpec(dpre.shape, lambda j: (0, 0, 0, 0)),
        ],
        out_specs=pl.BlockSpec((owners, rows, cols), lambda j: (0, 0, 0)),
        out_shape=jax.ShapeDtypeStruct((owners, rows, cols), BF),
        scratch_shapes=[pltpu.VMEM((frames, group * LANES, cols), BF)],
        compiler_params=pltpu.CompilerParams(vmem_limit_bytes=60 << 20),
        cost_estimate=cost(2e9, 10 << 20),
    )(at, dpre)


def add_parts_kernel(terms_ref, s0_ref, s1_ref, s2_ref, s3_ref, out_ref, sum_ref, sem):
    count, rows, cols = sum_ref.shape
    for n in range(count):
        value = s0_ref[n].astype(F32) + s1_ref[n].astype(F32) + s2_ref[n].astype(F32) + s3_ref[n].astype(F32)
        value = value.astype(BF)
        sum_ref[n] = jnp.concatenate([value[:, :cols], value[:, cols:]], axis=0)
    copy = pltpu.make_async_copy(sum_ref, out_ref.at[pl.ds(out_ref.shape[0] - count, count)], sem)
    copy.start()
    copy.wait()


def add_parts(terms, parts):
    count = parts[0].shape[0]
    return pl.pallas_call(
        add_parts_kernel,
        in_specs=[pl.BlockSpec(memory_space=pl.ANY)] + [pl.BlockSpec(memory_space=pltpu.VMEM)] * 4,
        out_specs=pl.BlockSpec(memory_space=pl.ANY),
        out_shape=jax.ShapeDtypeStruct(terms.shape, BF),
        input_output_aliases={0: 0},
        scratch_shapes=[pltpu.VMEM((count,) + terms.shape[1:], BF), pltpu.SemaphoreType.DMA],
        compiler_params=pltpu.CompilerParams(vmem_limit_bytes=60 << 20),
        cost_estimate=cost(1e7, 3 << 20),
    )(terms, *parts)


def sum_kernel(norm, dims, which_ref, terms_ref, out_ref):
    times, ys, xs = dims
    rows, cols = terms_ref.shape[1:]

    @pl.when(which_ref[0] == 1)
    def _():
        for x in range(xs):
            for c in range(2):
                acc = jnp.zeros((rows, cols), F32)
                for t in range(times):
                    for y in range(ys):
                        acc = acc + terms_ref[((t * ys + y) * xs + x) * 2 + c].astype(F32)
                out_ref[c * rows : (c + 1) * rows, x * cols : (x + 1) * cols] = acc * norm

    @pl.when(which_ref[0] == 0)
    def _():
        part = rows // 2
        for y in range(ys):
            for c in range(2):
                acc = jnp.zeros((rows, cols), F32)
                for t in range(times):
                    for x in range(xs):
                        acc = acc + terms_ref[((t * ys + y) * xs + x) * 2 + c].astype(F32)
                acc = acc * norm
                for h in range(2):
                    at = (2 * c + h) * cols
                    out_ref[y * part : (y + 1) * part, at : at + cols] = acc[h * part : (h + 1) * part]


def sum_terms(which, terms, norm, dims):
    owners, rows, cols = terms.shape
    return pl.pallas_call(
        functools.partial(sum_kernel, norm, dims),
        out_shape=jax.ShapeDtypeStruct((2 * rows, 4 * cols), F32),
        in_specs=[pl.BlockSpec(memory_space=pltpu.SMEM), pl.BlockSpec(memory_space=pltpu.VMEM)],
        compiler_params=CALL(),
        cost_estimate=cost(1e7, 1 << 20),
    )(which, terms)


def dpre_kernel(own_ref, next_ref, slope_ref, tw_ref, dpre_ref, near_ref):
    frames, width, chans = own_ref.shape
    group, _, _, cols = near_ref.shape
    ext = [own_ref[f] for f in range(frames)] + [next_ref[f] for f in range(frames)]
    for f in range(frames):
        acc = jnp.zeros((width, chans), F32)
        for k in range(3):
            acc = acc + dot_nt(ext[f + 2 - k], tw_ref[k * chans : (k + 1) * chans, :])
        value = (acc * slope_ref[f]).astype(BF)
        dpre_ref[f] = value
        for e in range(group):
            near_ref[e, f] = value[:, (e // 2) * cols : (e // 2 + 1) * cols]


def make_dpre(own, nxt, slope, tw):
    frames, width, chans = own.shape
    return pl.pallas_call(
        dpre_kernel,
        out_shape=(
            jax.ShapeDtypeStruct((frames, width, chans), BF),
            jax.ShapeDtypeStruct((GROUP, frames, width, 2 * chans // GROUP), BF),
        ),
        compiler_params=CALL(),
        cost_estimate=cost(5e8, 3 << 20),
    )(own, nxt, slope, tw)


def dact_kernel(mid_ref, above_ref, below_ref, dres_ref, x_ref, sw_ref, out_ref):
    frames, width, chans = mid_ref.shape
    line = lax.broadcasted_iota(jnp.int32, (width, chans), 0)
    for f in range(frames):
        acc = jnp.zeros((width, chans), F32)
        for i, src in enumerate((below_ref, mid_ref, above_ref)):
            plane = src[f]
            wide = plane.astype(F32)
            right = jnp.where(line == width - 1, 0.0, pltpu.roll(wide, width - 1, 0)).astype(BF)
            left = jnp.where(line == 0, 0.0, pltpu.roll(wide, 1, 0)).astype(BF)
            for j, value in enumerate((right, plane, left)):
                tap = 3 * i + j
                acc = acc + dot_nt(value, sw_ref[tap * chans : (tap + 1) * chans, :])
        x = x_ref[f].astype(F32)
        sigma = 1.0 / (1.0 + jnp.exp(-x))
        slope = sigma * (1.0 + x * (1.0 - sigma))
        out_ref[f] = (dres_ref[f] + acc * slope).astype(BF)


def make_grad_latents(mid, above, below, dres, x, sw):
    return pl.pallas_call(
        dact_kernel,
        out_shape=jax.ShapeDtypeStruct(mid.shape, BF),
        compiler_params=CALL(),
        cost_estimate=cost(2e9, 8 << 20),
    )(mid, above, below, dres, x, sw)


def silu_slope(value):
    sigma = jax.nn.sigmoid(value)
    return sigma * (1.0 + value * (1.0 - sigma))


def matmul(left, right):
    return jnp.dot(left, right, preferred_element_type=F32)


def shift(x, axis, by):
    count = lax.axis_size(axis)
    pairs = [(i, i + by) for i in range(count) if 0 <= i + by < count]
    return lax.ppermute(x, axis, pairs)


def swap(x):
    count = lax.axis_size("space")
    return lax.ppermute(x, "space", [(i, i ^ 1) for i in range(count)])


def neighbours(field):
    return shift(field, "space", 1), shift(field, "space", -1)


def exchange(x):
    count = lax.axis_size("space")
    groups = [list(range(at, at + GROUP)) for at in range(0, count, GROUP)]
    return lax.all_to_all(x, "space", 0, 0, axis_index_groups=groups, tiled=True)


def along_y(x, by):
    count = lax.axis_size("space")
    return lax.ppermute(x, "space", [(i, (i + by * GROUP) % count) for i in range(count)])


def pick_one(x, index):
    return lax.dynamic_index_in_dim(x, index, 0, keepdims=False)


def side_pad(field):
    return jnp.pad(field, ((0, 0), (0, 0), (1, 1), (0, 0)))


def taps_of(padded, width):
    pieces = [padded[:, i, j : j + width] for i in range(3) for j in range(3)]
    return jnp.concatenate(pieces, axis=-1).reshape(-1, 9 * padded.shape[-1])


def per_device(latents, spatial_weight, temporal_weight, qkv_weight, out_weight, cotangent):
    frames, rows, width, chans = latents.shape
    ntok = frames * width
    n_space = lax.axis_size("space")
    n_time = lax.axis_size("tm")
    owners = n_space * n_time
    depth = chans // HEADS
    norm = 1.0 / math.sqrt(ntok * n_space * n_time)
    here = lax.axis_index("space")
    core, line = here % 2, here // GROUP
    half = chans // 2
    share = 16 * chans // (2 * owners)

    x = latents.reshape(frames, width, chans)
    cot = cotangent.reshape(frames, width, chans)
    act = jax.nn.silu(x.astype(F32)).astype(BF)
    above, below = neighbours(act)
    pre = matmul(taps_of(side_pad(jnp.stack([above, act, below], axis=1)), width), fetch(spatial_weight))
    pre = pre.reshape(frames, width, chans)
    bact = jax.nn.silu(pre).astype(BF)
    bext = jnp.concatenate([shift(bact, "tm", 1), bact], axis=0)
    resid, rres, items = proj(x, bext, cot, temporal_weight, qkv_weight, out_weight)
    items = items.reshape(frames * HEADS, width, 4 * depth)
    items = lax.all_to_all(items, "space", 0, 0, tiled=True)

    early = pick(act, jnp.where(here % GROUP == 0, above, below), share)
    chalf = cot.reshape(frames, width, 2, half).transpose(2, 0, 1, 3)
    cpair = (pick_one(chalf, core), swap(pick_one(chalf, 1 - core)))
    rother, bother = swap(rres), swap(bext)
    early, cpair, rother, bother, items = lax.optimization_barrier((early, cpair, rother, bother, items))
    early = exchange(early)
    outs = attn(items.reshape(n_space * width, 4 * depth)).reshape(n_space, width, 4 * depth)
    outs, early, rother, bother = lax.optimization_barrier((outs, early, rother, bother))
    outs = lax.all_to_all(outs, "space", 0, 0, tiled=True)
    aturn = turn(early, frames)
    rturn, bturn = turn_pair(rres, rother, bext, bother)
    slope = silu_slope(pre)
    outs, aturn, rturn, bturn, slope = lax.optimization_barrier((outs, aturn, rturn, bturn, slope))

    core_at = core.astype(jnp.int32).reshape(1)
    outs = outs.reshape(frames, HEADS, width, 4 * depth)
    atted, dres, dresb, mine, other = post(core_at, outs, cot, qkv_weight)
    dnext = shift(dresb, "tm", -1)
    local = local_terms(line.astype(jnp.int32).reshape(1), rturn, bturn, (atted, swap(atted)), (mine, swap(other)), cpair)
    dpre, near = make_dpre(dresb, dnext, slope, temporal_weight)
    near = exchange(near)
    dabove, dbelow = neighbours(dpre)
    parts = [local[0]] + [along_y(local[by], by) for by in range(1, 4)]
    mixed = resid.reshape(ntok, chans) + matmul(atted.reshape(ntok, chans), out_weight)
    mixed = mixed.astype(BF).reshape(latents.shape)
    mixed, near = lax.optimization_barrier((mixed, near))
    terms = add_parts(conv_terms(aturn, near, owners, share), parts)
    terms, dpre = lax.optimization_barrier((terms, dpre))
    terms = lax.all_to_all(terms, ("tm", "space"), 0, 0, tiled=True)
    grad_latents = make_grad_latents(dpre, dabove, dbelow, dres, x, spatial_weight).reshape(latents.shape)
    index = lax.axis_index("tm") * n_space + here
    which = (index < 9 * chans // (2 * share)).astype(jnp.int32).reshape(1)
    grad_weights = sum_terms(which, terms, norm, (n_time, n_space // GROUP, GROUP // 2))
    return (mixed, grad_latents, grad_weights)


def solution(mesh):
    placed = (P("tm", "space", None, None), P(), P(), P(), P(), P("tm", "space", None, None))
    return jax.shard_map(
        per_device,
        mesh=mesh,
        in_specs=placed,
        out_specs=(
            P("tm", "space", None, None),
            P("tm", "space", None, None),
            P(("tm", "space"), None),
        ),
        check_vma=False,
    )
```

```python
import functools
import math

import jax
import jax.numpy as jnp
from jax import lax
from jax.experimental import pallas as pl
from jax.experimental.pallas import tpu as pltpu
from jax.sharding import PartitionSpec as P

HEADS = 16
GROUP = 8
F32 = jnp.float32
BF = jnp.bfloat16
NT = (((1,), (1,)), ((), ()))

def dot_nt(left, right):
    return lax.dot_general(left, right, NT, preferred_element_type=F32)


def proj_kernel(x_ref, bext_ref, cot_ref, tw_ref, qw_ref, ow_ref, resid_ref, rres_ref, items_ref):
    frames, width, chans = x_ref.shape
    d = chans // HEADS
    for f in range(frames):
        acc = x_ref[f].astype(F32)
        for k in range(3):
            tap = tw_ref[k * chans : (k + 1) * chans, :]
            acc = acc + jnp.dot(bext_ref[f + k], tap, preferred_element_type=F32)
        resid_ref[f] = acc
        rounded = acc.astype(BF)
        rres_ref[f] = rounded
        qkv = jnp.dot(rounded, qw_ref[...], preferred_element_type=F32)
        dattn = dot_nt(cot_ref[f], ow_ref[...])
        for h in range(HEADS):
            parts = [qkv[:, p * chans + h * d : p * chans + (h + 1) * d] for p in range(3)]
            parts.append(dattn[:, h * d : (h + 1) * d])
            items_ref[f, h] = jnp.concatenate(parts, axis=1).astype(BF)


def proj(x, bext, cot, tw, qw, ow):
    frames, width, chans = x.shape
    return pl.pallas_call(
        proj_kernel,
        out_shape=(
            jax.ShapeDtypeStruct((frames, width, chans), F32),
            jax.ShapeDtypeStruct((frames, width, chans), BF),
            jax.ShapeDtypeStruct((frames, HEADS, width, 4 * chans // HEADS), BF),
        ),
        compiler_params=pltpu.CompilerParams(vmem_limit_bytes=32 << 20),
        cost_estimate=pl.CostEstimate(flops=10**9 * 2, bytes_accessed=6 << 20, transcendentals=0),
    )(x, bext, cot, tw, qw, ow)


def post_kernel(core_ref, z_ref, cot_ref, qw_ref, attn_ref, dres_ref, dresb_ref, mine_ref, other_ref):
    frames, width, chans = cot_ref.shape
    d = chans // HEADS
    half = chans // 2
    all_parts = []
    for f in range(frames):
        heads = [z_ref[f, h].astype(F32) for h in range(HEADS)]
        dres = cot_ref[f].astype(F32)
        parts = [jnp.concatenate([z[:, p * d : (p + 1) * d] for z in heads], axis=1).astype(BF) for p in range(4)]
        attn_ref[f] = parts[0]
        for p in range(3):
            dres = dres + dot_nt(parts[p + 1], qw_ref[:, p * chans : (p + 1) * chans])
        dres_ref[f] = dres
        dresb = dres.astype(BF)
        dresb_ref[f] = dresb
        all_parts.append(parts[1:] + [dresb])

    def store(first, second):
        for f in range(frames):
            for at, part in enumerate(all_parts[f]):
                for out, c in ((first, 0), (second, 1)):
                    out[f, :, at * half : (at + 1) * half] = part[:, c * half : (c + 1) * half]

    @pl.when(core_ref[0] == 0)
    def _():
        store(mine_ref, other_ref)

    @pl.when(core_ref[0] == 1)
    def _():
        store(other_ref, mine_ref)


def post(core, z, cot, qw):
    frames, width, chans = cot.shape
    return pl.pallas_call(
        post_kernel,
        out_shape=(
            jax.ShapeDtypeStruct((frames, width, chans), BF),
            jax.ShapeDtypeStruct((frames, width, chans), F32),
            jax.ShapeDtypeStruct((frames, width, chans), BF),
            jax.ShapeDtypeStruct((frames, width, 2 * chans), BF),
            jax.ShapeDtypeStruct((frames, width, 2 * chans), BF),
        ),
        in_specs=[pl.BlockSpec(memory_space=pltpu.SMEM)] + [pl.BlockSpec(memory_space=pltpu.VMEM)] * 3,
        compiler_params=pltpu.CompilerParams(vmem_limit_bytes=32 << 20),
        cost_estimate=pl.CostEstimate(flops=10**9, bytes_accessed=6 << 20, transcendentals=0),
    )(core, z, cot, qw)


def fetch_kernel(w_ref, out_ref):
    out_ref[...] = w_ref[...]


def fetch(w):
    return pl.pallas_call(
        fetch_kernel,
        out_shape=jax.ShapeDtypeStruct(w.shape, w.dtype),
        compiler_params=pltpu.CompilerParams(vmem_limit_bytes=24 << 20),
        cost_estimate=pl.CostEstimate(flops=10**6, bytes_accessed=10 << 20, transcendentals=0),
    )(w)


def attn_kernel(scale, tq, ck, un, x_ref, o_ref, a_ref, kt_ref, vt_ref, s_ref, e_ref, acc_ref):
    tok = x_ref.shape[0]
    step = pl.program_id(0)
    nck = tok // ck
    d = 32
    @pl.when(step == 0)
    def _():
        k = x_ref[:, d:2*d]
        v = x_ref[:, 2*d:3*d]
        lane = lax.broadcasted_iota(jnp.int32, (tok, d), 1)
        ones = jnp.where(lane < 3, 1.0, 0.0).astype(BF)
        a_ref[...] = jnp.concatenate([k, k, v, ones], axis=1)
        kt_ref[...] = k.astype(F32).T.astype(BF)
        vt_ref[...] = jnp.concatenate([v, ones], axis=1).astype(F32).T[: d + 16].astype(BF)
        acc_ref[...] = jnp.zeros_like(acc_ref)
    rows = pl.ds(pl.multiple_of(step * tq, tq), tq)
    xb = x_ref[rows, :]
    q = xb[:, 0:d].astype(F32)
    do = xb[:, 3*d:4*d].astype(F32)
    zeros = jnp.zeros((tq, 2*d), BF)
    def split(z):
        hi = z.astype(BF)
        lo = (z - hi.astype(F32)).astype(BF)
        return hi, lo
    qh, ql = split(q * (scale * math.log2(math.e)))
    wq = jnp.concatenate([qh, ql, zeros], axis=1)
    def p1(i, m):
        r = pl.ds(pl.multiple_of(i * ck, ck), ck)
        s = lax.dot_general(a_ref[r, :], wq, NT, preferred_element_type=F32)
        s_ref[r, :] = s
        return jnp.maximum(m, jnp.max(s.reshape(ck // 8, 8, tq), axis=0))
    m = lax.fori_loop(0, nck, p1, jnp.full((8, tq), -jnp.inf, F32), unroll=un)
    m = jnp.max(m, axis=0, keepdims=True)
    def p2(i, o):
        r = pl.ds(pl.multiple_of(i * ck, ck), ck)
        e = jnp.exp2(s_ref[r, :] - m)
        s_ref[r, :] = e
        eb = e.astype(BF)
        e_ref[r, :] = eb
        return o + jnp.dot(vt_ref[:, r], eb, preferred_element_type=F32)
    o = lax.fori_loop(0, nck, p2, jnp.zeros((d + 16, tq), F32), unroll=un)
    inv = 1.0 / o[d:d+1, :]
    ot = o[:d] * inv
    ob = ot.T
    delta = jnp.sum(ob * do, axis=1, keepdims=True)
    invc = jnp.broadcast_to(inv, (8, tq)).T[:, 0:1]
    dh = (-delta).astype(BF); dr = -delta - dh.astype(F32)
    dm = dr.astype(BF); dl = (dr - dm.astype(F32)).astype(BF)
    lane = lax.broadcasted_iota(jnp.int32, (tq, d), 1)
    dd = jnp.where(lane == 0, dh.astype(F32), jnp.where(lane == 1, dm.astype(F32), jnp.where(lane == 2, dl.astype(F32), 0.0))).astype(BF)
    wd = jnp.concatenate([zeros, xb[:, 3*d:], dd], axis=1)
    gh, gl = split(do * invc)
    rh, rl = split(q * (invc * scale))
    we = jnp.concatenate([zeros, gh, gl], axis=1)
    ws = jnp.concatenate([rh, rl, zeros], axis=1)
    def p3(i, dq):
        r = pl.ds(pl.multiple_of(i * ck, ck), ck)
        dp = lax.dot_general(a_ref[r, :], wd, NT, preferred_element_type=F32)
        ds = (s_ref[r, :] * dp).astype(BF)
        acc_ref[r, :] += (jnp.dot(ds, ws, preferred_element_type=F32)
                          + jnp.dot(e_ref[r, :], we, preferred_element_type=F32))
        return dq + jnp.dot(kt_ref[:, r], ds, preferred_element_type=F32)
    dq = lax.fori_loop(0, nck, p3, jnp.zeros((d, tq), F32), unroll=un)
    dq = dq * (inv * scale)
    o_ref[rows, 0:2*d] = jnp.concatenate([ot, dq], axis=0).T.astype(BF)
    @pl.when(step == pl.num_programs(0) - 1)
    def _():
        acc = acc_ref[...]
        dk = acc[:, :d] + acc[:, d:2*d]
        dv = acc[:, 2*d:3*d] + acc[:, 3*d:]
        o_ref[:, 2*d:] = jnp.concatenate([dk, dv], axis=1).astype(BF)

def attn(x, tq=768, ck=3840, un=1):
    tok = x.shape[0]
    return pl.pallas_call(
        functools.partial(attn_kernel, 1.0/math.sqrt(32), tq, ck, un),
        grid=(tok // tq,),
        in_specs=[pl.BlockSpec((tok, 128), lambda i: (0, 0))],
        out_specs=pl.BlockSpec((tok, 128), lambda i: (0, 0)),
        out_shape=jax.ShapeDtypeStruct((tok, 128), BF),
        scratch_shapes=[pltpu.VMEM((tok, 128), BF), pltpu.VMEM((32, tok), BF), pltpu.VMEM((48, tok), BF),
                        pltpu.VMEM((tok, tq), F32), pltpu.VMEM((tok, tq), BF), pltpu.VMEM((tok, 128), F32)],
        compiler_params=pltpu.CompilerParams(vmem_limit_bytes=48 << 20),
        cost_estimate=pl.CostEstimate(flops=6*2*tok*tok*128, bytes_accessed=4*tok*128, transcendentals=tok*tok),
    )(x)


LANES = 128
CALL = functools.partial(pltpu.CompilerParams, vmem_limit_bytes=40 << 20)


def cost(flops, moved):
    return pl.CostEstimate(flops=int(flops), bytes_accessed=int(moved), transcendentals=0)


def padded(plane):
    width, chans = plane.shape
    return jnp.concatenate([plane.astype(F32), jnp.zeros((LANES - width, chans), F32)], axis=0)


def pick_kernel(rows, act_ref, outer_ref, out_ref):
    group = out_ref.shape[0]
    frames, width, chans = act_ref.shape
    for f in range(frames):
        for at, src in ((f, act_ref), (frames + f, outer_ref)):
            plane = src[f].astype(F32)
            for c in range(2):
                parts = [plane[:, b + c * rows : b + (c + 1) * rows] for b in range(0, chans, 2 * rows)]
                part = jnp.concatenate(parts, axis=1).astype(BF)
                for x in range(group // 2):
                    out_ref[2 * x + c, at] = part


def pick(act, outer, rows):
    frames, width, chans = act.shape
    return pl.pallas_call(
        functools.partial(pick_kernel, rows),
        out_shape=jax.ShapeDtypeStruct((GROUP, 2 * frames, width, chans // 2), BF),
        compiler_params=CALL(),
        cost_estimate=cost(1e8, 3 << 20),
    )(act, outer)


def turn_kernel(r_ref, at_ref):
    group = r_ref.shape[0]
    frames = at_ref.shape[1]
    for f in range(frames):
        for row in range(group + 2):
            if row == 0:
                plane = r_ref[0, frames + f]
            elif row == group + 1:
                plane = r_ref[group - 1, frames + f]
            else:
                plane = r_ref[row - 1, f]
            tile = padded(plane).T
            cols = slice(row * LANES, (row + 1) * LANES)
            at_ref[0, f, :, cols] = pltpu.roll(tile, 1, 1).astype(BF)
            at_ref[1, f, :, cols] = tile.astype(BF)
            at_ref[2, f, :, cols] = pltpu.roll(tile, LANES - 1, 1).astype(BF)


def turn(r, frames):
    group, _, _, chans = r.shape
    return pl.pallas_call(
        turn_kernel,
        out_shape=jax.ShapeDtypeStruct((3, frames, chans, (group + 2) * LANES), BF),
        compiler_params=CALL(),
        cost_estimate=cost(1e9, 6 << 20),
    )(r)


def turn_pair_kernel(*refs):
    ins, outs = refs[:4], refs[4:]
    for own, other, out in ((ins[0], ins[1], outs[0]), (ins[2], ins[3], outs[1])):
        count = own.shape[0]
        for d, src in enumerate((own, other)):
            for f in range(count):
                at = (d * count + f) * LANES
                out[:, at : at + LANES] = padded(src[f]).T.astype(BF)


def turn_pair(own_r, other_r, own_b, other_b):
    chans = own_r.shape[-1]
    return pl.pallas_call(
        turn_pair_kernel,
        out_shape=tuple(
            jax.ShapeDtypeStruct((chans, 2 * x.shape[0] * LANES), BF) for x in (own_r, own_b)
        ),
        compiler_params=CALL(),
        cost_estimate=cost(1e9, 4 << 20),
    )(own_r, other_r, own_b, other_b)


def local_terms_kernel(
    line_ref, rt_ref, bt_ref, a0_ref, a1_ref, p0_ref, p1_ref, c0_ref, c1_ref, *refs
):
    outs, (at_ref, pay_ref, cot_ref, mix_ref, out_ref) = refs[:4], refs[4:]
    frames, width, chans = a0_ref.shape
    half = chans // 2
    for d, (a, p, c) in enumerate(((a0_ref, p0_ref, c0_ref), (a1_ref, p1_ref, c1_ref))):
        for f in range(frames):
            at = (d * frames + f) * LANES
            at_ref[:, at : at + LANES] = padded(a[f]).T.astype(BF)
            pay_ref[at : at + LANES, :] = padded(p[f]).astype(BF)
            cot_ref[at : at + LANES, :] = padded(c[f]).astype(BF)
    parts, _, rows, _ = out_ref.shape
    block = parts * rows

    def put(first, value, lane=0):
        for n in range(value.shape[0] // block):
            for y in range(parts):
                at = n * block + y * rows
                out_ref[y, first + n, :, lane : lane + value.shape[1]] = value[at : at + rows].astype(BF)

    for k in range(3):
        acc = jnp.zeros((chans, half), F32)
        for d in range(2):
            left = bt_ref[:, (2 * d * frames + k) * LANES : (2 * d * frames + k + frames) * LANES]
            right = pay_ref[d * frames * LANES : (d + 1) * frames * LANES, 3 * half :]
            acc = acc + jnp.dot(left, right, preferred_element_type=F32)
        put(k * chans // block, acc)
    for p in range(3):
        right = pay_ref[:, p * half : (p + 1) * half]
        for lane in range(0, half, LANES):
            value = jnp.dot(rt_ref[...], right[:, lane : lane + LANES], preferred_element_type=F32)
            mix_ref[lane // LANES, pl.ds(p, chans, stride=3), :] = value
    for lane in range(0, half, LANES):
        put(3 * chans // block, mix_ref[lane // LANES], lane)
    put(6 * chans // block, jnp.dot(at_ref[...], cot_ref[...], preferred_element_type=F32))
    for k, out in enumerate(outs):
        out[...] = out_ref[lax.rem(line_ref[0] + k, parts)]


def local_terms(line, rt, bt, atted, pay, cot):
    frames, width, chans = atted[0].shape
    half = chans // 2
    span = 2 * frames * LANES
    piece = (7 * chans // 64, 16, half)
    return pl.pallas_call(
        local_terms_kernel,
        out_shape=(jax.ShapeDtypeStruct(piece, BF),) * 4,
        in_specs=[pl.BlockSpec(memory_space=pltpu.SMEM)] + [pl.BlockSpec(memory_space=pltpu.VMEM)] * 8,
        scratch_shapes=[
            pltpu.VMEM((chans, span), BF),
            pltpu.VMEM((span, 4 * half), BF),
            pltpu.VMEM((span, half), BF),
            pltpu.VMEM((half // LANES, 3 * chans, LANES), F32),
            pltpu.VMEM((4,) + piece, BF),
        ],
        compiler_params=CALL(),
        cost_estimate=cost(2e9, 10 << 20),
    )(line, rt, bt, *atted, *pay, *cot)


def conv_terms_kernel(at_ref, dpre_ref, *refs):
    parts, (out_ref, dp_ref, part_ref, sems) = refs[:4], refs[4:]
    step = pl.program_id(0)
    group, frames, width, cols = dpre_ref.shape
    chans = at_ref.shape[2]
    rows = out_ref.shape[1]
    blocks = chans // rows
    copies = [pltpu.make_async_copy(src, part_ref.at[k], sems.at[k]) for k, src in enumerate(parts)]

    @pl.when(step == 0)
    def _():
        for copy in copies:
            copy.start()
        for f in range(frames):
            for row in range(group):
                dp_ref[f, row * LANES : (row + 1) * LANES, :] = padded(dpre_ref[row, f]).astype(BF)

    span = group * LANES
    for i in range(3):
        acc = jnp.zeros((chans, cols), F32)
        for f in range(frames):
            left = at_ref[0, f, :, i * LANES : i * LANES + span]
            acc = acc + jnp.dot(left, dp_ref[f], preferred_element_type=F32)
        value = acc.astype(BF)
        for b in range(blocks):
            out_ref[(3 * i + step) * blocks + b] = value[b * rows : (b + 1) * rows]

    @pl.when(step == 2)
    def _():
        for copy in copies:
            copy.wait()
        for n in range(part_ref.shape[1]):
            value = part_ref[0, n].astype(F32)
            for k in range(1, 4):
                value = value + part_ref[k, n].astype(F32)
            value = value.astype(BF)
            out_ref[9 * blocks + n] = jnp.concatenate([value[:, :cols], value[:, cols:]], axis=0)


def conv_terms(at, dpre, parts, owners, rows):
    group, frames, width, cols = dpre.shape
    return pl.pallas_call(
        conv_terms_kernel,
        grid=(3,),
        in_specs=[
            pl.BlockSpec((1,) + at.shape[1:], lambda j: (j, 0, 0, 0)),
            pl.BlockSpec(dpre.shape, lambda j: (0, 0, 0, 0)),
        ]
        + [pl.BlockSpec(memory_space=pl.ANY)] * 4,
        out_specs=pl.BlockSpec((owners, rows, cols), lambda j: (0, 0, 0)),
        out_shape=jax.ShapeDtypeStruct((owners, rows, cols), BF),
        scratch_shapes=[
            pltpu.VMEM((frames, group * LANES, cols), BF),
            pltpu.VMEM((4,) + parts[0].shape, BF),
            pltpu.SemaphoreType.DMA((4,)),
        ],
        compiler_params=pltpu.CompilerParams(vmem_limit_bytes=60 << 20),
        cost_estimate=cost(2e9, 10 << 20),
    )(at, dpre, *parts)


def sum_kernel(norm, dims, which_ref, terms_ref, out_ref):
    times, ys, xs = dims
    rows, cols = terms_ref.shape[1:]

    @pl.when(which_ref[0] == 1)
    def _():
        for x in range(xs):
            for c in range(2):
                acc = jnp.zeros((rows, cols), F32)
                for t in range(times):
                    for y in range(ys):
                        acc = acc + terms_ref[((t * ys + y) * xs + x) * 2 + c].astype(F32)
                out_ref[c * rows : (c + 1) * rows, x * cols : (x + 1) * cols] = acc * norm

    @pl.when(which_ref[0] == 0)
    def _():
        part = rows // 2
        for y in range(ys):
            for c in range(2):
                acc = jnp.zeros((rows, cols), F32)
                for t in range(times):
                    for x in range(xs):
                        acc = acc + terms_ref[((t * ys + y) * xs + x) * 2 + c].astype(F32)
                acc = acc * norm
                for h in range(2):
                    at = (2 * c + h) * cols
                    out_ref[y * part : (y + 1) * part, at : at + cols] = acc[h * part : (h + 1) * part]


def sum_terms(which, terms, norm, dims):
    owners, rows, cols = terms.shape
    return pl.pallas_call(
        functools.partial(sum_kernel, norm, dims),
        out_shape=jax.ShapeDtypeStruct((2 * rows, 4 * cols), F32),
        in_specs=[pl.BlockSpec(memory_space=pltpu.SMEM), pl.BlockSpec(memory_space=pltpu.VMEM)],
        compiler_params=CALL(),
        cost_estimate=cost(1e7, 1 << 20),
    )(which, terms)


def dpre_kernel(own_ref, next_ref, slope_ref, tw_ref, dpre_ref, near_ref):
    frames, width, chans = own_ref.shape
    group, _, _, cols = near_ref.shape
    ext = [own_ref[f] for f in range(frames)] + [next_ref[f] for f in range(frames)]
    for f in range(frames):
        acc = jnp.zeros((width, chans), F32)
        for k in range(3):
            acc = acc + dot_nt(ext[f + 2 - k], tw_ref[k * chans : (k + 1) * chans, :])
        value = (acc * slope_ref[f]).astype(BF)
        dpre_ref[f] = value
        for e in range(group):
            near_ref[e, f] = value[:, (e // 2) * cols : (e // 2 + 1) * cols]


def make_dpre(own, nxt, slope, tw):
    frames, width, chans = own.shape
    return pl.pallas_call(
        dpre_kernel,
        out_shape=(
            jax.ShapeDtypeStruct((frames, width, chans), BF),
            jax.ShapeDtypeStruct((GROUP, frames, width, 2 * chans // GROUP), BF),
        ),
        compiler_params=CALL(),
        cost_estimate=cost(5e8, 3 << 20),
    )(own, nxt, slope, tw)


def dact_kernel(mid_ref, above_ref, below_ref, dres_ref, x_ref, sw_ref, out_ref):
    frames, width, chans = mid_ref.shape
    line = lax.broadcasted_iota(jnp.int32, (width, chans), 0)
    for f in range(frames):
        acc = jnp.zeros((width, chans), F32)
        for i, src in enumerate((below_ref, mid_ref, above_ref)):
            plane = src[f]
            wide = plane.astype(F32)
            right = jnp.where(line == width - 1, 0.0, pltpu.roll(wide, width - 1, 0)).astype(BF)
            left = jnp.where(line == 0, 0.0, pltpu.roll(wide, 1, 0)).astype(BF)
            for j, value in enumerate((right, plane, left)):
                tap = 3 * i + j
                acc = acc + dot_nt(value, sw_ref[tap * chans : (tap + 1) * chans, :])
        x = x_ref[f].astype(F32)
        sigma = 1.0 / (1.0 + jnp.exp(-x))
        slope = sigma * (1.0 + x * (1.0 - sigma))
        out_ref[f] = (dres_ref[f] + acc * slope).astype(BF)


def make_grad_latents(mid, above, below, dres, x, sw):
    return pl.pallas_call(
        dact_kernel,
        out_shape=jax.ShapeDtypeStruct(mid.shape, BF),
        compiler_params=CALL(),
        cost_estimate=cost(2e9, 8 << 20),
    )(mid, above, below, dres, x, sw)


def silu_slope(value):
    sigma = jax.nn.sigmoid(value)
    return sigma * (1.0 + value * (1.0 - sigma))


def matmul(left, right):
    return jnp.dot(left, right, preferred_element_type=F32)


def shift(x, axis, by):
    count = lax.axis_size(axis)
    pairs = [(i, i + by) for i in range(count) if 0 <= i + by < count]
    return lax.ppermute(x, axis, pairs)


def swap(x):
    count = lax.axis_size("space")
    return lax.ppermute(x, "space", [(i, i ^ 1) for i in range(count)])


def neighbours(field):
    return shift(field, "space", 1), shift(field, "space", -1)


def exchange(x):
    count = lax.axis_size("space")
    groups = [list(range(at, at + GROUP)) for at in range(0, count, GROUP)]
    return lax.all_to_all(x, "space", 0, 0, axis_index_groups=groups, tiled=True)


def along_y(x, by):
    count = lax.axis_size("space")
    return lax.ppermute(x, "space", [(i, (i + by * GROUP) % count) for i in range(count)])


def pick_one(x, index):
    return lax.dynamic_index_in_dim(x, index, 0, keepdims=False)


def side_pad(field):
    return jnp.pad(field, ((0, 0), (0, 0), (1, 1), (0, 0)))


def taps_of(padded, width):
    pieces = [padded[:, i, j : j + width] for i in range(3) for j in range(3)]
    return jnp.concatenate(pieces, axis=-1).reshape(-1, 9 * padded.shape[-1])


def per_device(latents, spatial_weight, temporal_weight, qkv_weight, out_weight, cotangent):
    frames, rows, width, chans = latents.shape
    ntok = frames * width
    n_space = lax.axis_size("space")
    n_time = lax.axis_size("tm")
    owners = n_space * n_time
    depth = chans // HEADS
    norm = 1.0 / math.sqrt(ntok * n_space * n_time)
    here = lax.axis_index("space")
    core, line = here % 2, here // GROUP
    half = chans // 2
    share = 16 * chans // (2 * owners)

    x = latents.reshape(frames, width, chans)
    cot = cotangent.reshape(frames, width, chans)
    act = jax.nn.silu(x.astype(F32)).astype(BF)
    above, below = neighbours(act)
    pre = matmul(taps_of(side_pad(jnp.stack([above, act, below], axis=1)), width), fetch(spatial_weight))
    pre = pre.reshape(frames, width, chans)
    bact = jax.nn.silu(pre).astype(BF)
    bext = jnp.concatenate([shift(bact, "tm", 1), bact], axis=0)
    resid, rres, items = proj(x, bext, cot, temporal_weight, qkv_weight, out_weight)
    items = items.reshape(frames * HEADS, width, 4 * depth)
    items = lax.all_to_all(items, "space", 0, 0, tiled=True)

    early = pick(act, jnp.where(here % GROUP == 0, above, below), share)
    chalf = cot.reshape(frames, width, 2, half).transpose(2, 0, 1, 3)
    cpair = (pick_one(chalf, core), swap(pick_one(chalf, 1 - core)))
    rother, bother = swap(rres), swap(bext)
    early, cpair, rother, bother, items = lax.optimization_barrier((early, cpair, rother, bother, items))
    early = exchange(early)
    outs = attn(items.reshape(n_space * width, 4 * depth)).reshape(n_space, width, 4 * depth)
    outs, early, rother, bother = lax.optimization_barrier((outs, early, rother, bother))
    outs = lax.all_to_all(outs, "space", 0, 0, tiled=True)
    aturn = turn(early, frames)
    rturn, bturn = turn_pair(rres, rother, bext, bother)
    slope = silu_slope(pre)
    outs, aturn, rturn, bturn, slope = lax.optimization_barrier((outs, aturn, rturn, bturn, slope))

    core_at = core.astype(jnp.int32).reshape(1)
    outs = outs.reshape(frames, HEADS, width, 4 * depth)
    atted, dres, dresb, mine, other = post(core_at, outs, cot, qkv_weight)
    dnext = shift(dresb, "tm", -1)
    local = local_terms(line.astype(jnp.int32).reshape(1), rturn, bturn, (atted, swap(atted)), (mine, swap(other)), cpair)
    dnext, _ = lax.optimization_barrier((dnext, local[0]))
    dpre, near = make_dpre(dresb, dnext, slope, temporal_weight)
    near = exchange(near)
    dabove, dbelow = neighbours(dpre)
    parts = [local[0]] + [along_y(local[by], by) for by in range(1, 4)]
    mixed = resid.reshape(ntok, chans) + matmul(atted.reshape(ntok, chans), out_weight)
    mixed = mixed.astype(BF).reshape(latents.shape)
    mixed, near = lax.optimization_barrier((mixed, near))
    terms = conv_terms(aturn, near, parts, owners, share)
    terms, dpre, dabove, dbelow = lax.optimization_barrier((terms, dpre, dabove, dbelow))
    terms = lax.all_to_all(terms, ("tm", "space"), 0, 0, tiled=True)
    grad_latents = make_grad_latents(dpre, dabove, dbelow, dres, x, spatial_weight).reshape(latents.shape)
    index = lax.axis_index("tm") * n_space + here
    which = (index < 9 * chans // (2 * share)).astype(jnp.int32).reshape(1)
    grad_weights = sum_terms(which, terms, norm, (n_time, n_space // GROUP, GROUP // 2))
    return (mixed, grad_latents, grad_weights)


def solution(mesh):
    placed = (P("tm", "space", None, None), P(), P(), P(), P(), P("tm", "space", None, None))
    return jax.shard_map(
        per_device,
        mesh=mesh,
        in_specs=placed,
        out_specs=(
            P("tm", "space", None, None),
            P("tm", "space", None, None),
            P(("tm", "space"), None),
        ),
        check_vma=False,
    )
```

```python
import functools
import math

import jax
import jax.numpy as jnp
from jax import lax
from jax.experimental import pallas as pl
from jax.experimental.pallas import tpu as pltpu
from jax.sharding import PartitionSpec as P

HEADS = 16
GROUP = 8
F32 = jnp.float32
BF = jnp.bfloat16
NT = (((1,), (1,)), ((), ()))

def dot_nt(left, right):
    return lax.dot_general(left, right, NT, preferred_element_type=F32)


def proj_kernel(x_ref, bext_ref, cot_ref, tw_ref, qw_ref, ow_ref, resid_ref, rres_ref, items_ref):
    frames, width, chans = x_ref.shape
    d = chans // HEADS
    for f in range(frames):
        acc = x_ref[f].astype(F32)
        for k in range(3):
            tap = tw_ref[k * chans : (k + 1) * chans, :]
            acc = acc + jnp.dot(bext_ref[f + k], tap, preferred_element_type=F32)
        resid_ref[f] = acc
        rounded = acc.astype(BF)
        rres_ref[f] = rounded
        qkv = jnp.dot(rounded, qw_ref[...], preferred_element_type=F32)
        dattn = dot_nt(cot_ref[f], ow_ref[...])
        for h in range(HEADS):
            parts = [qkv[:, p * chans + h * d : p * chans + (h + 1) * d] for p in range(3)]
            parts.append(dattn[:, h * d : (h + 1) * d])
            items_ref[f, h] = jnp.concatenate(parts, axis=1).astype(BF)


def proj(x, bext, cot, tw, qw, ow):
    frames, width, chans = x.shape
    return pl.pallas_call(
        proj_kernel,
        out_shape=(
            jax.ShapeDtypeStruct((frames, width, chans), F32),
            jax.ShapeDtypeStruct((frames, width, chans), BF),
            jax.ShapeDtypeStruct((frames, HEADS, width, 4 * chans // HEADS), BF),
        ),
        compiler_params=pltpu.CompilerParams(vmem_limit_bytes=32 << 20),
        cost_estimate=pl.CostEstimate(flops=10**9 * 2, bytes_accessed=6 << 20, transcendentals=0),
    )(x, bext, cot, tw, qw, ow)


def post_kernel(core_ref, z_ref, cot_ref, qw_ref, attn_ref, dres_ref, dresb_ref, mine_ref, other_ref):
    frames, width, chans = cot_ref.shape
    d = chans // HEADS
    half = chans // 2
    all_parts = []
    for f in range(frames):
        heads = [z_ref[f, h].astype(F32) for h in range(HEADS)]
        dres = cot_ref[f].astype(F32)
        parts = [jnp.concatenate([z[:, p * d : (p + 1) * d] for z in heads], axis=1).astype(BF) for p in range(4)]
        attn_ref[f] = parts[0]
        for p in range(3):
            dres = dres + dot_nt(parts[p + 1], qw_ref[:, p * chans : (p + 1) * chans])
        dres_ref[f] = dres
        dresb = dres.astype(BF)
        dresb_ref[f] = dresb
        all_parts.append(parts[1:] + [dresb])

    def store(first, second):
        for f in range(frames):
            for at, part in enumerate(all_parts[f]):
                for out, c in ((first, 0), (second, 1)):
                    out[f, :, at * half : (at + 1) * half] = part[:, c * half : (c + 1) * half]

    @pl.when(core_ref[0] == 0)
    def _():
        store(mine_ref, other_ref)

    @pl.when(core_ref[0] == 1)
    def _():
        store(other_ref, mine_ref)


def post(core, z, cot, qw):
    frames, width, chans = cot.shape
    return pl.pallas_call(
        post_kernel,
        out_shape=(
            jax.ShapeDtypeStruct((frames, width, chans), BF),
            jax.ShapeDtypeStruct((frames, width, chans), F32),
            jax.ShapeDtypeStruct((frames, width, chans), BF),
            jax.ShapeDtypeStruct((frames, width, 2 * chans), BF),
            jax.ShapeDtypeStruct((frames, width, 2 * chans), BF),
        ),
        in_specs=[pl.BlockSpec(memory_space=pltpu.SMEM)] + [pl.BlockSpec(memory_space=pltpu.VMEM)] * 3,
        compiler_params=pltpu.CompilerParams(vmem_limit_bytes=32 << 20),
        cost_estimate=pl.CostEstimate(flops=10**9, bytes_accessed=6 << 20, transcendentals=0),
    )(core, z, cot, qw)


def fetch_kernel(w_ref, out_ref):
    out_ref[...] = w_ref[...]


def fetch(w):
    return pl.pallas_call(
        fetch_kernel,
        out_shape=jax.ShapeDtypeStruct(w.shape, w.dtype),
        compiler_params=pltpu.CompilerParams(vmem_limit_bytes=24 << 20),
        cost_estimate=pl.CostEstimate(flops=10**6, bytes_accessed=10 << 20, transcendentals=0),
    )(w)


def attn_kernel(scale, tq, ck, un, x_ref, o_ref, a_ref, kt_ref, vt_ref, s_ref, e_ref, acc_ref):
    tok = x_ref.shape[0]
    step = pl.program_id(0)
    nck = tok // ck
    d = 32
    @pl.when(step == 0)
    def _():
        k = x_ref[:, d:2*d]
        v = x_ref[:, 2*d:3*d]
        lane = lax.broadcasted_iota(jnp.int32, (tok, d), 1)
        ones = jnp.where(lane < 3, 1.0, 0.0).astype(BF)
        a_ref[...] = jnp.concatenate([k, k, v, ones], axis=1)
        kt_ref[...] = k.astype(F32).T.astype(BF)
        vt_ref[...] = jnp.concatenate([v, ones], axis=1).astype(F32).T[: d + 16].astype(BF)
        acc_ref[...] = jnp.zeros_like(acc_ref)
    rows = pl.ds(pl.multiple_of(step * tq, tq), tq)
    xb = x_ref[rows, :]
    q = xb[:, 0:d].astype(F32)
    do = xb[:, 3*d:4*d].astype(F32)
    zeros = jnp.zeros((tq, 2*d), BF)
    def split(z):
        hi = z.astype(BF)
        lo = (z - hi.astype(F32)).astype(BF)
        return hi, lo
    qh, ql = split(q * (scale * math.log2(math.e)))
    wq = jnp.concatenate([qh, ql, zeros], axis=1)
    def p1(i, m):
        r = pl.ds(pl.multiple_of(i * ck, ck), ck)
        s = lax.dot_general(a_ref[r, :], wq, NT, preferred_element_type=F32)
        s_ref[r, :] = s
        return jnp.maximum(m, jnp.max(s.reshape(ck // 8, 8, tq), axis=0))
    m = lax.fori_loop(0, nck, p1, jnp.full((8, tq), -jnp.inf, F32), unroll=un)
    m = jnp.max(m, axis=0, keepdims=True)
    def p2(i, o):
        r = pl.ds(pl.multiple_of(i * ck, ck), ck)
        e = jnp.exp2(s_ref[r, :] - m)
        s_ref[r, :] = e
        eb = e.astype(BF)
        e_ref[r, :] = eb
        return o + jnp.dot(vt_ref[:, r], eb, preferred_element_type=F32)
    o = lax.fori_loop(0, nck, p2, jnp.zeros((d + 16, tq), F32), unroll=un)
    inv = 1.0 / o[d:d+1, :]
    ot = o[:d] * inv
    ob = ot.T
    delta = jnp.sum(ob * do, axis=1, keepdims=True)
    invc = jnp.broadcast_to(inv, (8, tq)).T[:, 0:1]
    dh = (-delta).astype(BF); dr = -delta - dh.astype(F32)
    dm = dr.astype(BF); dl = (dr - dm.astype(F32)).astype(BF)
    lane = lax.broadcasted_iota(jnp.int32, (tq, d), 1)
    dd = jnp.where(lane == 0, dh.astype(F32), jnp.where(lane == 1, dm.astype(F32), jnp.where(lane == 2, dl.astype(F32), 0.0))).astype(BF)
    wd = jnp.concatenate([zeros, xb[:, 3*d:], dd], axis=1)
    gh, gl = split(do * invc)
    rh, rl = split(q * (invc * scale))
    none = zeros[:, :d]
    we = jnp.concatenate([none, gl, none, gh], axis=1)
    ws = jnp.concatenate([rl, none, rh, none], axis=1)
    def p3(i, dq):
        r = pl.ds(pl.multiple_of(i * ck, ck), ck)
        dp = lax.dot_general(a_ref[r, :], wd, NT, preferred_element_type=F32)
        ds = (s_ref[r, :] * dp).astype(BF)
        acc_ref[r, :] += (jnp.dot(ds, ws, preferred_element_type=F32)
                          + jnp.dot(e_ref[r, :], we, preferred_element_type=F32))
        return dq + jnp.dot(kt_ref[:, r], ds, preferred_element_type=F32)
    dq = lax.fori_loop(0, nck, p3, jnp.zeros((d, tq), F32), unroll=un)
    dq = dq * (inv * scale)
    o_ref[rows, 0:2*d] = jnp.concatenate([ot, dq], axis=0).T.astype(BF)
    @pl.when(step == pl.num_programs(0) - 1)
    def _():
        acc = acc_ref[...]
        acc = acc + pltpu.roll(acc, 2*d, 1)
        o_ref[:, 2*d:] = acc[:, 2*d:].astype(BF)

def attn(x, tq=768, ck=3840, un=1):
    tok = x.shape[0]
    return pl.pallas_call(
        functools.partial(attn_kernel, 1.0/math.sqrt(32), tq, ck, un),
        grid=(tok // tq,),
        in_specs=[pl.BlockSpec((tok, 128), lambda i: (0, 0))],
        out_specs=pl.BlockSpec((tok, 128), lambda i: (0, 0)),
        out_shape=jax.ShapeDtypeStruct((tok, 128), BF),
        scratch_shapes=[pltpu.VMEM((tok, 128), BF), pltpu.VMEM((32, tok), BF), pltpu.VMEM((48, tok), BF),
                        pltpu.VMEM((tok, tq), F32), pltpu.VMEM((tok, tq), BF), pltpu.VMEM((tok, 128), F32)],
        compiler_params=pltpu.CompilerParams(vmem_limit_bytes=48 << 20),
        cost_estimate=pl.CostEstimate(flops=6*2*tok*tok*128, bytes_accessed=4*tok*128, transcendentals=tok*tok),
    )(x)


LANES = 128
CALL = functools.partial(pltpu.CompilerParams, vmem_limit_bytes=40 << 20)


def cost(flops, moved):
    return pl.CostEstimate(flops=int(flops), bytes_accessed=int(moved), transcendentals=0)


def padded(plane):
    width, chans = plane.shape
    return jnp.concatenate([plane.astype(F32), jnp.zeros((LANES - width, chans), F32)], axis=0)


def pick_kernel(rows, act_ref, outer_ref, out_ref):
    group = out_ref.shape[0]
    frames, width, chans = act_ref.shape
    for f in range(frames):
        for at, src in ((f, act_ref), (frames + f, outer_ref)):
            plane = src[f].astype(F32)
            for c in range(2):
                parts = [plane[:, b + c * rows : b + (c + 1) * rows] for b in range(0, chans, 2 * rows)]
                part = jnp.concatenate(parts, axis=1).astype(BF)
                for x in range(group // 2):
                    out_ref[2 * x + c, at] = part


def pick(act, outer, rows):
    frames, width, chans = act.shape
    return pl.pallas_call(
        functools.partial(pick_kernel, rows),
        out_shape=jax.ShapeDtypeStruct((GROUP, 2 * frames, width, chans // 2), BF),
        compiler_params=CALL(),
        cost_estimate=cost(1e8, 3 << 20),
    )(act, outer)


def turn_kernel(r_ref, at_ref):
    group = r_ref.shape[0]
    frames = at_ref.shape[1]
    for f in range(frames):
        for row in range(group + 2):
            if row == 0:
                plane = r_ref[0, frames + f]
            elif row == group + 1:
                plane = r_ref[group - 1, frames + f]
            else:
                plane = r_ref[row - 1, f]
            tile = padded(plane).T
            cols = slice(row * LANES, (row + 1) * LANES)
            at_ref[0, f, :, cols] = pltpu.roll(tile, 1, 1).astype(BF)
            at_ref[1, f, :, cols] = tile.astype(BF)
            at_ref[2, f, :, cols] = pltpu.roll(tile, LANES - 1, 1).astype(BF)


def turn(r, frames):
    group, _, _, chans = r.shape
    return pl.pallas_call(
        turn_kernel,
        out_shape=jax.ShapeDtypeStruct((3, frames, chans, (group + 2) * LANES), BF),
        compiler_params=CALL(),
        cost_estimate=cost(1e9, 6 << 20),
    )(r)


def turn_pair_kernel(*refs):
    ins, outs = refs[:4], refs[4:]
    for own, other, out in ((ins[0], ins[1], outs[0]), (ins[2], ins[3], outs[1])):
        count = own.shape[0]
        for d, src in enumerate((own, other)):
            for f in range(count):
                at = (d * count + f) * LANES
                out[:, at : at + LANES] = padded(src[f]).T.astype(BF)


def turn_pair(own_r, other_r, own_b, other_b):
    chans = own_r.shape[-1]
    return pl.pallas_call(
        turn_pair_kernel,
        out_shape=tuple(
            jax.ShapeDtypeStruct((chans, 2 * x.shape[0] * LANES), BF) for x in (own_r, own_b)
        ),
        compiler_params=CALL(),
        cost_estimate=cost(1e9, 4 << 20),
    )(own_r, other_r, own_b, other_b)


def local_terms_kernel(
    line_ref, rt_ref, bt_ref, a0_ref, a1_ref, p0_ref, p1_ref, c0_ref, c1_ref, *refs
):
    outs, (at_ref, pay_ref, cot_ref, mix_ref, out_ref) = refs[:4], refs[4:]
    frames, width, chans = a0_ref.shape
    half = chans // 2
    for d, (a, p, c) in enumerate(((a0_ref, p0_ref, c0_ref), (a1_ref, p1_ref, c1_ref))):
        for f in range(frames):
            at = (d * frames + f) * LANES
            at_ref[:, at : at + LANES] = padded(a[f]).T.astype(BF)
            pay_ref[at : at + LANES, :] = padded(p[f]).astype(BF)
            cot_ref[at : at + LANES, :] = padded(c[f]).astype(BF)
    parts, _, rows, _ = out_ref.shape
    block = parts * rows

    def put(first, value, lane=0):
        for n in range(value.shape[0] // block):
            for y in range(parts):
                at = n * block + y * rows
                out_ref[y, first + n, :, lane : lane + value.shape[1]] = value[at : at + rows].astype(BF)

    for k in range(3):
        acc = jnp.zeros((chans, half), F32)
        for d in range(2):
            left = bt_ref[:, (2 * d * frames + k) * LANES : (2 * d * frames + k + frames) * LANES]
            right = pay_ref[d * frames * LANES : (d + 1) * frames * LANES, 3 * half :]
            acc = acc + jnp.dot(left, right, preferred_element_type=F32)
        put(k * chans // block, acc)
    for p in range(3):
        right = pay_ref[:, p * half : (p + 1) * half]
        for lane in range(0, half, LANES):
            value = jnp.dot(rt_ref[...], right[:, lane : lane + LANES], preferred_element_type=F32)
            mix_ref[lane // LANES, pl.ds(p, chans, stride=3), :] = value
    for lane in range(0, half, LANES):
        put(3 * chans // block, mix_ref[lane // LANES], lane)
    put(6 * chans // block, jnp.dot(at_ref[...], cot_ref[...], preferred_element_type=F32))
    for k, out in enumerate(outs):
        out[...] = out_ref[lax.rem(line_ref[0] + k, parts)]


def local_terms(line, rt, bt, atted, pay, cot):
    frames, width, chans = atted[0].shape
    half = chans // 2
    span = 2 * frames * LANES
    piece = (7 * chans // 64, 16, half)
    return pl.pallas_call(
        local_terms_kernel,
        out_shape=(jax.ShapeDtypeStruct(piece, BF),) * 4,
        in_specs=[pl.BlockSpec(memory_space=pltpu.SMEM)] + [pl.BlockSpec(memory_space=pltpu.VMEM)] * 8,
        scratch_shapes=[
            pltpu.VMEM((chans, span), BF),
            pltpu.VMEM((span, 4 * half), BF),
            pltpu.VMEM((span, half), BF),
            pltpu.VMEM((half // LANES, 3 * chans, LANES), F32),
            pltpu.VMEM((4,) + piece, BF),
        ],
        compiler_params=CALL(),
        cost_estimate=cost(2e9, 10 << 20),
    )(line, rt, bt, *atted, *pay, *cot)


def conv_terms_kernel(at_ref, dpre_ref, *refs):
    parts, (out_ref, dp_ref, acc_ref, part_ref, sems) = refs[:4], refs[4:]
    step = pl.program_id(0)
    group, _, width, cols = dpre_ref.shape
    shifts, _, chans, _ = at_ref.shape
    rows = out_ref.shape[1]
    blocks = chans // rows
    copies = [pltpu.make_async_copy(src, part_ref.at[k], sems.at[k]) for k, src in enumerate(parts)]

    @pl.when(step == 0)
    def _():
        for copy in copies:
            copy.start()

    for row in range(group):
        dp_ref[row * LANES : (row + 1) * LANES, :] = padded(dpre_ref[row, 0]).astype(BF)
    span = group * LANES

    def product(i):
        left = at_ref[:, 0, :, i * LANES : i * LANES + span].reshape(shifts * chans, span)
        return jnp.dot(left, dp_ref[...], preferred_element_type=F32)

    @pl.when(step == 0)
    def _():
        for i in range(3):
            acc_ref[i] = product(i)

    @pl.when(step == 1)
    def _():
        for i in range(3):
            value = (acc_ref[i] + product(i)).astype(BF)
            for b in range(shifts * blocks):
                out_ref[i * shifts * blocks + b] = value[b * rows : (b + 1) * rows]
        for copy in copies:
            copy.wait()
        for n in range(part_ref.shape[1]):
            value = part_ref[0, n].astype(F32)
            for k in range(1, 4):
                value = value + part_ref[k, n].astype(F32)
            value = value.astype(BF)
            out_ref[3 * shifts * blocks + n] = jnp.concatenate([value[:, :cols], value[:, cols:]], axis=0)


def conv_terms(at, dpre, parts, owners, rows):
    group, frames, width, cols = dpre.shape
    shifts, _, chans, lanes = at.shape
    assert frames == 2
    return pl.pallas_call(
        conv_terms_kernel,
        grid=(frames,),
        in_specs=[
            pl.BlockSpec((shifts, 1, chans, lanes), lambda f: (0, f, 0, 0)),
            pl.BlockSpec((group, 1, width, cols), lambda f: (0, f, 0, 0)),
        ]
        + [pl.BlockSpec(memory_space=pl.ANY)] * 4,
        out_specs=pl.BlockSpec((owners, rows, cols), lambda f: (0, 0, 0)),
        out_shape=jax.ShapeDtypeStruct((owners, rows, cols), BF),
        scratch_shapes=[
            pltpu.VMEM((group * LANES, cols), BF),
            pltpu.VMEM((3, shifts * chans, cols), F32),
            pltpu.VMEM((4,) + parts[0].shape, BF),
            pltpu.SemaphoreType.DMA((4,)),
        ],
        compiler_params=pltpu.CompilerParams(vmem_limit_bytes=60 << 20),
        cost_estimate=cost(2e9, 10 << 20),
    )(at, dpre, *parts)


def sum_kernel(norm, dims, which_ref, terms_ref, out_ref):
    times, ys, xs = dims
    rows, cols = terms_ref.shape[1:]

    @pl.when(which_ref[0] == 1)
    def _():
        for x in range(xs):
            for c in range(2):
                acc = jnp.zeros((rows, cols), F32)
                for t in range(times):
                    for y in range(ys):
                        acc = acc + terms_ref[((t * ys + y) * xs + x) * 2 + c].astype(F32)
                out_ref[c * rows : (c + 1) * rows, x * cols : (x + 1) * cols] = acc * norm

    @pl.when(which_ref[0] == 0)
    def _():
        part = rows // 2
        for y in range(ys):
            for c in range(2):
                acc = jnp.zeros((rows, cols), F32)
                for t in range(times):
                    for x in range(xs):
                        acc = acc + terms_ref[((t * ys + y) * xs + x) * 2 + c].astype(F32)
                acc = acc * norm
                for h in range(2):
                    at = (2 * c + h) * cols
                    out_ref[y * part : (y + 1) * part, at : at + cols] = acc[h * part : (h + 1) * part]


def sum_terms(which, terms, norm, dims):
    owners, rows, cols = terms.shape
    return pl.pallas_call(
        functools.partial(sum_kernel, norm, dims),
        out_shape=jax.ShapeDtypeStruct((2 * rows, 4 * cols), F32),
        in_specs=[pl.BlockSpec(memory_space=pltpu.SMEM), pl.BlockSpec(memory_space=pltpu.VMEM)],
        compiler_params=CALL(),
        cost_estimate=cost(1e7, 1 << 20),
    )(which, terms)


def dpre_kernel(own_ref, next_ref, slope_ref, tw_ref, dpre_ref, near_ref):
    frames, width, chans = own_ref.shape
    group, _, _, cols = near_ref.shape
    ext = [own_ref[f] for f in range(frames)] + [next_ref[f] for f in range(frames)]
    for f in range(frames):
        acc = jnp.zeros((width, chans), F32)
        for k in range(3):
            acc = acc + dot_nt(ext[f + 2 - k], tw_ref[k * chans : (k + 1) * chans, :])
        value = (acc * slope_ref[f]).astype(BF)
        dpre_ref[f] = value
        for e in range(group):
            near_ref[e, f] = value[:, (e // 2) * cols : (e // 2 + 1) * cols]


def make_dpre(own, nxt, slope, tw):
    frames, width, chans = own.shape
    return pl.pallas_call(
        dpre_kernel,
        out_shape=(
            jax.ShapeDtypeStruct((frames, width, chans), BF),
            jax.ShapeDtypeStruct((GROUP, frames, width, 2 * chans // GROUP), BF),
        ),
        compiler_params=CALL(),
        cost_estimate=cost(5e8, 3 << 20),
    )(own, nxt, slope, tw)


def dact_kernel(mid_ref, above_ref, below_ref, dres_ref, x_ref, sw_ref, out_ref):
    frames, width, chans = mid_ref.shape
    line = lax.broadcasted_iota(jnp.int32, (width, chans), 0)
    for f in range(frames):
        acc = jnp.zeros((width, chans), F32)
        for i, src in enumerate((below_ref, mid_ref, above_ref)):
            plane = src[f]
            wide = plane.astype(F32)
            right = jnp.where(line == width - 1, 0.0, pltpu.roll(wide, width - 1, 0)).astype(BF)
            left = jnp.where(line == 0, 0.0, pltpu.roll(wide, 1, 0)).astype(BF)
            for j, value in enumerate((right, plane, left)):
                tap = 3 * i + j
                acc = acc + dot_nt(value, sw_ref[tap * chans : (tap + 1) * chans, :])
        x = x_ref[f].astype(F32)
        sigma = 1.0 / (1.0 + jnp.exp(-x))
        slope = sigma * (1.0 + x * (1.0 - sigma))
        out_ref[f] = (dres_ref[f] + acc * slope).astype(BF)


def make_grad_latents(mid, above, below, dres, x, sw):
    return pl.pallas_call(
        dact_kernel,
        out_shape=jax.ShapeDtypeStruct(mid.shape, BF),
        compiler_params=CALL(),
        cost_estimate=cost(2e9, 8 << 20),
    )(mid, above, below, dres, x, sw)


def silu_slope(value):
    sigma = jax.nn.sigmoid(value)
    return sigma * (1.0 + value * (1.0 - sigma))


def matmul(left, right):
    return jnp.dot(left, right, preferred_element_type=F32)


def shift(x, axis, by):
    count = lax.axis_size(axis)
    pairs = [(i, i + by) for i in range(count) if 0 <= i + by < count]
    return lax.ppermute(x, axis, pairs)


def swap(x):
    count = lax.axis_size("space")
    return lax.ppermute(x, "space", [(i, i ^ 1) for i in range(count)])


def neighbours(field):
    return shift(field, "space", 1), shift(field, "space", -1)


def exchange(x):
    count = lax.axis_size("space")
    groups = [list(range(at, at + GROUP)) for at in range(0, count, GROUP)]
    return lax.all_to_all(x, "space", 0, 0, axis_index_groups=groups, tiled=True)


def along_y(x, by):
    count = lax.axis_size("space")
    return lax.ppermute(x, "space", [(i, (i + by * GROUP) % count) for i in range(count)])


def pick_one(x, index):
    return lax.dynamic_index_in_dim(x, index, 0, keepdims=False)


def side_pad(field):
    return jnp.pad(field, ((0, 0), (0, 0), (1, 1), (0, 0)))


def taps_of(padded, width):
    pieces = [padded[:, i, j : j + width] for i in range(3) for j in range(3)]
    return jnp.concatenate(pieces, axis=-1).reshape(-1, 9 * padded.shape[-1])


def per_device(latents, spatial_weight, temporal_weight, qkv_weight, out_weight, cotangent):
    frames, rows, width, chans = latents.shape
    ntok = frames * width
    n_space = lax.axis_size("space")
    n_time = lax.axis_size("tm")
    owners = n_space * n_time
    depth = chans // HEADS
    norm = 1.0 / math.sqrt(ntok * n_space * n_time)
    here = lax.axis_index("space")
    core, line = here % 2, here // GROUP
    half = chans // 2
    share = 16 * chans // (2 * owners)

    x = latents.reshape(frames, width, chans)
    cot = cotangent.reshape(frames, width, chans)
    act = jax.nn.silu(x.astype(F32)).astype(BF)
    above, below = neighbours(act)
    pre = matmul(taps_of(side_pad(jnp.stack([above, act, below], axis=1)), width), fetch(spatial_weight))
    pre = pre.reshape(frames, width, chans)
    bact = jax.nn.silu(pre).astype(BF)
    bext = jnp.concatenate([shift(bact, "tm", 1), bact], axis=0)
    resid, rres, items = proj(x, bext, cot, temporal_weight, qkv_weight, out_weight)
    items = items.reshape(frames * HEADS, width, 4 * depth)
    items = lax.all_to_all(items, "space", 0, 0, tiled=True)

    early = pick(act, jnp.where(here % GROUP == 0, above, below), share)
    chalf = cot.reshape(frames, width, 2, half).transpose(2, 0, 1, 3)
    cpair = (pick_one(chalf, core), swap(pick_one(chalf, 1 - core)))
    rother, bother = swap(rres), swap(bext)
    early, cpair, rother, bother, items = lax.optimization_barrier((early, cpair, rother, bother, items))
    early = exchange(early)
    outs = attn(items.reshape(n_space * width, 4 * depth)).reshape(n_space, width, 4 * depth)
    outs, early, rother, bother = lax.optimization_barrier((outs, early, rother, bother))
    outs = lax.all_to_all(outs, "space", 0, 0, tiled=True)
    aturn = turn(early, frames)
    rturn, bturn = turn_pair(rres, rother, bext, bother)
    slope = silu_slope(pre)
    outs, aturn, rturn, bturn, slope = lax.optimization_barrier((outs, aturn, rturn, bturn, slope))

    core_at = core.astype(jnp.int32).reshape(1)
    outs = outs.reshape(frames, HEADS, width, 4 * depth)
    atted, dres, dresb, mine, other = post(core_at, outs, cot, qkv_weight)
    dnext = shift(dresb, "tm", -1)
    local = local_terms(line.astype(jnp.int32).reshape(1), rturn, bturn, (atted, swap(atted)), (mine, swap(other)), cpair)
    slope, _ = lax.optimization_barrier((slope, local[0]))
    dpre, near = make_dpre(dresb, dnext, slope, temporal_weight)
    near = exchange(near)
    dabove, dbelow = neighbours(dpre)
    parts = [local[0]] + [along_y(local[by], by) for by in range(1, 4)]
    mixed = resid.reshape(ntok, chans) + matmul(atted.reshape(ntok, chans), out_weight)
    mixed = mixed.astype(BF).reshape(latents.shape)
    mixed, near = lax.optimization_barrier((mixed, near))
    terms = conv_terms(aturn, near, parts, owners, share)
    terms, dpre, dabove, dbelow = lax.optimization_barrier((terms, dpre, dabove, dbelow))
    terms = lax.all_to_all(terms, ("tm", "space"), 0, 0, tiled=True)
    grad_latents = make_grad_latents(dpre, dabove, dbelow, dres, x, spatial_weight).reshape(latents.shape)
    index = lax.axis_index("tm") * n_space + here
    which = (index < 9 * chans // (2 * share)).astype(jnp.int32).reshape(1)
    grad_weights = sum_terms(which, terms, norm, (n_time, n_space // GROUP, GROUP // 2))
    return (mixed, grad_latents, grad_weights)


def solution(mesh):
    placed = (P("tm", "space", None, None), P(), P(), P(), P(), P("tm", "space", None, None))
    return jax.shard_map(
        per_device,
        mesh=mesh,
        in_specs=placed,
        out_specs=(
            P("tm", "space", None, None),
            P("tm", "space", None, None),
            P(("tm", "space"), None),
        ),
        check_vma=False,
    )
```

```python
import functools
import math

import jax
import jax.numpy as jnp
from jax import lax
from jax.experimental import pallas as pl
from jax.experimental.pallas import tpu as pltpu
from jax.sharding import PartitionSpec as P

HEADS = 16
GROUP = 8
F32 = jnp.float32
BF = jnp.bfloat16
NT = (((1,), (1,)), ((), ()))

def dot_nt(left, right):
    return lax.dot_general(left, right, NT, preferred_element_type=F32)


def proj_kernel(x_ref, bext_ref, cot_ref, tw_ref, qw_ref, ow_ref, resid_ref, rres_ref, items_ref):
    frames, width, chans = x_ref.shape
    d = chans // HEADS
    for f in range(frames):
        acc = x_ref[f].astype(F32)
        for k in range(3):
            tap = tw_ref[k * chans : (k + 1) * chans, :]
            acc = acc + jnp.dot(bext_ref[f + k], tap, preferred_element_type=F32)
        resid_ref[f] = acc
        rounded = acc.astype(BF)
        rres_ref[f] = rounded
        qkv = jnp.dot(rounded, qw_ref[...], preferred_element_type=F32)
        dattn = dot_nt(cot_ref[f], ow_ref[...])
        for h in range(HEADS):
            parts = [qkv[:, p * chans + h * d : p * chans + (h + 1) * d] for p in range(3)]
            parts.append(dattn[:, h * d : (h + 1) * d])
            items_ref[f, h] = jnp.concatenate(parts, axis=1).astype(BF)


def proj(x, bext, cot, tw, qw, ow):
    frames, width, chans = x.shape
    return pl.pallas_call(
        proj_kernel,
        out_shape=(
            pltpu.HBM((frames, width, chans), F32),
            jax.ShapeDtypeStruct((frames, width, chans), BF),
            jax.ShapeDtypeStruct((frames, HEADS, width, 4 * chans // HEADS), BF),
        ),
        compiler_params=pltpu.CompilerParams(vmem_limit_bytes=32 << 20),
        cost_estimate=pl.CostEstimate(flops=10**9 * 2, bytes_accessed=6 << 20, transcendentals=0),
    )(x, bext, cot, tw, qw, ow)


def post_kernel(
    core_ref, z_ref, cot_ref, qw_hbm, attn_ref, dres_hbm, dresb_ref, mine_hbm, other_ref, qw_ref, dres_ref, mine_ref, sems
):
    frames, width, chans = cot_ref.shape
    d = chans // HEADS
    half = chans // 2
    weight = pltpu.make_async_copy(qw_hbm, qw_ref, sems.at[0])
    weight.start()
    all_parts = []
    for f in range(frames):
        heads = [z_ref[f, h].astype(F32) for h in range(HEADS)]
        parts = [jnp.concatenate([z[:, p * d : (p + 1) * d] for z in heads], axis=1).astype(BF) for p in range(4)]
        attn_ref[f] = parts[0]
        all_parts.append(parts[1:])
    weight.wait()
    for f in range(frames):
        dres = cot_ref[f].astype(F32)
        for p in range(3):
            dres = dres + dot_nt(all_parts[f][p], qw_ref[:, p * chans : (p + 1) * chans])
        dres_ref[f] = dres
        dresb = dres.astype(BF)
        dresb_ref[f] = dresb
        all_parts[f].append(dresb)
    sent = pltpu.make_async_copy(dres_ref, dres_hbm, sems.at[1])
    sent.start()

    def store(first, second):
        for f in range(frames):
            for at, part in enumerate(all_parts[f]):
                for out, c in ((first, 0), (second, 1)):
                    out[f, :, at * half : (at + 1) * half] = part[:, c * half : (c + 1) * half]

    @pl.when(core_ref[0] == 0)
    def _():
        store(mine_ref, other_ref)

    @pl.when(core_ref[0] == 1)
    def _():
        store(other_ref, mine_ref)

    kept = pltpu.make_async_copy(mine_ref, mine_hbm, sems.at[2])
    kept.start()
    sent.wait()
    kept.wait()


def post(core, z, cot, qw):
    frames, width, chans = cot.shape
    vmem, hbm = pl.BlockSpec(memory_space=pltpu.VMEM), pl.BlockSpec(memory_space=pltpu.HBM)
    return pl.pallas_call(
        post_kernel,
        out_shape=(
            jax.ShapeDtypeStruct((frames, width, chans), BF),
            pltpu.HBM((frames, width, chans), F32),
            jax.ShapeDtypeStruct((frames, width, chans), BF),
            pltpu.HBM((frames, width, 2 * chans), BF),
            jax.ShapeDtypeStruct((frames, width, 2 * chans), BF),
        ),
        in_specs=[pl.BlockSpec(memory_space=pltpu.SMEM), vmem, vmem, hbm],
        out_specs=(vmem, hbm, vmem, hbm, vmem),
        scratch_shapes=[
            pltpu.VMEM(qw.shape, BF),
            pltpu.VMEM((frames, width, chans), F32),
            pltpu.VMEM((frames, width, 2 * chans), BF),
            pltpu.SemaphoreType.DMA((3,)),
        ],
        compiler_params=pltpu.CompilerParams(vmem_limit_bytes=32 << 20),
        cost_estimate=pl.CostEstimate(flops=10**9, bytes_accessed=6 << 20, transcendentals=0),
    )(core, z, cot, pltpu.with_memory_space_constraint(qw, pltpu.HBM))


def fetch_kernel(w_ref, out_ref):
    out_ref[...] = w_ref[...]


def fetch(w):
    return pl.pallas_call(
        fetch_kernel,
        out_shape=jax.ShapeDtypeStruct(w.shape, w.dtype),
        compiler_params=pltpu.CompilerParams(vmem_limit_bytes=24 << 20),
        cost_estimate=pl.CostEstimate(flops=10**6, bytes_accessed=10 << 20, transcendentals=0),
    )(w)


def attn_kernel(scale, tq, ck, un, x_ref, o_ref, a_ref, kt_ref, vt_ref, s_ref, e_ref, acc_ref):
    tok = x_ref.shape[0]
    step = pl.program_id(0)
    nck = tok // ck
    d = 32
    @pl.when(step == 0)
    def _():
        k = x_ref[:, d:2*d]
        v = x_ref[:, 2*d:3*d]
        lane = lax.broadcasted_iota(jnp.int32, (tok, d), 1)
        ones = jnp.where(lane < 3, 1.0, 0.0).astype(BF)
        a_ref[...] = jnp.concatenate([k, k, v, ones], axis=1)
        kt_ref[...] = k.astype(F32).T.astype(BF)
        vt_ref[...] = jnp.concatenate([v, ones], axis=1).astype(F32).T[: d + 16].astype(BF)
        acc_ref[...] = jnp.zeros_like(acc_ref)
    rows = pl.ds(pl.multiple_of(step * tq, tq), tq)
    xb = x_ref[rows, :]
    q = xb[:, 0:d].astype(F32)
    do = xb[:, 3*d:4*d].astype(F32)
    zeros = jnp.zeros((tq, 2*d), BF)
    def split(z):
        hi = z.astype(BF)
        lo = (z - hi.astype(F32)).astype(BF)
        return hi, lo
    qh, ql = split(q * (scale * math.log2(math.e)))
    wq = jnp.concatenate([qh, ql, zeros], axis=1)
    def p1(i, m):
        r = pl.ds(pl.multiple_of(i * ck, ck), ck)
        s = lax.dot_general(a_ref[r, :], wq, NT, preferred_element_type=F32)
        s_ref[r, :] = s
        return jnp.maximum(m, jnp.max(s.reshape(ck // 8, 8, tq), axis=0))
    m = lax.fori_loop(0, nck, p1, jnp.full((8, tq), -jnp.inf, F32), unroll=un)
    m = jnp.max(m, axis=0, keepdims=True)
    def p2(i, o):
        r = pl.ds(pl.multiple_of(i * ck, ck), ck)
        e = jnp.exp2(s_ref[r, :] - m)
        s_ref[r, :] = e
        eb = e.astype(BF)
        e_ref[r, :] = eb
        return o + jnp.dot(vt_ref[:, r], eb, preferred_element_type=F32)
    o = lax.fori_loop(0, nck, p2, jnp.zeros((d + 16, tq), F32), unroll=un)
    inv = 1.0 / o[d:d+1, :]
    ot = o[:d] * inv
    ob = ot.T
    delta = jnp.sum(ob * do, axis=1, keepdims=True)
    invc = jnp.broadcast_to(inv, (8, tq)).T[:, 0:1]
    dh = (-delta).astype(BF); dr = -delta - dh.astype(F32)
    dm = dr.astype(BF); dl = (dr - dm.astype(F32)).astype(BF)
    lane = lax.broadcasted_iota(jnp.int32, (tq, d), 1)
    dd = jnp.where(lane == 0, dh.astype(F32), jnp.where(lane == 1, dm.astype(F32), jnp.where(lane == 2, dl.astype(F32), 0.0))).astype(BF)
    wd = jnp.concatenate([zeros, xb[:, 3*d:], dd], axis=1)
    gh, gl = split(do * invc)
    rh, rl = split(q * (invc * scale))
    none = zeros[:, :d]
    we = jnp.concatenate([none, gl, none, gh], axis=1)
    ws = jnp.concatenate([rl, none, rh, none], axis=1)
    def p3(i, dq):
        r = pl.ds(pl.multiple_of(i * ck, ck), ck)
        dp = lax.dot_general(a_ref[r, :], wd, NT, preferred_element_type=F32)
        ds = (s_ref[r, :] * dp).astype(BF)
        acc_ref[r, :] += (jnp.dot(ds, ws, preferred_element_type=F32)
                          + jnp.dot(e_ref[r, :], we, preferred_element_type=F32))
        return dq + jnp.dot(kt_ref[:, r], ds, preferred_element_type=F32)
    dq = lax.fori_loop(0, nck, p3, jnp.zeros((d, tq), F32), unroll=un)
    dq = dq * (inv * scale)
    o_ref[rows, 0:2*d] = jnp.concatenate([ot, dq], axis=0).T.astype(BF)
    @pl.when(step == pl.num_programs(0) - 1)
    def _():
        acc = acc_ref[...]
        acc = acc + pltpu.roll(acc, 2*d, 1)
        o_ref[:, 2*d:] = acc[:, 2*d:].astype(BF)

def attn(x, tq=768, ck=3840, un=1):
    tok = x.shape[0]
    return pl.pallas_call(
        functools.partial(attn_kernel, 1.0/math.sqrt(32), tq, ck, un),
        grid=(tok // tq,),
        in_specs=[pl.BlockSpec((tok, 128), lambda i: (0, 0))],
        out_specs=pl.BlockSpec((tok, 128), lambda i: (0, 0)),
        out_shape=pltpu.HBM((tok, 128), BF),
        scratch_shapes=[pltpu.VMEM((tok, 128), BF), pltpu.VMEM((32, tok), BF), pltpu.VMEM((48, tok), BF),
                        pltpu.VMEM((tok, tq), F32), pltpu.VMEM((tok, tq), BF), pltpu.VMEM((tok, 128), F32)],
        compiler_params=pltpu.CompilerParams(vmem_limit_bytes=48 << 20),
        cost_estimate=pl.CostEstimate(flops=6*2*tok*tok*128, bytes_accessed=4*tok*128, transcendentals=tok*tok),
    )(x)


LANES = 128
CALL = functools.partial(pltpu.CompilerParams, vmem_limit_bytes=40 << 20)


def cost(flops, moved):
    return pl.CostEstimate(flops=int(flops), bytes_accessed=int(moved), transcendentals=0)


def padded(plane):
    width, chans = plane.shape
    return jnp.concatenate([plane.astype(F32), jnp.zeros((LANES - width, chans), F32)], axis=0)


def pick_kernel(rows, act_ref, outer_ref, out_ref):
    group = out_ref.shape[0]
    frames, width, chans = act_ref.shape
    for f in range(frames):
        for at, src in ((f, act_ref), (frames + f, outer_ref)):
            plane = src[f].astype(F32)
            for c in range(2):
                parts = [plane[:, b + c * rows : b + (c + 1) * rows] for b in range(0, chans, 2 * rows)]
                part = jnp.concatenate(parts, axis=1).astype(BF)
                for x in range(group // 2):
                    out_ref[2 * x + c, at] = part


def pick(act, outer, rows):
    frames, width, chans = act.shape
    return pl.pallas_call(
        functools.partial(pick_kernel, rows),
        out_shape=jax.ShapeDtypeStruct((GROUP, 2 * frames, width, chans // 2), BF),
        compiler_params=CALL(),
        cost_estimate=cost(1e8, 3 << 20),
    )(act, outer)


def turn_kernel(r_ref, at_ref):
    group = r_ref.shape[0]
    frames = at_ref.shape[1]
    for f in range(frames):
        for row in range(group + 2):
            if row == 0:
                plane = r_ref[0, frames + f]
            elif row == group + 1:
                plane = r_ref[group - 1, frames + f]
            else:
                plane = r_ref[row - 1, f]
            tile = padded(plane).T
            cols = slice(row * LANES, (row + 1) * LANES)
            at_ref[0, f, :, cols] = pltpu.roll(tile, 1, 1).astype(BF)
            at_ref[1, f, :, cols] = tile.astype(BF)
            at_ref[2, f, :, cols] = pltpu.roll(tile, LANES - 1, 1).astype(BF)


def turn(r, frames):
    group, _, _, chans = r.shape
    return pl.pallas_call(
        turn_kernel,
        out_shape=pltpu.HBM((3, frames, chans, (group + 2) * LANES), BF),
        compiler_params=CALL(),
        cost_estimate=cost(1e9, 6 << 20),
    )(r)


def turn_pair_kernel(*refs):
    ins, outs = refs[:4], refs[4:]
    for own, other, out in ((ins[0], ins[1], outs[0]), (ins[2], ins[3], outs[1])):
        count = own.shape[0]
        for d, src in enumerate((own, other)):
            for f in range(count):
                at = (d * count + f) * LANES
                out[:, at : at + LANES] = padded(src[f]).T.astype(BF)


def turn_pair(own_r, other_r, own_b, other_b):
    chans = own_r.shape[-1]
    return pl.pallas_call(
        turn_pair_kernel,
        out_shape=tuple(
            pltpu.HBM((chans, 2 * x.shape[0] * LANES), BF) for x in (own_r, own_b)
        ),
        compiler_params=CALL(),
        cost_estimate=cost(1e9, 4 << 20),
    )(own_r, other_r, own_b, other_b)


def local_terms_kernel(line_ref, a0_ref, a1_ref, p1_ref, *refs):
    far, outs, scratch = refs[:5], refs[5:9], refs[9:]
    near, (at_ref, pay_ref, cot_ref, mix_ref, out_ref, sems) = scratch[:5], scratch[5:]
    rt_ref, bt_ref, p0_ref, c0_ref, c1_ref = near
    copies = [pltpu.make_async_copy(src, dst, sems.at[k]) for k, (src, dst) in enumerate(zip(far, near))]
    for copy in copies:
        copy.start()
    for copy in copies:
        copy.wait()
    frames, width, chans = a0_ref.shape
    half = chans // 2
    for d, (a, p, c) in enumerate(((a0_ref, p0_ref, c0_ref), (a1_ref, p1_ref, c1_ref))):
        for f in range(frames):
            at = (d * frames + f) * LANES
            at_ref[:, at : at + LANES] = padded(a[f]).T.astype(BF)
            pay_ref[at : at + LANES, :] = padded(p[f]).astype(BF)
            cot_ref[at : at + LANES, :] = padded(c[f]).astype(BF)
    parts, _, rows, _ = out_ref.shape
    block = parts * rows

    def put(first, value, lane=0):
        for n in range(value.shape[0] // block):
            for y in range(parts):
                at = n * block + y * rows
                out_ref[y, first + n, :, lane : lane + value.shape[1]] = value[at : at + rows].astype(BF)

    for k in range(3):
        acc = jnp.zeros((chans, half), F32)
        for d in range(2):
            left = bt_ref[:, (2 * d * frames + k) * LANES : (2 * d * frames + k + frames) * LANES]
            right = pay_ref[d * frames * LANES : (d + 1) * frames * LANES, 3 * half :]
            acc = acc + jnp.dot(left, right, preferred_element_type=F32)
        put(k * chans // block, acc)
    for p in range(3):
        right = pay_ref[:, p * half : (p + 1) * half]
        for lane in range(0, half, LANES):
            value = jnp.dot(rt_ref[...], right[:, lane : lane + LANES], preferred_element_type=F32)
            mix_ref[lane // LANES, pl.ds(p, chans, stride=3), :] = value
    for lane in range(0, half, LANES):
        put(3 * chans // block, mix_ref[lane // LANES], lane)
    put(6 * chans // block, jnp.dot(at_ref[...], cot_ref[...], preferred_element_type=F32))
    for k, out in enumerate(outs):
        out[...] = out_ref[lax.rem(line_ref[0] + k, parts)]


def local_terms(line, rt, bt, atted, pay, cot):
    frames, width, chans = atted[0].shape
    half = chans // 2
    span = 2 * frames * LANES
    piece = (7 * chans // 64, 16, half)
    far = (rt, bt, pay[0], cot[0], cot[1])
    return pl.pallas_call(
        local_terms_kernel,
        out_shape=(pltpu.HBM(piece, BF),) + (jax.ShapeDtypeStruct(piece, BF),) * 3,
        in_specs=[pl.BlockSpec(memory_space=pltpu.SMEM)]
        + [pl.BlockSpec(memory_space=pltpu.VMEM)] * 3
        + [pl.BlockSpec(memory_space=pltpu.HBM)] * 5,
        scratch_shapes=[pltpu.VMEM(x.shape, BF) for x in far]
        + [
            pltpu.VMEM((chans, span), BF),
            pltpu.VMEM((span, 4 * half), BF),
            pltpu.VMEM((span, half), BF),
            pltpu.VMEM((half // LANES, 3 * chans, LANES), F32),
            pltpu.VMEM((4,) + piece, BF),
            pltpu.SemaphoreType.DMA((5,)),
        ],
        compiler_params=CALL(),
        cost_estimate=cost(2e9, 10 << 20),
    )(line, *atted, pay[1], *[pltpu.with_memory_space_constraint(v, pltpu.HBM) for v in far])


def conv_terms_kernel(at_ref, dpre_ref, *refs):
    parts, (out_ref, dp_ref, acc_ref, part_ref, sems) = refs[:4], refs[4:]
    step = pl.program_id(0)
    group, _, width, cols = dpre_ref.shape
    shifts, _, chans, _ = at_ref.shape
    rows = out_ref.shape[1]
    blocks = chans // rows
    copies = [pltpu.make_async_copy(src, part_ref.at[k], sems.at[k]) for k, src in enumerate(parts)]

    @pl.when(step == 0)
    def _():
        for copy in copies:
            copy.start()

    for row in range(group):
        dp_ref[row * LANES : (row + 1) * LANES, :] = padded(dpre_ref[row, 0]).astype(BF)
    span = group * LANES

    def product(i):
        left = at_ref[:, 0, :, i * LANES : i * LANES + span].reshape(shifts * chans, span)
        return jnp.dot(left, dp_ref[...], preferred_element_type=F32)

    @pl.when(step == 0)
    def _():
        for i in range(3):
            acc_ref[i] = product(i)

    @pl.when(step == 1)
    def _():
        for i in range(3):
            value = (acc_ref[i] + product(i)).astype(BF)
            for b in range(shifts * blocks):
                out_ref[i * shifts * blocks + b] = value[b * rows : (b + 1) * rows]
        for copy in copies:
            copy.wait()
        for n in range(part_ref.shape[1]):
            value = part_ref[0, n].astype(F32)
            for k in range(1, 4):
                value = value + part_ref[k, n].astype(F32)
            value = value.astype(BF)
            out_ref[3 * shifts * blocks + n] = jnp.concatenate([value[:, :cols], value[:, cols:]], axis=0)


def conv_terms(at, dpre, parts, owners, rows):
    group, frames, width, cols = dpre.shape
    shifts, _, chans, lanes = at.shape
    assert frames == 2
    return pl.pallas_call(
        conv_terms_kernel,
        grid=(frames,),
        in_specs=[
            pl.BlockSpec((shifts, 1, chans, lanes), lambda f: (0, f, 0, 0)),
            pl.BlockSpec((group, 1, width, cols), lambda f: (0, f, 0, 0)),
        ]
        + [pl.BlockSpec(memory_space=pl.ANY)] * 4,
        out_specs=pl.BlockSpec((owners, rows, cols), lambda f: (0, 0, 0)),
        out_shape=jax.ShapeDtypeStruct((owners, rows, cols), BF),
        scratch_shapes=[
            pltpu.VMEM((group * LANES, cols), BF),
            pltpu.VMEM((3, shifts * chans, cols), F32),
            pltpu.VMEM((4,) + parts[0].shape, BF),
            pltpu.SemaphoreType.DMA((4,)),
        ],
        compiler_params=pltpu.CompilerParams(vmem_limit_bytes=60 << 20),
        cost_estimate=cost(2e9, 10 << 20),
    )(at, dpre, *parts)


def sum_kernel(norm, dims, which_ref, terms_ref, out_ref):
    times, ys, xs = dims
    rows, cols = terms_ref.shape[1:]

    @pl.when(which_ref[0] == 1)
    def _():
        for x in range(xs):
            for c in range(2):
                acc = jnp.zeros((rows, cols), F32)
                for t in range(times):
                    for y in range(ys):
                        acc = acc + terms_ref[((t * ys + y) * xs + x) * 2 + c].astype(F32)
                out_ref[c * rows : (c + 1) * rows, x * cols : (x + 1) * cols] = acc * norm

    @pl.when(which_ref[0] == 0)
    def _():
        part = rows // 2
        for y in range(ys):
            for c in range(2):
                acc = jnp.zeros((rows, cols), F32)
                for t in range(times):
                    for x in range(xs):
                        acc = acc + terms_ref[((t * ys + y) * xs + x) * 2 + c].astype(F32)
                acc = acc * norm
                for h in range(2):
                    at = (2 * c + h) * cols
                    out_ref[y * part : (y + 1) * part, at : at + cols] = acc[h * part : (h + 1) * part]


def sum_terms(which, terms, norm, dims):
    owners, rows, cols = terms.shape
    return pl.pallas_call(
        functools.partial(sum_kernel, norm, dims),
        out_shape=jax.ShapeDtypeStruct((2 * rows, 4 * cols), F32),
        in_specs=[pl.BlockSpec(memory_space=pltpu.SMEM), pl.BlockSpec(memory_space=pltpu.VMEM)],
        compiler_params=CALL(),
        cost_estimate=cost(1e7, 1 << 20),
    )(which, terms)


def dpre_kernel(own_ref, next_ref, slope_ref, tw_ref, dpre_ref, near_ref):
    frames, width, chans = own_ref.shape
    group, _, _, cols = near_ref.shape
    ext = [own_ref[f] for f in range(frames)] + [next_ref[f] for f in range(frames)]
    for f in range(frames):
        acc = jnp.zeros((width, chans), F32)
        for k in range(3):
            acc = acc + dot_nt(ext[f + 2 - k], tw_ref[k * chans : (k + 1) * chans, :])
        value = (acc * slope_ref[f]).astype(BF)
        dpre_ref[f] = value
        for e in range(group):
            near_ref[e, f] = value[:, (e // 2) * cols : (e // 2 + 1) * cols]


def make_dpre(own, nxt, slope, tw):
    frames, width, chans = own.shape
    return pl.pallas_call(
        dpre_kernel,
        out_shape=(
            pltpu.HBM((frames, width, chans), BF),
            jax.ShapeDtypeStruct((GROUP, frames, width, 2 * chans // GROUP), BF),
        ),
        compiler_params=CALL(),
        cost_estimate=cost(5e8, 3 << 20),
    )(own, nxt, slope, tw)


def dact_kernel(mid_ref, above_ref, below_ref, dres_ref, x_ref, sw_ref, out_ref):
    frames, width, chans = mid_ref.shape
    line = lax.broadcasted_iota(jnp.int32, (width, chans), 0)
    for f in range(frames):
        acc = jnp.zeros((width, chans), F32)
        for i, src in enumerate((below_ref, mid_ref, above_ref)):
            plane = src[f]
            wide = plane.astype(F32)
            right = jnp.where(line == width - 1, 0.0, pltpu.roll(wide, width - 1, 0)).astype(BF)
            left = jnp.where(line == 0, 0.0, pltpu.roll(wide, 1, 0)).astype(BF)
            for j, value in enumerate((right, plane, left)):
                tap = 3 * i + j
                acc = acc + dot_nt(value, sw_ref[tap * chans : (tap + 1) * chans, :])
        x = x_ref[f].astype(F32)
        sigma = 1.0 / (1.0 + jnp.exp(-x))
        slope = sigma * (1.0 + x * (1.0 - sigma))
        out_ref[f] = (dres_ref[f] + acc * slope).astype(BF)


def make_grad_latents(mid, above, below, dres, x, sw):
    return pl.pallas_call(
        dact_kernel,
        out_shape=jax.ShapeDtypeStruct(mid.shape, BF),
        compiler_params=CALL(),
        cost_estimate=cost(2e9, 8 << 20),
    )(mid, above, below, dres, x, sw)


def silu_slope(value):
    sigma = jax.nn.sigmoid(value)
    return sigma * (1.0 + value * (1.0 - sigma))


def matmul(left, right):
    return jnp.dot(left, right, preferred_element_type=F32)


def shift(x, axis, by):
    count = lax.axis_size(axis)
    pairs = [(i, i + by) for i in range(count) if 0 <= i + by < count]
    return lax.ppermute(x, axis, pairs)


def swap(x):
    count = lax.axis_size("space")
    return lax.ppermute(x, "space", [(i, i ^ 1) for i in range(count)])


def neighbours(field):
    return shift(field, "space", 1), shift(field, "space", -1)


def exchange(x):
    count = lax.axis_size("space")
    groups = [list(range(at, at + GROUP)) for at in range(0, count, GROUP)]
    return lax.all_to_all(x, "space", 0, 0, axis_index_groups=groups, tiled=True)


def along_y(x, by):
    count = lax.axis_size("space")
    return lax.ppermute(x, "space", [(i, (i + by * GROUP) % count) for i in range(count)])


def pick_one(x, index):
    return lax.dynamic_index_in_dim(x, index, 0, keepdims=False)


def side_pad(field):
    return jnp.pad(field, ((0, 0), (0, 0), (1, 1), (0, 0)))


def taps_of(padded, width):
    pieces = [padded[:, i, j : j + width] for i in range(3) for j in range(3)]
    return jnp.concatenate(pieces, axis=-1).reshape(-1, 9 * padded.shape[-1])


def per_device(latents, spatial_weight, temporal_weight, qkv_weight, out_weight, cotangent):
    frames, rows, width, chans = latents.shape
    ntok = frames * width
    n_space = lax.axis_size("space")
    n_time = lax.axis_size("tm")
    owners = n_space * n_time
    depth = chans // HEADS
    norm = 1.0 / math.sqrt(ntok * n_space * n_time)
    here = lax.axis_index("space")
    core, line = here % 2, here // GROUP
    half = chans // 2
    share = 16 * chans // (2 * owners)

    x = latents.reshape(frames, width, chans)
    cot = cotangent.reshape(frames, width, chans)
    act = jax.nn.silu(x.astype(F32)).astype(BF)
    above, below = neighbours(act)
    pre = matmul(taps_of(side_pad(jnp.stack([above, act, below], axis=1)), width), fetch(spatial_weight))
    pre = pre.reshape(frames, width, chans)
    bact = jax.nn.silu(pre).astype(BF)
    bext = jnp.concatenate([shift(bact, "tm", 1), bact], axis=0)
    resid, rres, items = proj(x, bext, cot, temporal_weight, qkv_weight, out_weight)
    items = items.reshape(frames * HEADS, width, 4 * depth)
    items = lax.all_to_all(items, "space", 0, 0, tiled=True)

    early = pick(act, jnp.where(here % GROUP == 0, above, below), share)
    chalf = cot.reshape(frames, width, 2, half).transpose(2, 0, 1, 3)
    cpair = (pick_one(chalf, core), swap(pick_one(chalf, 1 - core)))
    rother, bother = swap(rres), swap(bext)
    early, cpair, rother, bother, items = lax.optimization_barrier((early, cpair, rother, bother, items))
    early = exchange(early)
    outs = attn(items.reshape(n_space * width, 4 * depth)).reshape(n_space, width, 4 * depth)
    outs, early, rother, bother = lax.optimization_barrier((outs, early, rother, bother))
    outs = lax.all_to_all(outs, "space", 0, 0, tiled=True)
    aturn = turn(early, frames)
    rturn, bturn = turn_pair(rres, rother, bext, bother)
    slope = silu_slope(pre)
    outs, aturn, rturn, bturn, slope = lax.optimization_barrier((outs, aturn, rturn, bturn, slope))

    core_at = core.astype(jnp.int32).reshape(1)
    outs = outs.reshape(frames, HEADS, width, 4 * depth)
    atted, dres, dresb, mine, other = post(core_at, outs, cot, qkv_weight)
    dnext = shift(dresb, "tm", -1)
    local = local_terms(line.astype(jnp.int32).reshape(1), rturn, bturn, (atted, swap(atted)), (mine, swap(other)), cpair)
    slope, _ = lax.optimization_barrier((slope, local[0]))
    dpre, near = make_dpre(dresb, dnext, slope, temporal_weight)
    near = exchange(near)
    dabove, dbelow = neighbours(dpre)
    parts = [local[0]] + [along_y(local[by], by) for by in range(1, 4)]
    mixed = resid.reshape(ntok, chans) + matmul(atted.reshape(ntok, chans), out_weight)
    mixed = mixed.astype(BF).reshape(latents.shape)
    mixed, near = lax.optimization_barrier((mixed, near))
    terms = conv_terms(aturn, near, parts, owners, share)
    terms, dpre, dabove, dbelow = lax.optimization_barrier((terms, dpre, dabove, dbelow))
    terms = lax.all_to_all(terms, ("tm", "space"), 0, 0, tiled=True)
    grad_latents = make_grad_latents(dpre, dabove, dbelow, dres, x, spatial_weight).reshape(latents.shape)
    index = lax.axis_index("tm") * n_space + here
    which = (index < 9 * chans // (2 * share)).astype(jnp.int32).reshape(1)
    grad_weights = sum_terms(which, terms, norm, (n_time, n_space // GROUP, GROUP // 2))
    return (mixed, grad_latents, grad_weights)


def solution(mesh):
    placed = (P("tm", "space", None, None), P(), P(), P(), P(), P("tm", "space", None, None))
    return jax.shard_map(
        per_device,
        mesh=mesh,
        in_specs=placed,
        out_specs=(
            P("tm", "space", None, None),
            P("tm", "space", None, None),
            P(("tm", "space"), None),
        ),
        check_vma=False,
    )
```

```python
import functools
import math

import jax
import jax.numpy as jnp
from jax import lax
from jax.experimental import pallas as pl
from jax.experimental.pallas import tpu as pltpu
from jax.sharding import PartitionSpec as P

HEADS = 16
GROUP = 8
F32 = jnp.float32
BF = jnp.bfloat16
NT = (((1,), (1,)), ((), ()))

def dot_nt(left, right):
    return lax.dot_general(left, right, NT, preferred_element_type=F32)


def own_kernel(x_ref, bact_ref, cot_ref, tw_ref, ow_ref, part_ref, dattn_ref):
    frames, width, chans = x_ref.shape
    for f in range(frames):
        acc = x_ref[f].astype(F32)
        for g in range(f + 1):
            k = g + 2 - f
            acc = acc + jnp.dot(bact_ref[g], tw_ref[k * chans : (k + 1) * chans, :], preferred_element_type=F32)
        part_ref[f] = acc
        dattn_ref[f] = dot_nt(cot_ref[f], ow_ref[...]).astype(BF)


def own_part(x, bact, cot, tw, ow):
    return pl.pallas_call(
        own_kernel,
        out_shape=(jax.ShapeDtypeStruct(x.shape, F32), jax.ShapeDtypeStruct(x.shape, BF)),
        compiler_params=pltpu.CompilerParams(vmem_limit_bytes=32 << 20),
        cost_estimate=pl.CostEstimate(flops=10**9, bytes_accessed=6 << 20, transcendentals=0),
    )(x, bact, cot, tw, ow)


def proj_kernel(part_ref, prev_ref, dattn_ref, tw_ref, qw_ref, resid_ref, rres_ref, items_ref):
    frames, width, chans = part_ref.shape
    d = chans // HEADS
    for f in range(frames):
        acc = part_ref[f]
        for k in range(frames - f):
            acc = acc + jnp.dot(prev_ref[f + k], tw_ref[k * chans : (k + 1) * chans, :], preferred_element_type=F32)
        resid_ref[f] = acc
        rounded = acc.astype(BF)
        rres_ref[f] = rounded
        qkv = jnp.dot(rounded, qw_ref[...], preferred_element_type=F32)
        dattn = dattn_ref[f].astype(F32)
        for h in range(HEADS):
            parts = [qkv[:, p * chans + h * d : p * chans + (h + 1) * d] for p in range(3)]
            parts.append(dattn[:, h * d : (h + 1) * d])
            items_ref[f, h] = jnp.concatenate(parts, axis=1).astype(BF)


def proj(part, prev, dattn, tw, qw):
    frames, width, chans = part.shape
    return pl.pallas_call(
        proj_kernel,
        out_shape=(
            pltpu.HBM((frames, width, chans), F32),
            jax.ShapeDtypeStruct((frames, width, chans), BF),
            jax.ShapeDtypeStruct((frames, HEADS, width, 4 * chans // HEADS), BF),
        ),
        compiler_params=pltpu.CompilerParams(vmem_limit_bytes=32 << 20),
        cost_estimate=pl.CostEstimate(flops=10**9, bytes_accessed=6 << 20, transcendentals=0),
    )(part, prev, dattn, tw, qw)


def post_kernel(
    core_ref, z_ref, cot_ref, qw_hbm, attn_ref, dres_hbm, dresb_ref, mine_hbm, other_ref, qw_ref, dres_ref, mine_ref, back_ref, sems
):
    frames, width, chans = cot_ref.shape
    d = chans // HEADS
    half = chans // 2
    weight = pltpu.make_async_copy(qw_hbm, qw_ref, sems.at[0])
    weight.start()
    all_parts = []
    for f in range(frames):
        heads = [z_ref[f, h].astype(F32) for h in range(HEADS)]
        parts = [jnp.concatenate([z[:, p * d : (p + 1) * d] for z in heads], axis=1).astype(BF) for p in range(4)]
        attn_ref[f] = parts[0]
        all_parts.append(parts[1:])
    def store(core, group):
        for f, p, value in group:
            for c in range(2):
                piece = value[:, c * half : (c + 1) * half]
                if c != core:
                    other_ref[f, :, p * half : (p + 1) * half] = piece
                elif p == 3:
                    back_ref[f] = piece
                else:
                    mine_ref[f, :, p * half : (p + 1) * half] = piece

    def by_core(group):
        @pl.when(core_ref[0] == 0)
        def _():
            store(0, group)

        @pl.when(core_ref[0] == 1)
        def _():
            store(1, group)

    by_core([(f, p, all_parts[f][p]) for f in range(frames) for p in range(3)])
    front, back = pl.ds(0, 3 * half), pl.ds(3 * half, half)
    kept = pltpu.make_async_copy(mine_ref, mine_hbm.at[:, :, front], sems.at[2])
    kept.start()
    weight.wait()
    rounded = []
    for f in range(frames):
        dres = cot_ref[f].astype(F32)
        for p in range(3):
            dres = dres + dot_nt(all_parts[f][p], qw_ref[:, p * chans : (p + 1) * chans])
        dres_ref[f] = dres
        rounded.append((f, 3, dres.astype(BF)))
        dresb_ref[f] = rounded[f][2]
    sent = pltpu.make_async_copy(dres_ref, dres_hbm, sems.at[1])
    sent.start()
    by_core(rounded)
    last = pltpu.make_async_copy(back_ref, mine_hbm.at[:, :, back], sems.at[3])
    last.start()
    sent.wait()
    kept.wait()
    last.wait()


def post(core, z, cot, qw):
    frames, width, chans = cot.shape
    vmem, hbm = pl.BlockSpec(memory_space=pltpu.VMEM), pl.BlockSpec(memory_space=pltpu.HBM)
    return pl.pallas_call(
        post_kernel,
        out_shape=(
            jax.ShapeDtypeStruct((frames, width, chans), BF),
            pltpu.HBM((frames, width, chans), F32),
            jax.ShapeDtypeStruct((frames, width, chans), BF),
            pltpu.HBM((frames, width, 2 * chans), BF),
            jax.ShapeDtypeStruct((frames, width, 2 * chans), BF),
        ),
        in_specs=[pl.BlockSpec(memory_space=pltpu.SMEM), vmem, vmem, hbm],
        out_specs=(vmem, hbm, vmem, hbm, vmem),
        scratch_shapes=[
            pltpu.VMEM(qw.shape, BF),
            pltpu.VMEM((frames, width, chans), F32),
            pltpu.VMEM((frames, width, 3 * chans // 2), BF),
            pltpu.VMEM((frames, width, chans // 2), BF),
            pltpu.SemaphoreType.DMA((4,)),
        ],
        compiler_params=pltpu.CompilerParams(vmem_limit_bytes=32 << 20),
        cost_estimate=pl.CostEstimate(flops=10**9, bytes_accessed=6 << 20, transcendentals=0),
    )(core, z, cot, pltpu.with_memory_space_constraint(qw, pltpu.HBM))


def fetch_kernel(w_ref, out_ref):
    out_ref[...] = w_ref[...]


def fetch(w):
    return pl.pallas_call(
        fetch_kernel,
        out_shape=jax.ShapeDtypeStruct(w.shape, w.dtype),
        compiler_params=pltpu.CompilerParams(vmem_limit_bytes=24 << 20),
        cost_estimate=pl.CostEstimate(flops=10**6, bytes_accessed=10 << 20, transcendentals=0),
    )(w)


def attn_kernel(scale, tq, ck, un, x_ref, o_ref, a_ref, kt_ref, vt_ref, s_ref, e_ref, acc_ref):
    tok = x_ref.shape[0]
    step = pl.program_id(0)
    nck = tok // ck
    d = 32
    @pl.when(step == 0)
    def _():
        k = x_ref[:, d:2*d]
        v = x_ref[:, 2*d:3*d]
        lane = lax.broadcasted_iota(jnp.int32, (tok, d), 1)
        ones = jnp.where(lane < 3, 1.0, 0.0).astype(BF)
        a_ref[...] = jnp.concatenate([k, k, v, ones], axis=1)
        kt_ref[...] = k.astype(F32).T.astype(BF)
        vt_ref[...] = jnp.concatenate([v, ones], axis=1).astype(F32).T[: d + 16].astype(BF)
        acc_ref[...] = jnp.zeros_like(acc_ref)
    rows = pl.ds(pl.multiple_of(step * tq, tq), tq)
    xb = x_ref[rows, :]
    q = xb[:, 0:d].astype(F32)
    do = xb[:, 3*d:4*d].astype(F32)
    zeros = jnp.zeros((tq, 2*d), BF)
    def split(z):
        hi = z.astype(BF)
        lo = (z - hi.astype(F32)).astype(BF)
        return hi, lo
    qh, ql = split(q * (scale * math.log2(math.e)))
    wq = jnp.concatenate([qh, ql, zeros], axis=1)
    def p1(i, m):
        r = pl.ds(pl.multiple_of(i * ck, ck), ck)
        s = lax.dot_general(a_ref[r, :], wq, NT, preferred_element_type=F32)
        s_ref[r, :] = s
        return jnp.maximum(m, jnp.max(s.reshape(ck // 8, 8, tq), axis=0))
    m = lax.fori_loop(0, nck, p1, jnp.full((8, tq), -jnp.inf, F32), unroll=un)
    m = jnp.max(m, axis=0, keepdims=True)
    def p2(i, o):
        r = pl.ds(pl.multiple_of(i * ck, ck), ck)
        e = jnp.exp2(s_ref[r, :] - m)
        s_ref[r, :] = e
        eb = e.astype(BF)
        e_ref[r, :] = eb
        return o + jnp.dot(vt_ref[:, r], eb, preferred_element_type=F32)
    o = lax.fori_loop(0, nck, p2, jnp.zeros((d + 16, tq), F32), unroll=un)
    inv = 1.0 / o[d:d+1, :]
    ot = o[:d] * inv
    ob = ot.T
    delta = jnp.sum(ob * do, axis=1, keepdims=True)
    invc = jnp.broadcast_to(inv, (8, tq)).T[:, 0:1]
    dh = (-delta).astype(BF); dr = -delta - dh.astype(F32)
    dm = dr.astype(BF); dl = (dr - dm.astype(F32)).astype(BF)
    lane = lax.broadcasted_iota(jnp.int32, (tq, d), 1)
    dd = jnp.where(lane == 0, dh.astype(F32), jnp.where(lane == 1, dm.astype(F32), jnp.where(lane == 2, dl.astype(F32), 0.0))).astype(BF)
    wd = jnp.concatenate([zeros, xb[:, 3*d:], dd], axis=1)
    gh, gl = split(do * invc)
    rh, rl = split(q * (invc * scale))
    none = zeros[:, :d]
    we = jnp.concatenate([none, gl, none, gh], axis=1)
    ws = jnp.concatenate([rl, none, rh, none], axis=1)
    def p3(i, dq):
        r = pl.ds(pl.multiple_of(i * ck, ck), ck)
        dp = lax.dot_general(a_ref[r, :], wd, NT, preferred_element_type=F32)
        ds = (s_ref[r, :] * dp).astype(BF)
        acc_ref[r, :] += (jnp.dot(ds, ws, preferred_element_type=F32)
                          + jnp.dot(e_ref[r, :], we, preferred_element_type=F32))
        return dq + jnp.dot(kt_ref[:, r], ds, preferred_element_type=F32)
    dq = lax.fori_loop(0, nck, p3, jnp.zeros((d, tq), F32), unroll=un)
    dq = dq * (inv * scale)
    o_ref[rows, 0:2*d] = jnp.concatenate([ot, dq], axis=0).T.astype(BF)
    @pl.when(step == pl.num_programs(0) - 1)
    def _():
        acc = acc_ref[...]
        acc = acc + pltpu.roll(acc, 2*d, 1)
        o_ref[:, 2*d:] = acc[:, 2*d:].astype(BF)

def attn(x, tq=768, ck=3840, un=1):
    tok = x.shape[0]
    return pl.pallas_call(
        functools.partial(attn_kernel, 1.0/math.sqrt(32), tq, ck, un),
        grid=(tok // tq,),
        in_specs=[pl.BlockSpec((tok, 128), lambda i: (0, 0))],
        out_specs=pl.BlockSpec((tok, 128), lambda i: (0, 0)),
        out_shape=pltpu.HBM((tok, 128), BF),
        scratch_shapes=[pltpu.VMEM((tok, 128), BF), pltpu.VMEM((32, tok), BF), pltpu.VMEM((48, tok), BF),
                        pltpu.VMEM((tok, tq), F32), pltpu.VMEM((tok, tq), BF), pltpu.VMEM((tok, 128), F32)],
        compiler_params=pltpu.CompilerParams(vmem_limit_bytes=48 << 20),
        cost_estimate=pl.CostEstimate(flops=6*2*tok*tok*128, bytes_accessed=4*tok*128, transcendentals=tok*tok),
    )(x)


LANES = 128
CALL = functools.partial(pltpu.CompilerParams, vmem_limit_bytes=40 << 20)


def cost(flops, moved):
    return pl.CostEstimate(flops=int(flops), bytes_accessed=int(moved), transcendentals=0)


def padded(plane):
    width, chans = plane.shape
    return jnp.concatenate([plane.astype(F32), jnp.zeros((LANES - width, chans), F32)], axis=0)


def pick_kernel(rows, act_ref, outer_ref, out_ref):
    group = out_ref.shape[0]
    frames, width, chans = act_ref.shape
    for f in range(frames):
        for at, src in ((f, act_ref), (frames + f, outer_ref)):
            plane = src[f].astype(F32)
            for c in range(2):
                parts = [plane[:, b + c * rows : b + (c + 1) * rows] for b in range(0, chans, 2 * rows)]
                part = jnp.concatenate(parts, axis=1).astype(BF)
                for x in range(group // 2):
                    out_ref[2 * x + c, at] = part


def pick(act, outer, rows):
    frames, width, chans = act.shape
    return pl.pallas_call(
        functools.partial(pick_kernel, rows),
        out_shape=jax.ShapeDtypeStruct((GROUP, 2 * frames, width, chans // 2), BF),
        compiler_params=CALL(),
        cost_estimate=cost(1e8, 3 << 20),
    )(act, outer)


def turn_kernel(r_ref, at_ref):
    group = r_ref.shape[0]
    frames = at_ref.shape[1]
    for f in range(frames):
        for row in range(group + 2):
            if row == 0:
                plane = r_ref[0, frames + f]
            elif row == group + 1:
                plane = r_ref[group - 1, frames + f]
            else:
                plane = r_ref[row - 1, f]
            tile = padded(plane).T
            cols = slice(row * LANES, (row + 1) * LANES)
            at_ref[0, f, :, cols] = pltpu.roll(tile, 1, 1).astype(BF)
            at_ref[1, f, :, cols] = tile.astype(BF)
            at_ref[2, f, :, cols] = pltpu.roll(tile, LANES - 1, 1).astype(BF)


def turn(r, frames):
    group, _, _, chans = r.shape
    return pl.pallas_call(
        turn_kernel,
        out_shape=pltpu.HBM((3, frames, chans, (group + 2) * LANES), BF),
        compiler_params=CALL(),
        cost_estimate=cost(1e9, 6 << 20),
    )(r)


def turn_pair_kernel(*refs):
    ins, outs = refs[:4], refs[4:]
    for own, other, out in ((ins[0], ins[1], outs[0]), (ins[2], ins[3], outs[1])):
        count = own.shape[0]
        for d, src in enumerate((own, other)):
            for f in range(count):
                at = (d * count + f) * LANES
                out[:, at : at + LANES] = padded(src[f]).T.astype(BF)


def turn_pair(own_r, other_r, own_b, other_b):
    chans = own_r.shape[-1]
    return pl.pallas_call(
        turn_pair_kernel,
        out_shape=tuple(
            pltpu.HBM((chans, 2 * x.shape[0] * LANES), BF) for x in (own_r, own_b)
        ),
        compiler_params=CALL(),
        cost_estimate=cost(1e9, 4 << 20),
    )(own_r, other_r, own_b, other_b)


def local_terms_kernel(line_ref, a0_ref, a1_ref, p1_ref, *refs):
    far, outs, scratch = refs[:5], refs[5:9], refs[9:]
    near, (at_ref, pay_ref, cot_ref, mix_ref, out_ref, sems) = scratch[:5], scratch[5:]
    rt_ref, bt_ref, p0_ref, c0_ref, c1_ref = near
    copies = [pltpu.make_async_copy(src, dst, sems.at[k]) for k, (src, dst) in enumerate(zip(far, near))]
    for copy in copies:
        copy.start()
    for copy in copies:
        copy.wait()
    frames, width, chans = a0_ref.shape
    half = chans // 2
    for d, (a, p, c) in enumerate(((a0_ref, p0_ref, c0_ref), (a1_ref, p1_ref, c1_ref))):
        for f in range(frames):
            at = (d * frames + f) * LANES
            at_ref[:, at : at + LANES] = padded(a[f]).T.astype(BF)
            pay_ref[at : at + LANES, :] = padded(p[f]).astype(BF)
            cot_ref[at : at + LANES, :] = padded(c[f]).astype(BF)
    parts, _, rows, _ = out_ref.shape
    block = parts * rows

    def put(first, value, lane=0):
        for n in range(value.shape[0] // block):
            for y in range(parts):
                at = n * block + y * rows
                out_ref[y, first + n, :, lane : lane + value.shape[1]] = value[at : at + rows].astype(BF)

    for k in range(3):
        acc = jnp.zeros((chans, half), F32)
        for d in range(2):
            left = bt_ref[:, (2 * d * frames + k) * LANES : (2 * d * frames + k + frames) * LANES]
            right = pay_ref[d * frames * LANES : (d + 1) * frames * LANES, 3 * half :]
            acc = acc + jnp.dot(left, right, preferred_element_type=F32)
        put(k * chans // block, acc)
    for p in range(3):
        right = pay_ref[:, p * half : (p + 1) * half]
        for lane in range(0, half, LANES):
            value = jnp.dot(rt_ref[...], right[:, lane : lane + LANES], preferred_element_type=F32)
            mix_ref[lane // LANES, pl.ds(p, chans, stride=3), :] = value
    for lane in range(0, half, LANES):
        put(3 * chans // block, mix_ref[lane // LANES], lane)
    put(6 * chans // block, jnp.dot(at_ref[...], cot_ref[...], preferred_element_type=F32))
    for k, out in enumerate(outs):
        out[...] = out_ref[lax.rem(line_ref[0] + k, parts)]


def local_terms(line, rt, bt, atted, pay, cot):
    frames, width, chans = atted[0].shape
    half = chans // 2
    span = 2 * frames * LANES
    piece = (7 * chans // 64, 16, half)
    far = (rt, bt, pay[0], cot[0], cot[1])
    return pl.pallas_call(
        local_terms_kernel,
        out_shape=(pltpu.HBM(piece, BF),) + (jax.ShapeDtypeStruct(piece, BF),) * 3,
        in_specs=[pl.BlockSpec(memory_space=pltpu.SMEM)]
        + [pl.BlockSpec(memory_space=pltpu.VMEM)] * 3
        + [pl.BlockSpec(memory_space=pltpu.HBM)] * 5,
        scratch_shapes=[pltpu.VMEM(x.shape, BF) for x in far]
        + [
            pltpu.VMEM((chans, span), BF),
            pltpu.VMEM((span, 4 * half), BF),
            pltpu.VMEM((span, half), BF),
            pltpu.VMEM((half // LANES, 3 * chans, LANES), F32),
            pltpu.VMEM((4,) + piece, BF),
            pltpu.SemaphoreType.DMA((5,)),
        ],
        compiler_params=CALL(),
        cost_estimate=cost(2e9, 10 << 20),
    )(line, *atted, pay[1], *[pltpu.with_memory_space_constraint(v, pltpu.HBM) for v in far])


def conv_terms_kernel(at_ref, dpre_ref, *refs):
    parts, (out_ref, dp_ref, acc_ref, part_ref, sems) = refs[:4], refs[4:]
    step = pl.program_id(0)
    group, _, width, cols = dpre_ref.shape
    shifts, _, chans, _ = at_ref.shape
    rows = out_ref.shape[1]
    blocks = chans // rows
    copies = [pltpu.make_async_copy(src, part_ref.at[k], sems.at[k]) for k, src in enumerate(parts)]

    @pl.when(step == 0)
    def _():
        for copy in copies:
            copy.start()

    for row in range(group):
        dp_ref[row * LANES : (row + 1) * LANES, :] = padded(dpre_ref[row, 0]).astype(BF)
    span = group * LANES

    def product(i):
        left = at_ref[:, 0, :, i * LANES : i * LANES + span].reshape(shifts * chans, span)
        return jnp.dot(left, dp_ref[...], preferred_element_type=F32)

    @pl.when(step == 0)
    def _():
        for i in range(3):
            acc_ref[i] = product(i)

    @pl.when(step == 1)
    def _():
        for i in range(3):
            value = (acc_ref[i] + product(i)).astype(BF)
            for b in range(shifts * blocks):
                out_ref[i * shifts * blocks + b] = value[b * rows : (b + 1) * rows]
        for copy in copies:
            copy.wait()
        for n in range(part_ref.shape[1]):
            value = part_ref[0, n].astype(F32)
            for k in range(1, 4):
                value = value + part_ref[k, n].astype(F32)
            value = value.astype(BF)
            out_ref[3 * shifts * blocks + n] = jnp.concatenate([value[:, :cols], value[:, cols:]], axis=0)


def conv_terms(at, dpre, parts, owners, rows):
    group, frames, width, cols = dpre.shape
    shifts, _, chans, lanes = at.shape
    assert frames == 2
    return pl.pallas_call(
        conv_terms_kernel,
        grid=(frames,),
        in_specs=[
            pl.BlockSpec((shifts, 1, chans, lanes), lambda f: (0, f, 0, 0)),
            pl.BlockSpec((group, 1, width, cols), lambda f: (0, f, 0, 0)),
        ]
        + [pl.BlockSpec(memory_space=pl.ANY)] * 4,
        out_specs=pl.BlockSpec((owners, rows, cols), lambda f: (0, 0, 0)),
        out_shape=jax.ShapeDtypeStruct((owners, rows, cols), BF),
        scratch_shapes=[
            pltpu.VMEM((group * LANES, cols), BF),
            pltpu.VMEM((3, shifts * chans, cols), F32),
            pltpu.VMEM((4,) + parts[0].shape, BF),
            pltpu.SemaphoreType.DMA((4,)),
        ],
        compiler_params=pltpu.CompilerParams(vmem_limit_bytes=60 << 20),
        cost_estimate=cost(2e9, 10 << 20),
    )(at, dpre, *parts)


def sum_kernel(norm, dims, which_ref, terms_ref, out_ref):
    times, ys, xs = dims
    rows, cols = terms_ref.shape[1:]

    @pl.when(which_ref[0] == 1)
    def _():
        for x in range(xs):
            for c in range(2):
                acc = jnp.zeros((rows, cols), F32)
                for t in range(times):
                    for y in range(ys):
                        acc = acc + terms_ref[((t * ys + y) * xs + x) * 2 + c].astype(F32)
                out_ref[c * rows : (c + 1) * rows, x * cols : (x + 1) * cols] = acc * norm

    @pl.when(which_ref[0] == 0)
    def _():
        part = rows // 2
        for y in range(ys):
            for c in range(2):
                acc = jnp.zeros((rows, cols), F32)
                for t in range(times):
                    for x in range(xs):
                        acc = acc + terms_ref[((t * ys + y) * xs + x) * 2 + c].astype(F32)
                acc = acc * norm
                for h in range(2):
                    at = (2 * c + h) * cols
                    out_ref[y * part : (y + 1) * part, at : at + cols] = acc[h * part : (h + 1) * part]


def sum_terms(which, terms, norm, dims):
    owners, rows, cols = terms.shape
    return pl.pallas_call(
        functools.partial(sum_kernel, norm, dims),
        out_shape=jax.ShapeDtypeStruct((2 * rows, 4 * cols), F32),
        in_specs=[pl.BlockSpec(memory_space=pltpu.SMEM), pl.BlockSpec(memory_space=pltpu.VMEM)],
        compiler_params=CALL(),
        cost_estimate=cost(1e7, 1 << 20),
    )(which, terms)


def dpre_kernel(own_ref, next_ref, slope_ref, tw_ref, dpre_ref, near_ref):
    frames, width, chans = own_ref.shape
    group, _, _, cols = near_ref.shape
    ext = [own_ref[f] for f in range(frames)] + [next_ref[f] for f in range(frames)]
    for f in range(frames):
        acc = jnp.zeros((width, chans), F32)
        for k in range(3):
            acc = acc + dot_nt(ext[f + 2 - k], tw_ref[k * chans : (k + 1) * chans, :])
        value = (acc * slope_ref[f]).astype(BF)
        dpre_ref[f] = value
        for e in range(group):
            near_ref[e, f] = value[:, (e // 2) * cols : (e // 2 + 1) * cols]


def make_dpre(own, nxt, slope, tw):
    frames, width, chans = own.shape
    return pl.pallas_call(
        dpre_kernel,
        out_shape=(
            pltpu.HBM((frames, width, chans), BF),
            jax.ShapeDtypeStruct((GROUP, frames, width, 2 * chans // GROUP), BF),
        ),
        compiler_params=CALL(),
        cost_estimate=cost(5e8, 3 << 20),
    )(own, nxt, slope, tw)


def dact_kernel(mid_ref, above_ref, below_ref, dres_ref, x_ref, sw_ref, out_ref):
    frames, width, chans = mid_ref.shape
    line = lax.broadcasted_iota(jnp.int32, (width, chans), 0)
    for f in range(frames):
        acc = jnp.zeros((width, chans), F32)
        for i, src in enumerate((below_ref, mid_ref, above_ref)):
            plane = src[f]
            wide = plane.astype(F32)
            right = jnp.where(line == width - 1, 0.0, pltpu.roll(wide, width - 1, 0)).astype(BF)
            left = jnp.where(line == 0, 0.0, pltpu.roll(wide, 1, 0)).astype(BF)
            for j, value in enumerate((right, plane, left)):
                tap = 3 * i + j
                acc = acc + dot_nt(value, sw_ref[tap * chans : (tap + 1) * chans, :])
        x = x_ref[f].astype(F32)
        sigma = 1.0 / (1.0 + jnp.exp(-x))
        slope = sigma * (1.0 + x * (1.0 - sigma))
        out_ref[f] = (dres_ref[f] + acc * slope).astype(BF)


def make_grad_latents(mid, above, below, dres, x, sw):
    return pl.pallas_call(
        dact_kernel,
        out_shape=jax.ShapeDtypeStruct(mid.shape, BF),
        compiler_params=CALL(),
        cost_estimate=cost(2e9, 8 << 20),
    )(mid, above, below, dres, x, sw)


def silu_slope(value):
    sigma = jax.nn.sigmoid(value)
    return sigma * (1.0 + value * (1.0 - sigma))


def matmul(left, right):
    return jnp.dot(left, right, preferred_element_type=F32)


def shift(x, axis, by):
    count = lax.axis_size(axis)
    pairs = [(i, i + by) for i in range(count) if 0 <= i + by < count]
    return lax.ppermute(x, axis, pairs)


def swap(x):
    count = lax.axis_size("space")
    return lax.ppermute(x, "space", [(i, i ^ 1) for i in range(count)])


def neighbours(field):
    return shift(field, "space", 1), shift(field, "space", -1)


def exchange(x):
    count = lax.axis_size("space")
    groups = [list(range(at, at + GROUP)) for at in range(0, count, GROUP)]
    return lax.all_to_all(x, "space", 0, 0, axis_index_groups=groups, tiled=True)


def along_y(x, by):
    count = lax.axis_size("space")
    return lax.ppermute(x, "space", [(i, (i + by * GROUP) % count) for i in range(count)])


def pick_one(x, index):
    return lax.dynamic_index_in_dim(x, index, 0, keepdims=False)


def side_pad(field):
    return jnp.pad(field, ((0, 0), (0, 0), (1, 1), (0, 0)))


def taps_of(padded, width):
    pieces = [padded[:, i, j : j + width] for i in range(3) for j in range(3)]
    return jnp.concatenate(pieces, axis=-1).reshape(-1, 9 * padded.shape[-1])


def per_device(latents, spatial_weight, temporal_weight, qkv_weight, out_weight, cotangent):
    frames, rows, width, chans = latents.shape
    ntok = frames * width
    n_space = lax.axis_size("space")
    n_time = lax.axis_size("tm")
    owners = n_space * n_time
    depth = chans // HEADS
    norm = 1.0 / math.sqrt(ntok * n_space * n_time)
    here = lax.axis_index("space")
    core, line = here % 2, here // GROUP
    half = chans // 2
    share = 16 * chans // (2 * owners)

    x = latents.reshape(frames, width, chans)
    cot = cotangent.reshape(frames, width, chans)
    act = jax.nn.silu(x.astype(F32)).astype(BF)
    above, below = neighbours(act)
    pre = matmul(taps_of(side_pad(jnp.stack([above, act, below], axis=1)), width), fetch(spatial_weight))
    pre = pre.reshape(frames, width, chans)
    bact = jax.nn.silu(pre).astype(BF)
    prev = shift(bact, "tm", 1)
    part, dattn = own_part(x, bact, cot, temporal_weight, out_weight)
    resid, rres, items = proj(part, prev, dattn, temporal_weight, qkv_weight)
    bext = jnp.concatenate([prev, bact], axis=0)
    items = items.reshape(frames * HEADS, width, 4 * depth)
    outer = jnp.where(here % GROUP == 0, above, below)
    act, outer, late, items = lax.optimization_barrier((act, outer, cot, items))
    items = lax.all_to_all(items, "space", 0, 0, tiled=True)

    early = pick(act, outer, share)
    chalf = late.reshape(frames, width, 2, half).transpose(2, 0, 1, 3)
    cpair = (pick_one(chalf, core), swap(pick_one(chalf, 1 - core)))
    rother, bother = swap(rres), swap(bext)
    early, cpair, rother, bother, items = lax.optimization_barrier((early, cpair, rother, bother, items))
    early = exchange(early)
    outs = attn(items.reshape(n_space * width, 4 * depth)).reshape(n_space, width, 4 * depth)
    outs, early, rother, bother = lax.optimization_barrier((outs, early, rother, bother))
    outs = lax.all_to_all(outs, "space", 0, 0, tiled=True)
    aturn = turn(early, frames)
    rturn, bturn = turn_pair(rres, rother, bext, bother)
    slope = silu_slope(pre)
    outs, aturn, rturn, bturn, slope = lax.optimization_barrier((outs, aturn, rturn, bturn, slope))

    core_at = core.astype(jnp.int32).reshape(1)
    outs = outs.reshape(frames, HEADS, width, 4 * depth)
    atted, dres, dresb, mine, other = post(core_at, outs, cot, qkv_weight)
    dnext = shift(dresb, "tm", -1)
    local = local_terms(line.astype(jnp.int32).reshape(1), rturn, bturn, (atted, swap(atted)), (mine, swap(other)), cpair)
    slope, _ = lax.optimization_barrier((slope, local[0]))
    dpre, near = make_dpre(dresb, dnext, slope, temporal_weight)
    near = exchange(near)
    dabove, dbelow = neighbours(dpre)
    parts = [local[0]] + [along_y(local[by], by) for by in range(1, 4)]
    mixed = resid.reshape(ntok, chans) + matmul(atted.reshape(ntok, chans), out_weight)
    mixed = mixed.astype(BF).reshape(latents.shape)
    mixed, near = lax.optimization_barrier((mixed, near))
    terms = conv_terms(aturn, near, parts, owners, share)
    terms, dpre, dabove, dbelow = lax.optimization_barrier((terms, dpre, dabove, dbelow))
    terms = lax.all_to_all(terms, ("tm", "space"), 0, 0, tiled=True)
    grad_latents = make_grad_latents(dpre, dabove, dbelow, dres, x, spatial_weight).reshape(latents.shape)
    index = lax.axis_index("tm") * n_space + here
    which = (index < 9 * chans // (2 * share)).astype(jnp.int32).reshape(1)
    grad_weights = sum_terms(which, terms, norm, (n_time, n_space // GROUP, GROUP // 2))
    return (mixed, grad_latents, grad_weights)


def solution(mesh):
    placed = (P("tm", "space", None, None), P(), P(), P(), P(), P("tm", "space", None, None))
    return jax.shard_map(
        per_device,
        mesh=mesh,
        in_specs=placed,
        out_specs=(
            P("tm", "space", None, None),
            P("tm", "space", None, None),
            P(("tm", "space"), None),
        ),
        check_vma=False,
    )
```

```python
import functools
import math

import jax
import jax.numpy as jnp
from jax import lax
from jax.experimental import pallas as pl
from jax.experimental.pallas import tpu as pltpu
from jax.sharding import PartitionSpec as P

HEADS = 16
GROUP = 8
F32 = jnp.float32
BF = jnp.bfloat16
NT = (((1,), (1,)), ((), ()))

def dot_nt(left, right):
    return lax.dot_general(left, right, NT, preferred_element_type=F32)


def proj_kernel(x_ref, bext_ref, cot_ref, tw_ref, qw_ref, ow_ref, resid_ref, rres_ref, items_ref):
    frames, width, chans = x_ref.shape
    d = chans // HEADS
    for f in range(frames):
        acc = x_ref[f].astype(F32)
        for k in range(3):
            tap = tw_ref[k * chans : (k + 1) * chans, :]
            acc = acc + jnp.dot(bext_ref[f + k], tap, preferred_element_type=F32)
        resid_ref[f] = acc
        rounded = acc.astype(BF)
        rres_ref[f] = rounded
        qkv = jnp.dot(rounded, qw_ref[...], preferred_element_type=F32)
        dattn = dot_nt(cot_ref[f], ow_ref[...])
        for h in range(HEADS):
            parts = [qkv[:, p * chans + h * d : p * chans + (h + 1) * d] for p in range(3)]
            parts.append(dattn[:, h * d : (h + 1) * d])
            items_ref[f, h] = jnp.concatenate(parts, axis=1).astype(BF)


def proj(x, bext, cot, tw, qw, ow):
    frames, width, chans = x.shape
    return pl.pallas_call(
        proj_kernel,
        out_shape=(
            pltpu.HBM((frames, width, chans), F32),
            jax.ShapeDtypeStruct((frames, width, chans), BF),
            jax.ShapeDtypeStruct((frames, HEADS, width, 4 * chans // HEADS), BF),
        ),
        compiler_params=pltpu.CompilerParams(vmem_limit_bytes=32 << 20),
        cost_estimate=pl.CostEstimate(flops=10**9 * 2, bytes_accessed=6 << 20, transcendentals=0),
    )(x, bext, cot, tw, qw, ow)


def post_kernel(
    core_ref, z_ref, cot_ref, qw_hbm, attn_ref, dres_hbm, dresb_ref, mine_hbm, other_ref, qw_ref, dres_ref, mine_ref, sems
):
    frames, width, chans = cot_ref.shape
    d = chans // HEADS
    half = chans // 2
    weight = pltpu.make_async_copy(qw_hbm, qw_ref, sems.at[0])
    weight.start()
    all_parts = []
    for f in range(frames):
        heads = [z_ref[f, h].astype(F32) for h in range(HEADS)]
        parts = [jnp.concatenate([z[:, p * d : (p + 1) * d] for z in heads], axis=1).astype(BF) for p in range(4)]
        attn_ref[f] = parts[0]
        all_parts.append(parts[1:])
    weight.wait()
    for f in range(frames):
        dres = cot_ref[f].astype(F32)
        for p in range(3):
            dres = dres + dot_nt(all_parts[f][p], qw_ref[:, p * chans : (p + 1) * chans])
        dres_ref[f] = dres
        dresb = dres.astype(BF)
        dresb_ref[f] = dresb
        all_parts[f].append(dresb)
    sent = pltpu.make_async_copy(dres_ref, dres_hbm, sems.at[1])
    sent.start()

    def store(first, second):
        for f in range(frames):
            for at, part in enumerate(all_parts[f]):
                for out, c in ((first, 0), (second, 1)):
                    out[f, :, at * half : (at + 1) * half] = part[:, c * half : (c + 1) * half]

    @pl.when(core_ref[0] == 0)
    def _():
        store(mine_ref, other_ref)

    @pl.when(core_ref[0] == 1)
    def _():
        store(other_ref, mine_ref)

    kept = pltpu.make_async_copy(mine_ref, mine_hbm, sems.at[2])
    kept.start()
    sent.wait()
    kept.wait()


def post(core, z, cot, qw):
    frames, width, chans = cot.shape
    vmem, hbm = pl.BlockSpec(memory_space=pltpu.VMEM), pl.BlockSpec(memory_space=pltpu.HBM)
    return pl.pallas_call(
        post_kernel,
        out_shape=(
            jax.ShapeDtypeStruct((frames, width, chans), BF),
            pltpu.HBM((frames, width, chans), F32),
            jax.ShapeDtypeStruct((frames, width, chans), BF),
            pltpu.HBM((frames, width, 2 * chans), BF),
            jax.ShapeDtypeStruct((frames, width, 2 * chans), BF),
        ),
        in_specs=[pl.BlockSpec(memory_space=pltpu.SMEM), vmem, vmem, hbm],
        out_specs=(vmem, hbm, vmem, hbm, vmem),
        scratch_shapes=[
            pltpu.VMEM(qw.shape, BF),
            pltpu.VMEM((frames, width, chans), F32),
            pltpu.VMEM((frames, width, 2 * chans), BF),
            pltpu.SemaphoreType.DMA((3,)),
        ],
        compiler_params=pltpu.CompilerParams(vmem_limit_bytes=32 << 20),
        cost_estimate=pl.CostEstimate(flops=10**9, bytes_accessed=6 << 20, transcendentals=0),
    )(core, z, cot, pltpu.with_memory_space_constraint(qw, pltpu.HBM))


def fetch_kernel(w_ref, out_ref):
    out_ref[...] = w_ref[...]


def fetch(w):
    return pl.pallas_call(
        fetch_kernel,
        out_shape=jax.ShapeDtypeStruct(w.shape, w.dtype),
        compiler_params=pltpu.CompilerParams(vmem_limit_bytes=24 << 20),
        cost_estimate=pl.CostEstimate(flops=10**6, bytes_accessed=10 << 20, transcendentals=0),
    )(w)


def attn_kernel(scale, tq, ck, un, x_ref, o_ref, a_ref, kt_ref, vt_ref, s_ref, e_ref, acc_ref):
    tok = x_ref.shape[0]
    step = pl.program_id(0)
    nck = tok // ck
    d = 32
    @pl.when(step == 0)
    def _():
        k = x_ref[:, d:2*d]
        v = x_ref[:, 2*d:3*d]
        lane = lax.broadcasted_iota(jnp.int32, (tok, d), 1)
        ones = jnp.where(lane < 3, 1.0, 0.0).astype(BF)
        a_ref[...] = jnp.concatenate([k, k, v, ones], axis=1)
        kt_ref[...] = k.astype(F32).T.astype(BF)
        vt_ref[...] = jnp.concatenate([v, ones], axis=1).astype(F32).T[: d + 16].astype(BF)
        acc_ref[...] = jnp.zeros_like(acc_ref)
    rows = pl.ds(pl.multiple_of(step * tq, tq), tq)
    xb = x_ref[rows, :]
    q = xb[:, 0:d].astype(F32)
    do = xb[:, 3*d:4*d].astype(F32)
    zeros = jnp.zeros((tq, 2*d), BF)
    def split(z):
        hi = z.astype(BF)
        lo = (z - hi.astype(F32)).astype(BF)
        return hi, lo
    qh, ql = split(q * (scale * math.log2(math.e)))
    wq = jnp.concatenate([qh, ql, zeros], axis=1)
    def p1(i, m):
        r = pl.ds(pl.multiple_of(i * ck, ck), ck)
        s = lax.dot_general(a_ref[r, :], wq, NT, preferred_element_type=F32)
        s_ref[r, :] = s
        return jnp.maximum(m, jnp.max(s.reshape(ck // 8, 8, tq), axis=0))
    m = lax.fori_loop(0, nck, p1, jnp.full((8, tq), -jnp.inf, F32), unroll=un)
    m = jnp.max(m, axis=0, keepdims=True)
    def p2(i, o):
        r = pl.ds(pl.multiple_of(i * ck, ck), ck)
        e = jnp.exp2(s_ref[r, :] - m)
        s_ref[r, :] = e
        eb = e.astype(BF)
        e_ref[r, :] = eb
        return o + jnp.dot(vt_ref[:, r], eb, preferred_element_type=F32)
    o = lax.fori_loop(0, nck, p2, jnp.zeros((d + 16, tq), F32), unroll=un)
    inv = 1.0 / o[d:d+1, :]
    ot = o[:d] * inv
    ob = ot.T
    delta = jnp.sum(ob * do, axis=1, keepdims=True)
    invc = jnp.broadcast_to(inv, (8, tq)).T[:, 0:1]
    dh = (-delta).astype(BF); dr = -delta - dh.astype(F32)
    dm = dr.astype(BF); dl = (dr - dm.astype(F32)).astype(BF)
    lane = lax.broadcasted_iota(jnp.int32, (tq, d), 1)
    dd = jnp.where(lane == 0, dh.astype(F32), jnp.where(lane == 1, dm.astype(F32), jnp.where(lane == 2, dl.astype(F32), 0.0))).astype(BF)
    wd = jnp.concatenate([zeros, xb[:, 3*d:], dd], axis=1)
    gh, gl = split(do * invc)
    rh, rl = split(q * (invc * scale))
    none = zeros[:, :d]
    we = jnp.concatenate([none, gl, none, gh], axis=1)
    ws = jnp.concatenate([rl, none, rh, none], axis=1)
    def p3(i, dq):
        r = pl.ds(pl.multiple_of(i * ck, ck), ck)
        dp = lax.dot_general(a_ref[r, :], wd, NT, preferred_element_type=F32)
        ds = (s_ref[r, :] * dp).astype(BF)
        acc_ref[r, :] += (jnp.dot(ds, ws, preferred_element_type=F32)
                          + jnp.dot(e_ref[r, :], we, preferred_element_type=F32))
        return dq + jnp.dot(kt_ref[:, r], ds, preferred_element_type=F32)
    dq = lax.fori_loop(0, nck, p3, jnp.zeros((d, tq), F32), unroll=un)
    dq = dq * (inv * scale)
    o_ref[rows, 0:2*d] = jnp.concatenate([ot, dq], axis=0).T.astype(BF)
    @pl.when(step == pl.num_programs(0) - 1)
    def _():
        acc = acc_ref[...]
        acc = acc + pltpu.roll(acc, 2*d, 1)
        o_ref[:, 2*d:] = acc[:, 2*d:].astype(BF)

def attn(x, tq=768, ck=3840, un=1):
    tok = x.shape[0]
    return pl.pallas_call(
        functools.partial(attn_kernel, 1.0/math.sqrt(32), tq, ck, un),
        grid=(tok // tq,),
        in_specs=[pl.BlockSpec((tok, 128), lambda i: (0, 0))],
        out_specs=pl.BlockSpec((tok, 128), lambda i: (0, 0)),
        out_shape=pltpu.HBM((tok, 128), BF),
        scratch_shapes=[pltpu.VMEM((tok, 128), BF), pltpu.VMEM((32, tok), BF), pltpu.VMEM((48, tok), BF),
                        pltpu.VMEM((tok, tq), F32), pltpu.VMEM((tok, tq), BF), pltpu.VMEM((tok, 128), F32)],
        compiler_params=pltpu.CompilerParams(vmem_limit_bytes=48 << 20),
        cost_estimate=pl.CostEstimate(flops=6*2*tok*tok*128, bytes_accessed=4*tok*128, transcendentals=tok*tok),
    )(x)


LANES = 128
CALL = functools.partial(pltpu.CompilerParams, vmem_limit_bytes=40 << 20)


def cost(flops, moved):
    return pl.CostEstimate(flops=int(flops), bytes_accessed=int(moved), transcendentals=0)


def padded(plane):
    width, chans = plane.shape
    return jnp.concatenate([plane.astype(F32), jnp.zeros((LANES - width, chans), F32)], axis=0)


def pick_kernel(rows, act_ref, outer_ref, out_ref):
    group = out_ref.shape[0]
    frames, width, chans = act_ref.shape
    for f in range(frames):
        for at, src in ((f, act_ref), (frames + f, outer_ref)):
            plane = src[f].astype(F32)
            for c in range(2):
                parts = [plane[:, b + c * rows : b + (c + 1) * rows] for b in range(0, chans, 2 * rows)]
                part = jnp.concatenate(parts, axis=1).astype(BF)
                for x in range(group // 2):
                    out_ref[2 * x + c, at] = part


def pick(act, outer, rows):
    frames, width, chans = act.shape
    return pl.pallas_call(
        functools.partial(pick_kernel, rows),
        out_shape=jax.ShapeDtypeStruct((GROUP, 2 * frames, width, chans // 2), BF),
        compiler_params=CALL(),
        cost_estimate=cost(1e8, 3 << 20),
    )(act, outer)


def turn_kernel(r_ref, at_ref):
    group = r_ref.shape[0]
    frames = at_ref.shape[1]
    for f in range(frames):
        for row in range(group + 2):
            if row == 0:
                plane = r_ref[0, frames + f]
            elif row == group + 1:
                plane = r_ref[group - 1, frames + f]
            else:
                plane = r_ref[row - 1, f]
            tile = padded(plane).T
            cols = slice(row * LANES, (row + 1) * LANES)
            at_ref[0, f, :, cols] = pltpu.roll(tile, 1, 1).astype(BF)
            at_ref[1, f, :, cols] = tile.astype(BF)
            at_ref[2, f, :, cols] = pltpu.roll(tile, LANES - 1, 1).astype(BF)


def turn(r, frames):
    group, _, _, chans = r.shape
    return pl.pallas_call(
        turn_kernel,
        out_shape=pltpu.HBM((3, frames, chans, (group + 2) * LANES), BF),
        compiler_params=CALL(),
        cost_estimate=cost(1e9, 6 << 20),
    )(r)


def turn_pair_kernel(*refs):
    ins, outs = refs[:4], refs[4:]
    for own, other, out in ((ins[0], ins[1], outs[0]), (ins[2], ins[3], outs[1])):
        count = own.shape[0]
        for d, src in enumerate((own, other)):
            for f in range(count):
                at = (d * count + f) * LANES
                out[:, at : at + LANES] = padded(src[f]).T.astype(BF)


def turn_pair(own_r, other_r, own_b, other_b):
    chans = own_r.shape[-1]
    return pl.pallas_call(
        turn_pair_kernel,
        out_shape=tuple(
            pltpu.HBM((chans, 2 * x.shape[0] * LANES), BF) for x in (own_r, own_b)
        ),
        compiler_params=CALL(),
        cost_estimate=cost(1e9, 4 << 20),
    )(own_r, other_r, own_b, other_b)


def local_terms_kernel(line_ref, a0_ref, a1_ref, p1_ref, *refs):
    far, outs, scratch = refs[:5], refs[5:9], refs[9:]
    near, (at_ref, pay_ref, cot_ref, mix_ref, out_ref, sems) = scratch[:5], scratch[5:]
    rt_ref, bt_ref, p0_ref, c0_ref, c1_ref = near
    copies = [pltpu.make_async_copy(src, dst, sems.at[k]) for k, (src, dst) in enumerate(zip(far, near))]
    for at in (3, 4, 2, 0, 1):
        copies[at].start()
    frames, width, chans = a0_ref.shape
    half = chans // 2
    places = [(d, f, (d * frames + f) * LANES) for d in range(2) for f in range(frames)]
    for d, f, at in places:
        at_ref[:, at : at + LANES] = padded((a0_ref, a1_ref)[d][f]).T.astype(BF)
    parts, _, rows, _ = out_ref.shape
    block = parts * rows

    def put(first, value, lane=0):
        for n in range(value.shape[0] // block):
            for y in range(parts):
                at = n * block + y * rows
                out_ref[y, first + n, :, lane : lane + value.shape[1]] = value[at : at + rows].astype(BF)

    copies[3].wait()
    copies[4].wait()
    for d, f, at in places:
        cot_ref[at : at + LANES, :] = padded((c0_ref, c1_ref)[d][f]).astype(BF)
    put(6 * chans // block, jnp.dot(at_ref[...], cot_ref[...], preferred_element_type=F32))
    copies[2].wait()
    for d, f, at in places:
        pay_ref[at : at + LANES, :] = padded((p0_ref, p1_ref)[d][f]).astype(BF)
    copies[0].wait()
    for p in range(3):
        right = pay_ref[:, p * half : (p + 1) * half]
        for lane in range(0, half, LANES):
            value = jnp.dot(rt_ref[...], right[:, lane : lane + LANES], preferred_element_type=F32)
            mix_ref[lane // LANES, pl.ds(p, chans, stride=3), :] = value
    for lane in range(0, half, LANES):
        put(3 * chans // block, mix_ref[lane // LANES], lane)
    copies[1].wait()
    for k in range(3):
        acc = jnp.zeros((chans, half), F32)
        for d in range(2):
            left = bt_ref[:, (2 * d * frames + k) * LANES : (2 * d * frames + k + frames) * LANES]
            right = pay_ref[d * frames * LANES : (d + 1) * frames * LANES, 3 * half :]
            acc = acc + jnp.dot(left, right, preferred_element_type=F32)
        put(k * chans // block, acc)
    for k, out in enumerate(outs):
        out[...] = out_ref[lax.rem(line_ref[0] + k, parts)]


def local_terms(line, rt, bt, atted, pay, cot):
    frames, width, chans = atted[0].shape
    half = chans // 2
    span = 2 * frames * LANES
    piece = (7 * chans // 64, 16, half)
    far = (rt, bt, pay[0], cot[0], cot[1])
    return pl.pallas_call(
        local_terms_kernel,
        out_shape=(pltpu.HBM(piece, BF),) + (jax.ShapeDtypeStruct(piece, BF),) * 3,
        in_specs=[pl.BlockSpec(memory_space=pltpu.SMEM)]
        + [pl.BlockSpec(memory_space=pltpu.VMEM)] * 3
        + [pl.BlockSpec(memory_space=pltpu.HBM)] * 5,
        scratch_shapes=[pltpu.VMEM(x.shape, BF) for x in far]
        + [
            pltpu.VMEM((chans, span), BF),
            pltpu.VMEM((span, 4 * half), BF),
            pltpu.VMEM((span, half), BF),
            pltpu.VMEM((half // LANES, 3 * chans, LANES), F32),
            pltpu.VMEM((4,) + piece, BF),
            pltpu.SemaphoreType.DMA((5,)),
        ],
        compiler_params=CALL(),
        cost_estimate=cost(2e9, 10 << 20),
    )(line, *atted, pay[1], *[pltpu.with_memory_space_constraint(v, pltpu.HBM) for v in far])


def conv_terms_kernel(at_ref, dpre_ref, *refs):
    parts, (out_ref, dp_ref, acc_ref, part_ref, sems) = refs[:4], refs[4:]
    step = pl.program_id(0)
    group, _, width, cols = dpre_ref.shape
    shifts, _, chans, _ = at_ref.shape
    rows = out_ref.shape[1]
    blocks = chans // rows
    copies = [pltpu.make_async_copy(src, part_ref.at[k], sems.at[k]) for k, src in enumerate(parts)]

    @pl.when(step == 0)
    def _():
        for copy in copies:
            copy.start()

    for row in range(group):
        dp_ref[row * LANES : (row + 1) * LANES, :] = padded(dpre_ref[row, 0]).astype(BF)
    span = group * LANES

    def product(i):
        left = at_ref[:, 0, :, i * LANES : i * LANES + span].reshape(shifts * chans, span)
        return jnp.dot(left, dp_ref[...], preferred_element_type=F32)

    @pl.when(step == 0)
    def _():
        for i in range(3):
            acc_ref[i] = product(i)

    @pl.when(step == 1)
    def _():
        for i in range(3):
            value = (acc_ref[i] + product(i)).astype(BF)
            for b in range(shifts * blocks):
                out_ref[i * shifts * blocks + b] = value[b * rows : (b + 1) * rows]
        for copy in copies:
            copy.wait()
        for n in range(part_ref.shape[1]):
            value = part_ref[0, n].astype(F32)
            for k in range(1, 4):
                value = value + part_ref[k, n].astype(F32)
            value = value.astype(BF)
            out_ref[3 * shifts * blocks + n] = jnp.concatenate([value[:, :cols], value[:, cols:]], axis=0)


def conv_terms(at, dpre, parts, owners, rows):
    group, frames, width, cols = dpre.shape
    shifts, _, chans, lanes = at.shape
    assert frames == 2
    return pl.pallas_call(
        conv_terms_kernel,
        grid=(frames,),
        in_specs=[
            pl.BlockSpec((shifts, 1, chans, lanes), lambda f: (0, f, 0, 0)),
            pl.BlockSpec((group, 1, width, cols), lambda f: (0, f, 0, 0)),
        ]
        + [pl.BlockSpec(memory_space=pl.ANY)] * 4,
        out_specs=pl.BlockSpec((owners, rows, cols), lambda f: (0, 0, 0)),
        out_shape=jax.ShapeDtypeStruct((owners, rows, cols), BF),
        scratch_shapes=[
            pltpu.VMEM((group * LANES, cols), BF),
            pltpu.VMEM((3, shifts * chans, cols), F32),
            pltpu.VMEM((4,) + parts[0].shape, BF),
            pltpu.SemaphoreType.DMA((4,)),
        ],
        compiler_params=pltpu.CompilerParams(vmem_limit_bytes=60 << 20),
        cost_estimate=cost(2e9, 10 << 20),
    )(at, dpre, *parts)


def sum_kernel(norm, dims, which_ref, terms_ref, out_ref):
    times, ys, xs = dims
    rows, cols = terms_ref.shape[1:]

    @pl.when(which_ref[0] == 1)
    def _():
        for x in range(xs):
            for c in range(2):
                acc = jnp.zeros((rows, cols), F32)
                for t in range(times):
                    for y in range(ys):
                        acc = acc + terms_ref[((t * ys + y) * xs + x) * 2 + c].astype(F32)
                out_ref[c * rows : (c + 1) * rows, x * cols : (x + 1) * cols] = acc * norm

    @pl.when(which_ref[0] == 0)
    def _():
        part = rows // 2
        for y in range(ys):
            for c in range(2):
                acc = jnp.zeros((rows, cols), F32)
                for t in range(times):
                    for x in range(xs):
                        acc = acc + terms_ref[((t * ys + y) * xs + x) * 2 + c].astype(F32)
                acc = acc * norm
                for h in range(2):
                    at = (2 * c + h) * cols
                    out_ref[y * part : (y + 1) * part, at : at + cols] = acc[h * part : (h + 1) * part]


def sum_terms(which, terms, norm, dims):
    owners, rows, cols = terms.shape
    return pl.pallas_call(
        functools.partial(sum_kernel, norm, dims),
        out_shape=jax.ShapeDtypeStruct((2 * rows, 4 * cols), F32),
        in_specs=[pl.BlockSpec(memory_space=pltpu.SMEM), pl.BlockSpec(memory_space=pltpu.VMEM)],
        compiler_params=CALL(),
        cost_estimate=cost(1e7, 1 << 20),
    )(which, terms)


def dpre_kernel(own_ref, next_ref, slope_ref, tw_ref, dpre_ref, near_ref):
    frames, width, chans = own_ref.shape
    group, _, _, cols = near_ref.shape
    ext = [own_ref[f] for f in range(frames)] + [next_ref[f] for f in range(frames)]
    for f in range(frames):
        acc = jnp.zeros((width, chans), F32)
        for k in range(3):
            acc = acc + dot_nt(ext[f + 2 - k], tw_ref[k * chans : (k + 1) * chans, :])
        value = (acc * slope_ref[f]).astype(BF)
        dpre_ref[f] = value
        for e in range(group):
            near_ref[e, f] = value[:, (e // 2) * cols : (e // 2 + 1) * cols]


def make_dpre(own, nxt, slope, tw):
    frames, width, chans = own.shape
    return pl.pallas_call(
        dpre_kernel,
        out_shape=(
            pltpu.HBM((frames, width, chans), BF),
            jax.ShapeDtypeStruct((GROUP, frames, width, 2 * chans // GROUP), BF),
        ),
        compiler_params=CALL(),
        cost_estimate=cost(5e8, 3 << 20),
    )(own, nxt, slope, tw)


def dact_kernel(mid_ref, above_ref, below_ref, dres_ref, x_ref, sw_ref, out_ref):
    frames, width, chans = mid_ref.shape
    line = lax.broadcasted_iota(jnp.int32, (width, chans), 0)
    for f in range(frames):
        acc = jnp.zeros((width, chans), F32)
        for i, src in enumerate((below_ref, mid_ref, above_ref)):
            plane = src[f]
            wide = plane.astype(F32)
            right = jnp.where(line == width - 1, 0.0, pltpu.roll(wide, width - 1, 0)).astype(BF)
            left = jnp.where(line == 0, 0.0, pltpu.roll(wide, 1, 0)).astype(BF)
            for j, value in enumerate((right, plane, left)):
                tap = 3 * i + j
                acc = acc + dot_nt(value, sw_ref[tap * chans : (tap + 1) * chans, :])
        x = x_ref[f].astype(F32)
        sigma = 1.0 / (1.0 + jnp.exp(-x))
        slope = sigma * (1.0 + x * (1.0 - sigma))
        out_ref[f] = (dres_ref[f] + acc * slope).astype(BF)


def make_grad_latents(mid, above, below, dres, x, sw):
    return pl.pallas_call(
        dact_kernel,
        out_shape=jax.ShapeDtypeStruct(mid.shape, BF),
        compiler_params=CALL(),
        cost_estimate=cost(2e9, 8 << 20),
    )(mid, above, below, dres, x, sw)


def silu_slope(value):
    sigma = jax.nn.sigmoid(value)
    return sigma * (1.0 + value * (1.0 - sigma))


def matmul(left, right):
    return jnp.dot(left, right, preferred_element_type=F32)


def shift(x, axis, by):
    count = lax.axis_size(axis)
    pairs = [(i, i + by) for i in range(count) if 0 <= i + by < count]
    return lax.ppermute(x, axis, pairs)


def swap(x):
    count = lax.axis_size("space")
    return lax.ppermute(x, "space", [(i, i ^ 1) for i in range(count)])


def neighbours(field):
    return shift(field, "space", 1), shift(field, "space", -1)


def exchange(x):
    count = lax.axis_size("space")
    groups = [list(range(at, at + GROUP)) for at in range(0, count, GROUP)]
    return lax.all_to_all(x, "space", 0, 0, axis_index_groups=groups, tiled=True)


def along_y(x, by):
    count = lax.axis_size("space")
    return lax.ppermute(x, "space", [(i, (i + by * GROUP) % count) for i in range(count)])


def pick_one(x, index):
    return lax.dynamic_index_in_dim(x, index, 0, keepdims=False)


def side_pad(field):
    return jnp.pad(field, ((0, 0), (0, 0), (1, 1), (0, 0)))


def taps_of(padded, width):
    pieces = [padded[:, i, j : j + width] for i in range(3) for j in range(3)]
    return jnp.concatenate(pieces, axis=-1).reshape(-1, 9 * padded.shape[-1])


def per_device(latents, spatial_weight, temporal_weight, qkv_weight, out_weight, cotangent):
    frames, rows, width, chans = latents.shape
    ntok = frames * width
    n_space = lax.axis_size("space")
    n_time = lax.axis_size("tm")
    owners = n_space * n_time
    depth = chans // HEADS
    norm = 1.0 / math.sqrt(ntok * n_space * n_time)
    here = lax.axis_index("space")
    core, line = here % 2, here // GROUP
    half = chans // 2
    share = 16 * chans // (2 * owners)

    x = latents.reshape(frames, width, chans)
    cot = cotangent.reshape(frames, width, chans)
    act = jax.nn.silu(x.astype(F32)).astype(BF)
    above, below = neighbours(act)
    pre = matmul(taps_of(side_pad(jnp.stack([above, act, below], axis=1)), width), fetch(spatial_weight))
    pre = pre.reshape(frames, width, chans)
    bact = jax.nn.silu(pre).astype(BF)
    bext = jnp.concatenate([shift(bact, "tm", 1), bact], axis=0)
    resid, rres, items = proj(x, bext, cot, temporal_weight, qkv_weight, out_weight)
    items = items.reshape(frames * HEADS, width, 4 * depth)
    items = lax.all_to_all(items, "space", 0, 0, tiled=True)

    early = pick(act, jnp.where(here % GROUP == 0, above, below), share)
    chalf = cot.reshape(frames, width, 2, half).transpose(2, 0, 1, 3)
    cpair = (pick_one(chalf, core), swap(pick_one(chalf, 1 - core)))
    rother, bother = swap(rres), swap(bext)
    early, cpair, rother, bother, items = lax.optimization_barrier((early, cpair, rother, bother, items))
    early = exchange(early)
    outs = attn(items.reshape(n_space * width, 4 * depth)).reshape(n_space, width, 4 * depth)
    outs, early, rother, bother = lax.optimization_barrier((outs, early, rother, bother))
    outs = lax.all_to_all(outs, "space", 0, 0, tiled=True)
    aturn = turn(early, frames)
    rturn, bturn = turn_pair(rres, rother, bext, bother)
    slope = silu_slope(pre)
    outs, aturn, rturn, bturn, slope = lax.optimization_barrier((outs, aturn, rturn, bturn, slope))

    core_at = core.astype(jnp.int32).reshape(1)
    outs = outs.reshape(frames, HEADS, width, 4 * depth)
    atted, dres, dresb, mine, other = post(core_at, outs, cot, qkv_weight)
    dnext = shift(dresb, "tm", -1)
    local = local_terms(line.astype(jnp.int32).reshape(1), rturn, bturn, (atted, swap(atted)), (mine, swap(other)), cpair)
    slope, _ = lax.optimization_barrier((slope, local[0]))
    dpre, near = make_dpre(dresb, dnext, slope, temporal_weight)
    near = exchange(near)
    dabove, dbelow = neighbours(dpre)
    parts = [along_y(local[by], by) for by in (2, 1, 3)] + [local[0]]
    mixed = resid.reshape(ntok, chans) + matmul(atted.reshape(ntok, chans), out_weight)
    mixed = mixed.astype(BF).reshape(latents.shape)
    mixed, near = lax.optimization_barrier((mixed, near))
    terms = conv_terms(aturn, near, parts, owners, share)
    terms, dpre, dabove, dbelow = lax.optimization_barrier((terms, dpre, dabove, dbelow))
    terms = lax.all_to_all(terms, ("tm", "space"), 0, 0, tiled=True)
    grad_latents = make_grad_latents(dpre, dabove, dbelow, dres, x, spatial_weight).reshape(latents.shape)
    index = lax.axis_index("tm") * n_space + here
    which = (index < 9 * chans // (2 * share)).astype(jnp.int32).reshape(1)
    grad_weights = sum_terms(which, terms, norm, (n_time, n_space // GROUP, GROUP // 2))
    return (mixed, grad_latents, grad_weights)


def solution(mesh):
    placed = (P("tm", "space", None, None), P(), P(), P(), P(), P("tm", "space", None, None))
    return jax.shard_map(
        per_device,
        mesh=mesh,
        in_specs=placed,
        out_specs=(
            P("tm", "space", None, None),
            P("tm", "space", None, None),
            P(("tm", "space"), None),
        ),
        check_vma=False,
    )
```

```python
import functools
import math

import jax
import jax.numpy as jnp
from jax import lax
from jax.experimental import pallas as pl
from jax.experimental.pallas import tpu as pltpu
from jax.sharding import PartitionSpec as P

HEADS = 16
GROUP = 8
F32 = jnp.float32
BF = jnp.bfloat16
NT = (((1,), (1,)), ((), ()))

def dot_nt(left, right):
    return lax.dot_general(left, right, NT, preferred_element_type=F32)


def proj_kernel(x_ref, bext_ref, cot_ref, tw_ref, qw_ref, ow_ref, resid_ref, rres_ref, items_ref):
    frames, width, chans = x_ref.shape
    d = chans // HEADS
    for f in range(frames):
        acc = x_ref[f].astype(F32)
        for k in range(3):
            tap = tw_ref[k * chans : (k + 1) * chans, :]
            acc = acc + jnp.dot(bext_ref[f + k], tap, preferred_element_type=F32)
        resid_ref[f] = acc
        rounded = acc.astype(BF)
        rres_ref[f] = rounded
        qkv = jnp.dot(rounded, qw_ref[...], preferred_element_type=F32)
        dattn = dot_nt(cot_ref[f], ow_ref[...])
        for h in range(HEADS):
            parts = [qkv[:, p * chans + h * d : p * chans + (h + 1) * d] for p in range(3)]
            parts.append(dattn[:, h * d : (h + 1) * d])
            items_ref[f, h] = jnp.concatenate(parts, axis=1).astype(BF)


def proj(x, bext, cot, tw, qw, ow):
    frames, width, chans = x.shape
    return pl.pallas_call(
        proj_kernel,
        out_shape=(
            pltpu.HBM((frames, width, chans), F32),
            jax.ShapeDtypeStruct((frames, width, chans), BF),
            jax.ShapeDtypeStruct((frames, HEADS, width, 4 * chans // HEADS), BF),
        ),
        compiler_params=pltpu.CompilerParams(vmem_limit_bytes=32 << 20),
        cost_estimate=pl.CostEstimate(flops=10**9 * 2, bytes_accessed=6 << 20, transcendentals=0),
    )(x, bext, cot, tw, qw, ow)


def post_kernel(
    core_ref, z_ref, cot_ref, qw_hbm, attn_ref, dres_hbm, dresb_ref, mine_hbm, other_ref, qw_ref, dres_ref, mine_ref, sems
):
    frames, width, chans = cot_ref.shape
    d = chans // HEADS
    half = chans // 2
    weight = pltpu.make_async_copy(qw_hbm, qw_ref, sems.at[0])
    weight.start()
    all_parts = []
    for f in range(frames):
        heads = [z_ref[f, h].astype(F32) for h in range(HEADS)]
        parts = [jnp.concatenate([z[:, p * d : (p + 1) * d] for z in heads], axis=1).astype(BF) for p in range(4)]
        attn_ref[f] = parts[0]
        all_parts.append(parts[1:])
    weight.wait()
    for f in range(frames):
        dres = cot_ref[f].astype(F32)
        for p in range(3):
            dres = dres + dot_nt(all_parts[f][p], qw_ref[:, p * chans : (p + 1) * chans])
        dres_ref[f] = dres
        dresb = dres.astype(BF)
        dresb_ref[f] = dresb
        all_parts[f].append(dresb)
    sent = pltpu.make_async_copy(dres_ref, dres_hbm, sems.at[1])
    sent.start()

    def store(first, second):
        for f in range(frames):
            for at, part in enumerate(all_parts[f]):
                for out, c in ((first, 0), (second, 1)):
                    out[f, :, at * half : (at + 1) * half] = part[:, c * half : (c + 1) * half]

    @pl.when(core_ref[0] == 0)
    def _():
        store(mine_ref, other_ref)

    @pl.when(core_ref[0] == 1)
    def _():
        store(other_ref, mine_ref)

    kept = pltpu.make_async_copy(mine_ref, mine_hbm, sems.at[2])
    kept.start()
    sent.wait()
    kept.wait()


def post(core, z, cot, qw):
    frames, width, chans = cot.shape
    vmem, hbm = pl.BlockSpec(memory_space=pltpu.VMEM), pl.BlockSpec(memory_space=pltpu.HBM)
    return pl.pallas_call(
        post_kernel,
        out_shape=(
            jax.ShapeDtypeStruct((frames, width, chans), BF),
            pltpu.HBM((frames, width, chans), F32),
            jax.ShapeDtypeStruct((frames, width, chans), BF),
            pltpu.HBM((frames, width, 2 * chans), BF),
            jax.ShapeDtypeStruct((frames, width, 2 * chans), BF),
        ),
        in_specs=[pl.BlockSpec(memory_space=pltpu.SMEM), vmem, vmem, hbm],
        out_specs=(vmem, hbm, vmem, hbm, vmem),
        scratch_shapes=[
            pltpu.VMEM(qw.shape, BF),
            pltpu.VMEM((frames, width, chans), F32),
            pltpu.VMEM((frames, width, 2 * chans), BF),
            pltpu.SemaphoreType.DMA((3,)),
        ],
        compiler_params=pltpu.CompilerParams(vmem_limit_bytes=32 << 20),
        cost_estimate=pl.CostEstimate(flops=10**9, bytes_accessed=6 << 20, transcendentals=0),
    )(core, z, cot, pltpu.with_memory_space_constraint(qw, pltpu.HBM))


def fetch_kernel(w_ref, out_ref):
    out_ref[...] = w_ref[...]


def fetch(w):
    return pl.pallas_call(
        fetch_kernel,
        out_shape=jax.ShapeDtypeStruct(w.shape, w.dtype),
        compiler_params=pltpu.CompilerParams(vmem_limit_bytes=24 << 20),
        cost_estimate=pl.CostEstimate(flops=10**6, bytes_accessed=10 << 20, transcendentals=0),
    )(w)


def attn_kernel(scale, tq, ck, un, x_ref, o_ref, a_ref, kt_ref, vt_ref, s_ref, e_ref, acc_ref):
    tok = x_ref.shape[0]
    step = pl.program_id(0)
    nck = tok // ck
    d = 32
    @pl.when(step == 0)
    def _():
        k = x_ref[:, d:2*d]
        v = x_ref[:, 2*d:3*d]
        lane = lax.broadcasted_iota(jnp.int32, (tok, d), 1)
        ones = jnp.where(lane < 3, 1.0, 0.0).astype(BF)
        a_ref[...] = jnp.concatenate([k, k, v, ones], axis=1)
        kt_ref[...] = k.astype(F32).T.astype(BF)
        vt_ref[...] = jnp.concatenate([v, ones], axis=1).astype(F32).T[: d + 16].astype(BF)
        acc_ref[...] = jnp.zeros_like(acc_ref)
    rows = pl.ds(pl.multiple_of(step * tq, tq), tq)
    xb = x_ref[rows, :]
    q = xb[:, 0:d].astype(F32)
    do = xb[:, 3*d:4*d].astype(F32)
    zeros = jnp.zeros((tq, 2*d), BF)
    def split(z):
        hi = z.astype(BF)
        lo = (z - hi.astype(F32)).astype(BF)
        return hi, lo
    qh, ql = split(q * (scale * math.log2(math.e)))
    wq = jnp.concatenate([qh, ql, zeros], axis=1)
    def p1(i, m):
        r = pl.ds(pl.multiple_of(i * ck, ck), ck)
        s = lax.dot_general(a_ref[r, :], wq, NT, preferred_element_type=F32)
        s_ref[r, :] = s
        return jnp.maximum(m, jnp.max(s.reshape(ck // 8, 8, tq), axis=0))
    m = lax.fori_loop(0, nck, p1, jnp.full((8, tq), -jnp.inf, F32), unroll=un)
    m = jnp.max(m, axis=0, keepdims=True)
    def p2(i, o):
        r = pl.ds(pl.multiple_of(i * ck, ck), ck)
        e = jnp.exp2(s_ref[r, :] - m)
        s_ref[r, :] = e
        eb = e.astype(BF)
        e_ref[r, :] = eb
        return o + jnp.dot(vt_ref[:, r], eb, preferred_element_type=F32)
    o = lax.fori_loop(0, nck, p2, jnp.zeros((d + 16, tq), F32), unroll=un)
    inv = 1.0 / o[d:d+1, :]
    ot = o[:d] * inv
    ob = ot.T
    delta = jnp.sum(ob * do, axis=1, keepdims=True)
    invc = jnp.broadcast_to(inv, (8, tq)).T[:, 0:1]
    dh = (-delta).astype(BF); dr = -delta - dh.astype(F32)
    dm = dr.astype(BF); dl = (dr - dm.astype(F32)).astype(BF)
    lane = lax.broadcasted_iota(jnp.int32, (tq, d), 1)
    dd = jnp.where(lane == 0, dh.astype(F32), jnp.where(lane == 1, dm.astype(F32), jnp.where(lane == 2, dl.astype(F32), 0.0))).astype(BF)
    wd = jnp.concatenate([zeros, xb[:, 3*d:], dd], axis=1)
    gh, gl = split(do * invc)
    rh, rl = split(q * (invc * scale))
    none = zeros[:, :d]
    we = jnp.concatenate([none, gl, none, gh], axis=1)
    ws = jnp.concatenate([rl, none, rh, none], axis=1)
    def p3(i, dq):
        r = pl.ds(pl.multiple_of(i * ck, ck), ck)
        dp = lax.dot_general(a_ref[r, :], wd, NT, preferred_element_type=F32)
        ds = (s_ref[r, :] * dp).astype(BF)
        acc_ref[r, :] += (jnp.dot(ds, ws, preferred_element_type=F32)
                          + jnp.dot(e_ref[r, :], we, preferred_element_type=F32))
        return dq + jnp.dot(kt_ref[:, r], ds, preferred_element_type=F32)
    dq = lax.fori_loop(0, nck, p3, jnp.zeros((d, tq), F32), unroll=un)
    dq = dq * (inv * scale)
    o_ref[rows, 0:2*d] = jnp.concatenate([ot, dq], axis=0).T.astype(BF)
    @pl.when(step == pl.num_programs(0) - 1)
    def _():
        acc = acc_ref[...]
        acc = acc + pltpu.roll(acc, 2*d, 1)
        o_ref[:, 2*d:] = acc[:, 2*d:].astype(BF)

def attn(x, tq=768, ck=3840, un=1):
    tok = x.shape[0]
    return pl.pallas_call(
        functools.partial(attn_kernel, 1.0/math.sqrt(32), tq, ck, un),
        grid=(tok // tq,),
        in_specs=[pl.BlockSpec((tok, 128), lambda i: (0, 0))],
        out_specs=pl.BlockSpec((tok, 128), lambda i: (0, 0)),
        out_shape=pltpu.HBM((tok, 128), BF),
        scratch_shapes=[pltpu.VMEM((tok, 128), BF), pltpu.VMEM((32, tok), BF), pltpu.VMEM((48, tok), BF),
                        pltpu.VMEM((tok, tq), F32), pltpu.VMEM((tok, tq), BF), pltpu.VMEM((tok, 128), F32)],
        compiler_params=pltpu.CompilerParams(vmem_limit_bytes=48 << 20),
        cost_estimate=pl.CostEstimate(flops=6*2*tok*tok*128, bytes_accessed=4*tok*128, transcendentals=tok*tok),
    )(x)


LANES = 128
CALL = functools.partial(pltpu.CompilerParams, vmem_limit_bytes=40 << 20)


def cost(flops, moved):
    return pl.CostEstimate(flops=int(flops), bytes_accessed=int(moved), transcendentals=0)


def padded(plane):
    width, chans = plane.shape
    return jnp.concatenate([plane.astype(F32), jnp.zeros((LANES - width, chans), F32)], axis=0)


def pick_kernel(rows, act_ref, outer_ref, out_ref):
    group = out_ref.shape[0]
    frames, width, chans = act_ref.shape
    for f in range(frames):
        for at, src in ((f, act_ref), (frames + f, outer_ref)):
            plane = src[f].astype(F32)
            for c in range(2):
                parts = [plane[:, b + c * rows : b + (c + 1) * rows] for b in range(0, chans, 2 * rows)]
                part = jnp.concatenate(parts, axis=1).astype(BF)
                for x in range(group // 2):
                    out_ref[2 * x + c, at] = part


def pick(act, outer, rows):
    frames, width, chans = act.shape
    return pl.pallas_call(
        functools.partial(pick_kernel, rows),
        out_shape=jax.ShapeDtypeStruct((GROUP, 2 * frames, width, chans // 2), BF),
        compiler_params=CALL(),
        cost_estimate=cost(1e8, 3 << 20),
    )(act, outer)


def turn_kernel(r_ref, at_ref):
    group = r_ref.shape[0]
    frames = at_ref.shape[1]
    for f in range(frames):
        for row in range(group + 2):
            if row == 0:
                plane = r_ref[0, frames + f]
            elif row == group + 1:
                plane = r_ref[group - 1, frames + f]
            else:
                plane = r_ref[row - 1, f]
            tile = padded(plane).T
            cols = slice(row * LANES, (row + 1) * LANES)
            at_ref[0, f, :, cols] = pltpu.roll(tile, 1, 1).astype(BF)
            at_ref[1, f, :, cols] = tile.astype(BF)
            at_ref[2, f, :, cols] = pltpu.roll(tile, LANES - 1, 1).astype(BF)


def turn(r, frames):
    group, _, _, chans = r.shape
    return pl.pallas_call(
        turn_kernel,
        out_shape=pltpu.HBM((3, frames, chans, (group + 2) * LANES), BF),
        compiler_params=CALL(),
        cost_estimate=cost(1e9, 6 << 20),
    )(r)


def turn_pair_kernel(*refs):
    ins, outs = refs[:4], refs[4:]
    for own, other, out in ((ins[0], ins[1], outs[0]), (ins[2], ins[3], outs[1])):
        count = own.shape[0]
        for d, src in enumerate((own, other)):
            for f in range(count):
                at = (d * count + f) * LANES
                out[:, at : at + LANES] = padded(src[f]).T.astype(BF)


def turn_pair(own_r, other_r, own_b, other_b):
    chans = own_r.shape[-1]
    return pl.pallas_call(
        turn_pair_kernel,
        out_shape=tuple(
            pltpu.HBM((chans, 2 * x.shape[0] * LANES), BF) for x in (own_r, own_b)
        ),
        compiler_params=CALL(),
        cost_estimate=cost(1e9, 4 << 20),
    )(own_r, other_r, own_b, other_b)


def local_terms_kernel(line_ref, a0_ref, a1_ref, p1_ref, *refs):
    far, outs, scratch = refs[:5], refs[5:10], refs[10:]
    near, (at_ref, pay_ref, cot_ref, mix_ref, out_ref, sems) = scratch[:5], scratch[5:]
    rt_ref, bt_ref, p0_ref, c0_ref, c1_ref = near
    copies = [pltpu.make_async_copy(src, dst, sems.at[k]) for k, (src, dst) in enumerate(zip(far, near))]
    for at in (3, 4, 2, 0, 1):
        copies[at].start()
    frames, width, chans = a0_ref.shape
    half = chans // 2
    places = [(d, f, (d * frames + f) * LANES) for d in range(2) for f in range(frames)]
    for d, f, at in places:
        at_ref[:, at : at + LANES] = padded((a0_ref, a1_ref)[d][f]).T.astype(BF)
    parts, _, rows, _ = out_ref.shape
    block = parts * rows

    def put(first, value, lane=0):
        for n in range(value.shape[0] // block):
            for y in range(parts):
                at = n * block + y * rows
                out_ref[y, first + n, :, lane : lane + value.shape[1]] = value[at : at + rows].astype(BF)

    copies[3].wait()
    copies[4].wait()
    for d, f, at in places:
        cot_ref[at : at + LANES, :] = padded((c0_ref, c1_ref)[d][f]).astype(BF)
    put(6 * chans // block, jnp.dot(at_ref[...], cot_ref[...], preferred_element_type=F32))
    copies[2].wait()
    for d, f, at in places:
        pay_ref[at : at + LANES, :] = padded((p0_ref, p1_ref)[d][f]).astype(BF)
    copies[0].wait()
    for p in range(3):
        right = pay_ref[:, p * half : (p + 1) * half]
        for lane in range(0, half, LANES):
            value = jnp.dot(rt_ref[...], right[:, lane : lane + LANES], preferred_element_type=F32)
            mix_ref[lane // LANES, pl.ds(p, chans, stride=3), :] = value
    for lane in range(0, half, LANES):
        put(3 * chans // block, mix_ref[lane // LANES], lane)
    copies[1].wait()
    for k in range(3):
        acc = jnp.zeros((chans, half), F32)
        for d in range(2):
            left = bt_ref[:, (2 * d * frames + k) * LANES : (2 * d * frames + k + frames) * LANES]
            right = pay_ref[d * frames * LANES : (d + 1) * frames * LANES, 3 * half :]
            acc = acc + jnp.dot(left, right, preferred_element_type=F32)
        put(k * chans // block, acc)
    count = outs[2].shape[0]
    for out, k, at in zip(outs, (0, 1, 2, 2, 3), (0, 0, 0, count, 0)):
        out[...] = out_ref[lax.rem(line_ref[0] + k, parts), at : at + out.shape[0]]


def local_terms(line, rt, bt, atted, pay, cot):
    frames, width, chans = atted[0].shape
    half = chans // 2
    span = 2 * frames * LANES
    piece = (7 * chans // 64, 16, half)
    half_piece = (piece[0] // 2,) + piece[1:]
    far = (rt, bt, pay[0], cot[0], cot[1])
    return pl.pallas_call(
        local_terms_kernel,
        out_shape=(pltpu.HBM(piece, BF),)
        + tuple(jax.ShapeDtypeStruct(shape, BF) for shape in (piece, half_piece, half_piece, piece)),
        in_specs=[pl.BlockSpec(memory_space=pltpu.SMEM)]
        + [pl.BlockSpec(memory_space=pltpu.VMEM)] * 3
        + [pl.BlockSpec(memory_space=pltpu.HBM)] * 5,
        scratch_shapes=[pltpu.VMEM(x.shape, BF) for x in far]
        + [
            pltpu.VMEM((chans, span), BF),
            pltpu.VMEM((span, 4 * half), BF),
            pltpu.VMEM((span, half), BF),
            pltpu.VMEM((half // LANES, 3 * chans, LANES), F32),
            pltpu.VMEM((4,) + piece, BF),
            pltpu.SemaphoreType.DMA((5,)),
        ],
        compiler_params=CALL(),
        cost_estimate=cost(2e9, 10 << 20),
    )(line, *atted, pay[1], *[pltpu.with_memory_space_constraint(v, pltpu.HBM) for v in far])


def conv_terms_kernel(at_ref, dpre_ref, *refs):
    parts, (out_ref, dp_ref, acc_ref, part_ref, sems) = refs[:5], refs[5:]
    step = pl.program_id(0)
    group, _, width, cols = dpre_ref.shape
    shifts, _, chans, _ = at_ref.shape
    rows = out_ref.shape[1]
    blocks = chans // rows
    count = part_ref.shape[1] // 2
    places = [part_ref.at[0], part_ref.at[1], part_ref.at[2, pl.ds(0, count)], part_ref.at[2, pl.ds(count, count)], part_ref.at[3]]
    copies = [pltpu.make_async_copy(src, dst, sems.at[k]) for k, (src, dst) in enumerate(zip(parts, places))]

    @pl.when(step == 0)
    def _():
        for copy in copies:
            copy.start()

    for row in range(group):
        dp_ref[row * LANES : (row + 1) * LANES, :] = padded(dpre_ref[row, 0]).astype(BF)
    span = group * LANES

    def product(i):
        left = at_ref[:, 0, :, i * LANES : i * LANES + span].reshape(shifts * chans, span)
        return jnp.dot(left, dp_ref[...], preferred_element_type=F32)

    @pl.when(step == 0)
    def _():
        for i in range(3):
            acc_ref[i] = product(i)

    @pl.when(step == 1)
    def _():
        for i in range(3):
            value = (acc_ref[i] + product(i)).astype(BF)
            for b in range(shifts * blocks):
                out_ref[i * shifts * blocks + b] = value[b * rows : (b + 1) * rows]
        for copy in copies:
            copy.wait()
        for n in range(part_ref.shape[1]):
            value = part_ref[0, n].astype(F32)
            for k in range(1, 4):
                value = value + part_ref[k, n].astype(F32)
            value = value.astype(BF)
            out_ref[3 * shifts * blocks + n] = jnp.concatenate([value[:, :cols], value[:, cols:]], axis=0)


def conv_terms(at, dpre, parts, owners, rows):
    group, frames, width, cols = dpre.shape
    shifts, _, chans, lanes = at.shape
    assert frames == 2
    return pl.pallas_call(
        conv_terms_kernel,
        grid=(frames,),
        in_specs=[
            pl.BlockSpec((shifts, 1, chans, lanes), lambda f: (0, f, 0, 0)),
            pl.BlockSpec((group, 1, width, cols), lambda f: (0, f, 0, 0)),
        ]
        + [pl.BlockSpec(memory_space=pl.ANY)] * 5,
        out_specs=pl.BlockSpec((owners, rows, cols), lambda f: (0, 0, 0)),
        out_shape=jax.ShapeDtypeStruct((owners, rows, cols), BF),
        scratch_shapes=[
            pltpu.VMEM((group * LANES, cols), BF),
            pltpu.VMEM((3, shifts * chans, cols), F32),
            pltpu.VMEM((4,) + parts[0].shape, BF),
            pltpu.SemaphoreType.DMA((5,)),
        ],
        compiler_params=pltpu.CompilerParams(vmem_limit_bytes=60 << 20),
        cost_estimate=cost(2e9, 10 << 20),
    )(at, dpre, *parts)


def sum_kernel(norm, dims, which_ref, terms_ref, out_ref):
    times, ys, xs = dims
    rows, cols = terms_ref.shape[1:]

    @pl.when(which_ref[0] == 1)
    def _():
        for x in range(xs):
            for c in range(2):
                acc = jnp.zeros((rows, cols), F32)
                for t in range(times):
                    for y in range(ys):
                        acc = acc + terms_ref[((t * ys + y) * xs + x) * 2 + c].astype(F32)
                out_ref[c * rows : (c + 1) * rows, x * cols : (x + 1) * cols] = acc * norm

    @pl.when(which_ref[0] == 0)
    def _():
        part = rows // 2
        for y in range(ys):
            for c in range(2):
                acc = jnp.zeros((rows, cols), F32)
                for t in range(times):
                    for x in range(xs):
                        acc = acc + terms_ref[((t * ys + y) * xs + x) * 2 + c].astype(F32)
                acc = acc * norm
                for h in range(2):
                    at = (2 * c + h) * cols
                    out_ref[y * part : (y + 1) * part, at : at + cols] = acc[h * part : (h + 1) * part]


def sum_terms(which, terms, norm, dims):
    owners, rows, cols = terms.shape
    return pl.pallas_call(
        functools.partial(sum_kernel, norm, dims),
        out_shape=jax.ShapeDtypeStruct((2 * rows, 4 * cols), F32),
        in_specs=[pl.BlockSpec(memory_space=pltpu.SMEM), pl.BlockSpec(memory_space=pltpu.VMEM)],
        compiler_params=CALL(),
        cost_estimate=cost(1e7, 1 << 20),
    )(which, terms)


def dpre_kernel(own_ref, next_ref, slope_ref, tw_ref, dpre_ref, near_ref):
    frames, width, chans = own_ref.shape
    group, _, _, cols = near_ref.shape
    ext = [own_ref[f] for f in range(frames)] + [next_ref[f] for f in range(frames)]
    for f in range(frames):
        acc = jnp.zeros((width, chans), F32)
        for k in range(3):
            acc = acc + dot_nt(ext[f + 2 - k], tw_ref[k * chans : (k + 1) * chans, :])
        value = (acc * slope_ref[f]).astype(BF)
        dpre_ref[f] = value
        for e in range(group):
            near_ref[e, f] = value[:, (e // 2) * cols : (e // 2 + 1) * cols]


def make_dpre(own, nxt, slope, tw):
    frames, width, chans = own.shape
    return pl.pallas_call(
        dpre_kernel,
        out_shape=(
            pltpu.HBM((frames, width, chans), BF),
            jax.ShapeDtypeStruct((GROUP, frames, width, 2 * chans // GROUP), BF),
        ),
        compiler_params=CALL(),
        cost_estimate=cost(5e8, 3 << 20),
    )(own, nxt, slope, tw)


def dact_kernel(mid_ref, above_ref, below_ref, dres_ref, x_ref, sw_ref, out_ref):
    frames, width, chans = mid_ref.shape
    line = lax.broadcasted_iota(jnp.int32, (width, chans), 0)
    for f in range(frames):
        acc = jnp.zeros((width, chans), F32)
        for i, src in enumerate((below_ref, mid_ref, above_ref)):
            plane = src[f]
            wide = plane.astype(F32)
            right = jnp.where(line == width - 1, 0.0, pltpu.roll(wide, width - 1, 0)).astype(BF)
            left = jnp.where(line == 0, 0.0, pltpu.roll(wide, 1, 0)).astype(BF)
            for j, value in enumerate((right, plane, left)):
                tap = 3 * i + j
                acc = acc + dot_nt(value, sw_ref[tap * chans : (tap + 1) * chans, :])
        x = x_ref[f].astype(F32)
        sigma = 1.0 / (1.0 + jnp.exp(-x))
        slope = sigma * (1.0 + x * (1.0 - sigma))
        out_ref[f] = (dres_ref[f] + acc * slope).astype(BF)


def make_grad_latents(mid, above, below, dres, x, sw):
    return pl.pallas_call(
        dact_kernel,
        out_shape=jax.ShapeDtypeStruct(mid.shape, BF),
        compiler_params=CALL(),
        cost_estimate=cost(2e9, 8 << 20),
    )(mid, above, below, dres, x, sw)


def silu_slope(value):
    sigma = jax.nn.sigmoid(value)
    return sigma * (1.0 + value * (1.0 - sigma))


def matmul(left, right):
    return jnp.dot(left, right, preferred_element_type=F32)


def shift(x, axis, by):
    count = lax.axis_size(axis)
    pairs = [(i, i + by) for i in range(count) if 0 <= i + by < count]
    return lax.ppermute(x, axis, pairs)


def swap(x):
    count = lax.axis_size("space")
    return lax.ppermute(x, "space", [(i, i ^ 1) for i in range(count)])


def neighbours(field):
    return shift(field, "space", 1), shift(field, "space", -1)


def exchange(x):
    count = lax.axis_size("space")
    groups = [list(range(at, at + GROUP)) for at in range(0, count, GROUP)]
    return lax.all_to_all(x, "space", 0, 0, axis_index_groups=groups, tiled=True)


def along_y(x, by):
    count = lax.axis_size("space")
    return lax.ppermute(x, "space", [(i, (i + by * GROUP) % count) for i in range(count)])


def pick_one(x, index):
    return lax.dynamic_index_in_dim(x, index, 0, keepdims=False)


def side_pad(field):
    return jnp.pad(field, ((0, 0), (0, 0), (1, 1), (0, 0)))


def taps_of(padded, width):
    pieces = [padded[:, i, j : j + width] for i in range(3) for j in range(3)]
    return jnp.concatenate(pieces, axis=-1).reshape(-1, 9 * padded.shape[-1])


def per_device(latents, spatial_weight, temporal_weight, qkv_weight, out_weight, cotangent):
    frames, rows, width, chans = latents.shape
    ntok = frames * width
    n_space = lax.axis_size("space")
    n_time = lax.axis_size("tm")
    owners = n_space * n_time
    depth = chans // HEADS
    norm = 1.0 / math.sqrt(ntok * n_space * n_time)
    here = lax.axis_index("space")
    core, line = here % 2, here // GROUP
    half = chans // 2
    share = 16 * chans // (2 * owners)

    x = latents.reshape(frames, width, chans)
    cot = cotangent.reshape(frames, width, chans)
    act = jax.nn.silu(x.astype(F32)).astype(BF)
    above, below = neighbours(act)
    pre = matmul(taps_of(side_pad(jnp.stack([above, act, below], axis=1)), width), fetch(spatial_weight))
    pre = pre.reshape(frames, width, chans)
    bact = jax.nn.silu(pre).astype(BF)
    bext = jnp.concatenate([shift(bact, "tm", 1), bact], axis=0)
    resid, rres, items = proj(x, bext, cot, temporal_weight, qkv_weight, out_weight)
    items = items.reshape(frames * HEADS, width, 4 * depth)
    items = lax.all_to_all(items, "space", 0, 0, tiled=True)

    early = pick(act, jnp.where(here % GROUP == 0, above, below), share)
    chalf = cot.reshape(frames, width, 2, half).transpose(2, 0, 1, 3)
    cpair = (pick_one(chalf, core), swap(pick_one(chalf, 1 - core)))
    rother, bother = swap(rres), swap(bext)
    early, cpair, rother, bother, items = lax.optimization_barrier((early, cpair, rother, bother, items))
    early = exchange(early)
    outs = attn(items.reshape(n_space * width, 4 * depth)).reshape(n_space, width, 4 * depth)
    outs, early, rother, bother = lax.optimization_barrier((outs, early, rother, bother))
    outs = lax.all_to_all(outs, "space", 0, 0, tiled=True)
    aturn = turn(early, frames)
    rturn, bturn = turn_pair(rres, rother, bext, bother)
    slope = silu_slope(pre)
    outs, aturn, rturn, bturn, slope = lax.optimization_barrier((outs, aturn, rturn, bturn, slope))

    core_at = core.astype(jnp.int32).reshape(1)
    outs = outs.reshape(frames, HEADS, width, 4 * depth)
    atted, dres, dresb, mine, other = post(core_at, outs, cot, qkv_weight)
    dnext = shift(dresb, "tm", -1)
    local = local_terms(line.astype(jnp.int32).reshape(1), rturn, bturn, (atted, swap(atted)), (mine, swap(other)), cpair)
    slope, _ = lax.optimization_barrier((slope, local[0]))
    dpre, near = make_dpre(dresb, dnext, slope, temporal_weight)
    near = exchange(near)
    dabove, dbelow = neighbours(dpre)
    relayed = along_y(local[3], 3)
    parts = [local[0], along_y(local[1], 1), along_y(local[2], 2), along_y(relayed, 3), along_y(local[4], 3)]
    mixed = resid.reshape(ntok, chans) + matmul(atted.reshape(ntok, chans), out_weight)
    mixed = mixed.astype(BF).reshape(latents.shape)
    mixed, near = lax.optimization_barrier((mixed, near))
    terms = conv_terms(aturn, near, parts, owners, share)
    terms, dpre, dabove, dbelow = lax.optimization_barrier((terms, dpre, dabove, dbelow))
    terms = lax.all_to_all(terms, ("tm", "space"), 0, 0, tiled=True)
    grad_latents = make_grad_latents(dpre, dabove, dbelow, dres, x, spatial_weight).reshape(latents.shape)
    index = lax.axis_index("tm") * n_space + here
    which = (index < 9 * chans // (2 * share)).astype(jnp.int32).reshape(1)
    grad_weights = sum_terms(which, terms, norm, (n_time, n_space // GROUP, GROUP // 2))
    return (mixed, grad_latents, grad_weights)


def solution(mesh):
    placed = (P("tm", "space", None, None), P(), P(), P(), P(), P("tm", "space", None, None))
    return jax.shard_map(
        per_device,
        mesh=mesh,
        in_specs=placed,
        out_specs=(
            P("tm", "space", None, None),
            P("tm", "space", None, None),
            P(("tm", "space"), None),
        ),
        check_vma=False,
    )
```

```python
import functools
import math

import jax
import jax.numpy as jnp
from jax import lax
from jax.experimental import pallas as pl
from jax.experimental.pallas import tpu as pltpu
from jax.sharding import PartitionSpec as P

HEADS = 16
GROUP = 8
F32 = jnp.float32
BF = jnp.bfloat16
NT = (((1,), (1,)), ((), ()))

def dot_nt(left, right):
    return lax.dot_general(left, right, NT, preferred_element_type=F32)


def proj_kernel(x_ref, bext_ref, cot_ref, tw_ref, qw_ref, ow_ref, resid_ref, rres_ref, items_ref):
    frames, width, chans = x_ref.shape
    d = chans // HEADS
    for f in range(frames):
        acc = x_ref[f].astype(F32)
        for k in range(3):
            tap = tw_ref[k * chans : (k + 1) * chans, :]
            acc = acc + jnp.dot(bext_ref[f + k], tap, preferred_element_type=F32)
        resid_ref[f] = acc
        rounded = acc.astype(BF)
        rres_ref[f] = rounded
        qkv = jnp.dot(rounded, qw_ref[...], preferred_element_type=F32)
        dattn = dot_nt(cot_ref[f], ow_ref[...])
        for h in range(HEADS):
            parts = [qkv[:, p * chans + h * d : p * chans + (h + 1) * d] for p in range(3)]
            parts.append(dattn[:, h * d : (h + 1) * d])
            items_ref[f, h] = jnp.concatenate(parts, axis=1).astype(BF)


def proj(x, bext, cot, tw, qw, ow):
    frames, width, chans = x.shape
    return pl.pallas_call(
        proj_kernel,
        out_shape=(
            pltpu.HBM((frames, width, chans), F32),
            jax.ShapeDtypeStruct((frames, width, chans), BF),
            jax.ShapeDtypeStruct((frames, HEADS, width, 4 * chans // HEADS), BF),
        ),
        compiler_params=pltpu.CompilerParams(vmem_limit_bytes=32 << 20),
        cost_estimate=pl.CostEstimate(flops=10**9 * 2, bytes_accessed=6 << 20, transcendentals=0),
    )(x, bext, cot, tw, qw, ow)


def post_kernel(
    core_ref, z_ref, cot_ref, qw_hbm, attn_ref, dres_hbm, dresb_ref, mine_hbm, other_ref, qw_ref, dres_ref, mine_ref, sems
):
    frames, width, chans = cot_ref.shape
    d = chans // HEADS
    half = chans // 2
    weight = pltpu.make_async_copy(qw_hbm, qw_ref, sems.at[0])
    weight.start()
    all_parts = []
    for f in range(frames):
        heads = [z_ref[f, h].astype(F32) for h in range(HEADS)]
        parts = [jnp.concatenate([z[:, p * d : (p + 1) * d] for z in heads], axis=1).astype(BF) for p in range(4)]
        attn_ref[f] = parts[0]
        all_parts.append(parts[1:])
    weight.wait()
    for f in range(frames):
        dres = cot_ref[f].astype(F32)
        for p in range(3):
            dres = dres + dot_nt(all_parts[f][p], qw_ref[:, p * chans : (p + 1) * chans])
        dres_ref[f] = dres
        dresb = dres.astype(BF)
        dresb_ref[f] = dresb
        all_parts[f].append(dresb)
    sent = pltpu.make_async_copy(dres_ref, dres_hbm, sems.at[1])
    sent.start()

    def store(first, second):
        for f in range(frames):
            for at, part in enumerate(all_parts[f]):
                for out, c in ((first, 0), (second, 1)):
                    out[f, :, at * half : (at + 1) * half] = part[:, c * half : (c + 1) * half]

    @pl.when(core_ref[0] == 0)
    def _():
        store(mine_ref, other_ref)

    @pl.when(core_ref[0] == 1)
    def _():
        store(other_ref, mine_ref)

    kept = pltpu.make_async_copy(mine_ref, mine_hbm, sems.at[2])
    kept.start()
    sent.wait()
    kept.wait()


def post(core, z, cot, qw):
    frames, width, chans = cot.shape
    vmem, hbm = pl.BlockSpec(memory_space=pltpu.VMEM), pl.BlockSpec(memory_space=pltpu.HBM)
    return pl.pallas_call(
        post_kernel,
        out_shape=(
            jax.ShapeDtypeStruct((frames, width, chans), BF),
            pltpu.HBM((frames, width, chans), F32),
            jax.ShapeDtypeStruct((frames, width, chans), BF),
            pltpu.HBM((frames, width, 2 * chans), BF),
            jax.ShapeDtypeStruct((frames, width, 2 * chans), BF),
        ),
        in_specs=[pl.BlockSpec(memory_space=pltpu.SMEM), vmem, vmem, hbm],
        out_specs=(vmem, hbm, vmem, hbm, vmem),
        scratch_shapes=[
            pltpu.VMEM(qw.shape, BF),
            pltpu.VMEM((frames, width, chans), F32),
            pltpu.VMEM((frames, width, 2 * chans), BF),
            pltpu.SemaphoreType.DMA((3,)),
        ],
        compiler_params=pltpu.CompilerParams(vmem_limit_bytes=32 << 20),
        cost_estimate=pl.CostEstimate(flops=10**9, bytes_accessed=6 << 20, transcendentals=0),
    )(core, z, cot, pltpu.with_memory_space_constraint(qw, pltpu.HBM))


def fetch_kernel(w_ref, out_ref):
    out_ref[...] = w_ref[...]


def fetch(w):
    return pl.pallas_call(
        fetch_kernel,
        out_shape=jax.ShapeDtypeStruct(w.shape, w.dtype),
        compiler_params=pltpu.CompilerParams(vmem_limit_bytes=24 << 20),
        cost_estimate=pl.CostEstimate(flops=10**6, bytes_accessed=10 << 20, transcendentals=0),
    )(w)


def attn_kernel(scale, tq, ck, un, x_ref, o_ref, a_ref, kt_ref, vt_ref, s_ref, e_ref, acc_ref):
    tok = x_ref.shape[0]
    step = pl.program_id(0)
    nck = tok // ck
    d = 32
    @pl.when(step == 0)
    def _():
        k = x_ref[:, d:2*d]
        v = x_ref[:, 2*d:3*d]
        lane = lax.broadcasted_iota(jnp.int32, (tok, d), 1)
        ones = jnp.where(lane < 3, 1.0, 0.0).astype(BF)
        a_ref[...] = jnp.concatenate([k, k, v, ones], axis=1)
        kt_ref[...] = k.astype(F32).T.astype(BF)
        vt_ref[...] = jnp.concatenate([v, ones], axis=1).astype(F32).T[: d + 16].astype(BF)
        acc_ref[...] = jnp.zeros_like(acc_ref)
    rows = pl.ds(pl.multiple_of(step * tq, tq), tq)
    xb = x_ref[rows, :]
    q = xb[:, 0:d].astype(F32)
    do = xb[:, 3*d:4*d].astype(F32)
    zeros = jnp.zeros((tq, 2*d), BF)
    def split(z):
        hi = z.astype(BF)
        lo = (z - hi.astype(F32)).astype(BF)
        return hi, lo
    qh, ql = split(q * (scale * math.log2(math.e)))
    wq = jnp.concatenate([qh, ql, zeros], axis=1)
    def p1(i, m):
        r = pl.ds(pl.multiple_of(i * ck, ck), ck)
        s = lax.dot_general(a_ref[r, :], wq, NT, preferred_element_type=F32)
        s_ref[r, :] = s
        return jnp.maximum(m, jnp.max(s.reshape(ck // 8, 8, tq), axis=0))
    m = lax.fori_loop(0, nck, p1, jnp.full((8, tq), -jnp.inf, F32), unroll=un)
    m = jnp.max(m, axis=0, keepdims=True)
    def p2(i, o):
        r = pl.ds(pl.multiple_of(i * ck, ck), ck)
        e = jnp.exp2(s_ref[r, :] - m)
        s_ref[r, :] = e
        eb = e.astype(BF)
        e_ref[r, :] = eb
        return o + jnp.dot(vt_ref[:, r], eb, preferred_element_type=F32)
    o = lax.fori_loop(0, nck, p2, jnp.zeros((d + 16, tq), F32), unroll=un)
    inv = 1.0 / o[d:d+1, :]
    ot = o[:d] * inv
    ob = ot.T
    delta = jnp.sum(ob * do, axis=1, keepdims=True)
    invc = jnp.broadcast_to(inv, (8, tq)).T[:, 0:1]
    dh = (-delta).astype(BF); dr = -delta - dh.astype(F32)
    dm = dr.astype(BF); dl = (dr - dm.astype(F32)).astype(BF)
    lane = lax.broadcasted_iota(jnp.int32, (tq, d), 1)
    dd = jnp.where(lane == 0, dh.astype(F32), jnp.where(lane == 1, dm.astype(F32), jnp.where(lane == 2, dl.astype(F32), 0.0))).astype(BF)
    wd = jnp.concatenate([zeros, xb[:, 3*d:], dd], axis=1)
    gh, gl = split(do * invc)
    rh, rl = split(q * (invc * scale))
    none = zeros[:, :d]
    we = jnp.concatenate([none, gl, none, gh], axis=1)
    ws = jnp.concatenate([rl, none, rh, none], axis=1)
    def p3(i, dq):
        r = pl.ds(pl.multiple_of(i * ck, ck), ck)
        dp = lax.dot_general(a_ref[r, :], wd, NT, preferred_element_type=F32)
        ds = (s_ref[r, :] * dp).astype(BF)
        acc_ref[r, :] += (jnp.dot(ds, ws, preferred_element_type=F32)
                          + jnp.dot(e_ref[r, :], we, preferred_element_type=F32))
        return dq + jnp.dot(kt_ref[:, r], ds, preferred_element_type=F32)
    dq = lax.fori_loop(0, nck, p3, jnp.zeros((d, tq), F32), unroll=un)
    dq = dq * (inv * scale)
    o_ref[rows, 0:2*d] = jnp.concatenate([ot, dq], axis=0).T.astype(BF)
    @pl.when(step == pl.num_programs(0) - 1)
    def _():
        acc = acc_ref[...]
        acc = acc + pltpu.roll(acc, 2*d, 1)
        o_ref[:, 2*d:] = acc[:, 2*d:].astype(BF)

def attn(x, tq=768, ck=3840, un=1):
    tok = x.shape[0]
    return pl.pallas_call(
        functools.partial(attn_kernel, 1.0/math.sqrt(32), tq, ck, un),
        grid=(tok // tq,),
        in_specs=[pl.BlockSpec((tok, 128), lambda i: (0, 0))],
        out_specs=pl.BlockSpec((tok, 128), lambda i: (0, 0)),
        out_shape=pltpu.HBM((tok, 128), BF),
        scratch_shapes=[pltpu.VMEM((tok, 128), BF), pltpu.VMEM((32, tok), BF), pltpu.VMEM((48, tok), BF),
                        pltpu.VMEM((tok, tq), F32), pltpu.VMEM((tok, tq), BF), pltpu.VMEM((tok, 128), F32)],
        compiler_params=pltpu.CompilerParams(vmem_limit_bytes=48 << 20),
        cost_estimate=pl.CostEstimate(flops=6*2*tok*tok*128, bytes_accessed=4*tok*128, transcendentals=tok*tok),
    )(x)


LANES = 128
CALL = functools.partial(pltpu.CompilerParams, vmem_limit_bytes=40 << 20)


def cost(flops, moved):
    return pl.CostEstimate(flops=int(flops), bytes_accessed=int(moved), transcendentals=0)


def padded(plane):
    width, chans = plane.shape
    return jnp.concatenate([plane.astype(F32), jnp.zeros((LANES - width, chans), F32)], axis=0)


def pick_kernel(rows, act_ref, outer_ref, out_ref):
    group = out_ref.shape[0]
    frames, width, chans = act_ref.shape
    for f in range(frames):
        for at, src in ((f, act_ref), (frames + f, outer_ref)):
            plane = src[f].astype(F32)
            for c in range(2):
                parts = [plane[:, b + c * rows : b + (c + 1) * rows] for b in range(0, chans, 2 * rows)]
                part = jnp.concatenate(parts, axis=1).astype(BF)
                for x in range(group // 2):
                    out_ref[2 * x + c, at] = part


def pick(act, outer, rows):
    frames, width, chans = act.shape
    return pl.pallas_call(
        functools.partial(pick_kernel, rows),
        out_shape=jax.ShapeDtypeStruct((GROUP, 2 * frames, width, chans // 2), BF),
        compiler_params=CALL(),
        cost_estimate=cost(1e8, 3 << 20),
    )(act, outer)


def turn_kernel(r_ref, at_ref):
    group = r_ref.shape[0]
    frames = at_ref.shape[1]
    for f in range(frames):
        for row in range(group + 2):
            if row == 0:
                plane = r_ref[0, frames + f]
            elif row == group + 1:
                plane = r_ref[group - 1, frames + f]
            else:
                plane = r_ref[row - 1, f]
            tile = padded(plane).T
            cols = slice(row * LANES, (row + 1) * LANES)
            at_ref[0, f, :, cols] = pltpu.roll(tile, 1, 1).astype(BF)
            at_ref[1, f, :, cols] = tile.astype(BF)
            at_ref[2, f, :, cols] = pltpu.roll(tile, LANES - 1, 1).astype(BF)


def turn(r, frames):
    group, _, _, chans = r.shape
    return pl.pallas_call(
        turn_kernel,
        out_shape=pltpu.HBM((3, frames, chans, (group + 2) * LANES), BF),
        compiler_params=CALL(),
        cost_estimate=cost(1e9, 6 << 20),
    )(r)


def turn_pair_kernel(*refs):
    ins, outs = refs[:4], refs[4:]
    for own, other, out in ((ins[0], ins[1], outs[0]), (ins[2], ins[3], outs[1])):
        count = own.shape[0]
        for d, src in enumerate((own, other)):
            for f in range(count):
                at = (d * count + f) * LANES
                out[:, at : at + LANES] = padded(src[f]).T.astype(BF)


def turn_pair(own_r, other_r, own_b, other_b):
    chans = own_r.shape[-1]
    return pl.pallas_call(
        turn_pair_kernel,
        out_shape=tuple(
            pltpu.HBM((chans, 2 * x.shape[0] * LANES), BF) for x in (own_r, own_b)
        ),
        compiler_params=CALL(),
        cost_estimate=cost(1e9, 4 << 20),
    )(own_r, other_r, own_b, other_b)


def local_terms_kernel(line_ref, a0_ref, a1_ref, p1_ref, *refs):
    far, outs, scratch = refs[:5], refs[5:9], refs[9:]
    near, (at_ref, pay_ref, cot_ref, mix_ref, out_ref, sems) = scratch[:5], scratch[5:]
    rt_ref, bt_ref, p0_ref, c0_ref, c1_ref = near
    copies = [pltpu.make_async_copy(src, dst, sems.at[k]) for k, (src, dst) in enumerate(zip(far, near))]
    for at in (3, 4, 2, 0, 1):
        copies[at].start()
    frames, width, chans = a0_ref.shape
    half = chans // 2
    places = [(d, f, (d * frames + f) * LANES) for d in range(2) for f in range(frames)]
    for d, f, at in places:
        at_ref[:, at : at + LANES] = padded((a0_ref, a1_ref)[d][f]).T.astype(BF)
    parts, _, rows, _ = out_ref.shape
    block = parts * rows

    def put(first, value, lane=0):
        for n in range(value.shape[0] // block):
            for y in range(parts):
                at = n * block + y * rows
                out_ref[y, first + n, :, lane : lane + value.shape[1]] = value[at : at + rows].astype(BF)

    copies[3].wait()
    copies[4].wait()
    for d, f, at in places:
        cot_ref[at : at + LANES, :] = padded((c0_ref, c1_ref)[d][f]).astype(BF)
    put(6 * chans // block, jnp.dot(at_ref[...], cot_ref[...], preferred_element_type=F32))
    copies[2].wait()
    for d, f, at in places:
        pay_ref[at : at + LANES, :] = padded((p0_ref, p1_ref)[d][f]).astype(BF)
    copies[0].wait()
    for p in range(3):
        right = pay_ref[:, p * half : (p + 1) * half]
        for lane in range(0, half, LANES):
            value = jnp.dot(rt_ref[...], right[:, lane : lane + LANES], preferred_element_type=F32)
            mix_ref[lane // LANES, pl.ds(p, chans, stride=3), :] = value
    for lane in range(0, half, LANES):
        put(3 * chans // block, mix_ref[lane // LANES], lane)
    copies[1].wait()
    for k in range(3):
        acc = jnp.zeros((chans, half), F32)
        for d in range(2):
            left = bt_ref[:, (2 * d * frames + k) * LANES : (2 * d * frames + k + frames) * LANES]
            right = pay_ref[d * frames * LANES : (d + 1) * frames * LANES, 3 * half :]
            acc = acc + jnp.dot(left, right, preferred_element_type=F32)
        put(k * chans // block, acc)
    for k, out in enumerate(outs):
        out[...] = out_ref[lax.rem(line_ref[0] + k, parts)]


def local_terms(line, rt, bt, atted, pay, cot):
    frames, width, chans = atted[0].shape
    half = chans // 2
    span = 2 * frames * LANES
    piece = (7 * chans // 64, 16, half)
    far = (rt, bt, pay[0], cot[0], cot[1])
    return pl.pallas_call(
        local_terms_kernel,
        out_shape=(pltpu.HBM(piece, BF),) + (jax.ShapeDtypeStruct(piece, BF),) * 3,
        in_specs=[pl.BlockSpec(memory_space=pltpu.SMEM)]
        + [pl.BlockSpec(memory_space=pltpu.VMEM)] * 3
        + [pl.BlockSpec(memory_space=pltpu.HBM)] * 5,
        scratch_shapes=[pltpu.VMEM(x.shape, BF) for x in far]
        + [
            pltpu.VMEM((chans, span), BF),
            pltpu.VMEM((span, 4 * half), BF),
            pltpu.VMEM((span, half), BF),
            pltpu.VMEM((half // LANES, 3 * chans, LANES), F32),
            pltpu.VMEM((4,) + piece, BF),
            pltpu.SemaphoreType.DMA((5,)),
        ],
        compiler_params=CALL(),
        cost_estimate=cost(2e9, 10 << 20),
    )(line, *atted, pay[1], *[pltpu.with_memory_space_constraint(v, pltpu.HBM) for v in far])


def conv_terms_kernel(at_ref, dpre_ref, *refs):
    parts, (out_ref, dp_ref, acc_ref, part_ref, sems) = refs[:4], refs[4:]
    step = pl.program_id(0)
    group, _, width, cols = dpre_ref.shape
    shifts, _, chans, _ = at_ref.shape
    rows = out_ref.shape[1]
    blocks = chans // rows
    copies = [pltpu.make_async_copy(src, part_ref.at[k], sems.at[k]) for k, src in enumerate(parts)]

    @pl.when(step == 0)
    def _():
        for copy in copies:
            copy.start()

    for row in range(group):
        dp_ref[row * LANES : (row + 1) * LANES, :] = padded(dpre_ref[row, 0]).astype(BF)
    span = group * LANES

    def product(i):
        left = at_ref[:, 0, :, i * LANES : i * LANES + span].reshape(shifts * chans, span)
        return jnp.dot(left, dp_ref[...], preferred_element_type=F32)

    @pl.when(step == 0)
    def _():
        for i in range(3):
            acc_ref[i] = product(i)

    @pl.when(step == 1)
    def _():
        for i in range(3):
            value = (acc_ref[i] + product(i)).astype(BF)
            for b in range(shifts * blocks):
                out_ref[i * shifts * blocks + b] = value[b * rows : (b + 1) * rows]
        for copy in copies:
            copy.wait()
        for n in range(part_ref.shape[1]):
            value = part_ref[0, n].astype(F32)
            for k in range(1, 4):
                value = value + part_ref[k, n].astype(F32)
            value = value.astype(BF)
            out_ref[3 * shifts * blocks + n] = jnp.concatenate([value[:, :cols], value[:, cols:]], axis=0)


def conv_terms(at, dpre, parts, owners, rows):
    group, frames, width, cols = dpre.shape
    shifts, _, chans, lanes = at.shape
    assert frames == 2
    return pl.pallas_call(
        conv_terms_kernel,
        grid=(frames,),
        in_specs=[
            pl.BlockSpec((shifts, 1, chans, lanes), lambda f: (0, f, 0, 0)),
            pl.BlockSpec((group, 1, width, cols), lambda f: (0, f, 0, 0)),
        ]
        + [pl.BlockSpec(memory_space=pl.ANY)] * 4,
        out_specs=pl.BlockSpec((owners, rows, cols), lambda f: (0, 0, 0)),
        out_shape=jax.ShapeDtypeStruct((owners, rows, cols), BF),
        scratch_shapes=[
            pltpu.VMEM((group * LANES, cols), BF),
            pltpu.VMEM((3, shifts * chans, cols), F32),
            pltpu.VMEM((4,) + parts[0].shape, BF),
            pltpu.SemaphoreType.DMA((4,)),
        ],
        compiler_params=pltpu.CompilerParams(vmem_limit_bytes=60 << 20),
        cost_estimate=cost(2e9, 10 << 20),
    )(at, dpre, *parts)


def sum_kernel(norm, dims, which_ref, terms_ref, out_ref):
    times, ys, xs = dims
    rows, cols = terms_ref.shape[1:]

    @pl.when(which_ref[0] == 1)
    def _():
        for x in range(xs):
            for c in range(2):
                acc = jnp.zeros((rows, cols), F32)
                for t in range(times):
                    for y in range(ys):
                        acc = acc + terms_ref[((t * ys + y) * xs + x) * 2 + c].astype(F32)
                out_ref[c * rows : (c + 1) * rows, x * cols : (x + 1) * cols] = acc * norm

    @pl.when(which_ref[0] == 0)
    def _():
        part = rows // 2
        for y in range(ys):
            for c in range(2):
                acc = jnp.zeros((rows, cols), F32)
                for t in range(times):
                    for x in range(xs):
                        acc = acc + terms_ref[((t * ys + y) * xs + x) * 2 + c].astype(F32)
                acc = acc * norm
                for h in range(2):
                    at = (2 * c + h) * cols
                    out_ref[y * part : (y + 1) * part, at : at + cols] = acc[h * part : (h + 1) * part]


def sum_terms(which, terms, norm, dims):
    owners, rows, cols = terms.shape
    return pl.pallas_call(
        functools.partial(sum_kernel, norm, dims),
        out_shape=jax.ShapeDtypeStruct((2 * rows, 4 * cols), F32),
        in_specs=[pl.BlockSpec(memory_space=pltpu.SMEM), pl.BlockSpec(memory_space=pltpu.VMEM)],
        compiler_params=CALL(),
        cost_estimate=cost(1e7, 1 << 20),
    )(which, terms)


def dpre_kernel(own_ref, next_ref, slope_ref, tw_ref, dpre_ref, near_ref):
    frames, width, chans = own_ref.shape
    group, _, _, cols = near_ref.shape
    ext = [own_ref[f] for f in range(frames)] + [next_ref[f] for f in range(frames)]
    for f in range(frames):
        acc = jnp.zeros((width, chans), F32)
        for k in range(3):
            acc = acc + dot_nt(ext[f + 2 - k], tw_ref[k * chans : (k + 1) * chans, :])
        value = (acc * slope_ref[f]).astype(BF)
        dpre_ref[f] = value
        for e in range(group):
            near_ref[e, f] = value[:, (e // 2) * cols : (e // 2 + 1) * cols]


def make_dpre(own, nxt, slope, tw):
    frames, width, chans = own.shape
    return pl.pallas_call(
        dpre_kernel,
        out_shape=(
            pltpu.HBM((frames, width, chans), BF),
            jax.ShapeDtypeStruct((GROUP, frames, width, 2 * chans // GROUP), BF),
        ),
        compiler_params=CALL(),
        cost_estimate=cost(5e8, 3 << 20),
    )(own, nxt, slope, tw)


def dact_kernel(mid_ref, above_ref, below_ref, dres_ref, x_ref, sw_ref, out_ref):
    frames, width, chans = mid_ref.shape
    line = lax.broadcasted_iota(jnp.int32, (width, chans), 0)
    for f in range(frames):
        acc = jnp.zeros((width, chans), F32)
        for i, src in enumerate((below_ref, mid_ref, above_ref)):
            plane = src[f]
            wide = plane.astype(F32)
            right = jnp.where(line == width - 1, 0.0, pltpu.roll(wide, width - 1, 0)).astype(BF)
            left = jnp.where(line == 0, 0.0, pltpu.roll(wide, 1, 0)).astype(BF)
            for j, value in enumerate((right, plane, left)):
                tap = 3 * i + j
                acc = acc + dot_nt(value, sw_ref[tap * chans : (tap + 1) * chans, :])
        x = x_ref[f].astype(F32)
        sigma = 1.0 / (1.0 + jnp.exp(-x))
        slope = sigma * (1.0 + x * (1.0 - sigma))
        out_ref[f] = (dres_ref[f] + acc * slope).astype(BF)


def make_grad_latents(mid, above, below, dres, x, sw):
    return pl.pallas_call(
        dact_kernel,
        out_shape=jax.ShapeDtypeStruct(mid.shape, BF),
        compiler_params=CALL(),
        cost_estimate=cost(2e9, 8 << 20),
    )(mid, above, below, dres, x, sw)


def silu_slope(value):
    sigma = jax.nn.sigmoid(value)
    return sigma * (1.0 + value * (1.0 - sigma))


def matmul(left, right):
    return jnp.dot(left, right, preferred_element_type=F32)


def shift(x, axis, by):
    count = lax.axis_size(axis)
    pairs = [(i, i + by) for i in range(count) if 0 <= i + by < count]
    return lax.ppermute(x, axis, pairs)


def swap(x):
    count = lax.axis_size("space")
    return lax.ppermute(x, "space", [(i, i ^ 1) for i in range(count)])


def neighbours(field):
    return shift(field, "space", 1), shift(field, "space", -1)


def exchange(x):
    count = lax.axis_size("space")
    groups = [list(range(at, at + GROUP)) for at in range(0, count, GROUP)]
    return lax.all_to_all(x, "space", 0, 0, axis_index_groups=groups, tiled=True)


def along_y(x, by):
    count = lax.axis_size("space")
    return lax.ppermute(x, "space", [(i, (i + by * GROUP) % count) for i in range(count)])


def pick_one(x, index):
    return lax.dynamic_index_in_dim(x, index, 0, keepdims=False)


def side_pad(field):
    return jnp.pad(field, ((0, 0), (0, 0), (1, 1), (0, 0)))


def taps_of(padded, width):
    pieces = [padded[:, i, j : j + width] for i in range(3) for j in range(3)]
    return jnp.concatenate(pieces, axis=-1).reshape(-1, 9 * padded.shape[-1])


def per_device(latents, spatial_weight, temporal_weight, qkv_weight, out_weight, cotangent):
    frames, rows, width, chans = latents.shape
    ntok = frames * width
    n_space = lax.axis_size("space")
    n_time = lax.axis_size("tm")
    owners = n_space * n_time
    depth = chans // HEADS
    norm = 1.0 / math.sqrt(ntok * n_space * n_time)
    here = lax.axis_index("space")
    core, line = here % 2, here // GROUP
    half = chans // 2
    share = 16 * chans // (2 * owners)

    x = latents.reshape(frames, width, chans)
    cot = cotangent.reshape(frames, width, chans)
    act = jax.nn.silu(x.astype(F32)).astype(BF)
    above, below = neighbours(act)
    pre = matmul(taps_of(side_pad(jnp.stack([above, act, below], axis=1)), width), spatial_weight)
    pre = pre.reshape(frames, width, chans)
    bact = jax.nn.silu(pre).astype(BF)
    bext = jnp.concatenate([shift(bact, "tm", 1), bact], axis=0)
    resid, rres, items = proj(x, bext, cot, temporal_weight, qkv_weight, out_weight)
    items = items.reshape(frames * HEADS, width, 4 * depth)
    items = lax.all_to_all(items, "space", 0, 0, tiled=True)

    early = pick(act, jnp.where(here % GROUP == 0, above, below), share)
    chalf = cot.reshape(frames, width, 2, half).transpose(2, 0, 1, 3)
    cpair = (pick_one(chalf, core), swap(pick_one(chalf, 1 - core)))
    rother, bother = swap(rres), swap(bext)
    early, cpair, rother, bother, items = lax.optimization_barrier((early, cpair, rother, bother, items))
    early = exchange(early)
    outs = attn(items.reshape(n_space * width, 4 * depth)).reshape(n_space, width, 4 * depth)
    outs, early, rother, bother = lax.optimization_barrier((outs, early, rother, bother))
    outs = lax.all_to_all(outs, "space", 0, 0, tiled=True)
    aturn = turn(early, frames)
    rturn, bturn = turn_pair(rres, rother, bext, bother)
    slope = silu_slope(pre)
    outs, aturn, rturn, bturn, slope = lax.optimization_barrier((outs, aturn, rturn, bturn, slope))

    core_at = core.astype(jnp.int32).reshape(1)
    outs = outs.reshape(frames, HEADS, width, 4 * depth)
    atted, dres, dresb, mine, other = post(core_at, outs, cot, qkv_weight)
    dnext = shift(dresb, "tm", -1)
    local = local_terms(line.astype(jnp.int32).reshape(1), rturn, bturn, (atted, swap(atted)), (mine, swap(other)), cpair)
    slope, _ = lax.optimization_barrier((slope, local[0]))
    dpre, near = make_dpre(dresb, dnext, slope, temporal_weight)
    near = exchange(near)
    dabove, dbelow = neighbours(dpre)
    parts = [along_y(local[by], by) for by in (2, 1, 3)] + [local[0]]
    mixed = resid.reshape(ntok, chans) + matmul(atted.reshape(ntok, chans), out_weight)
    mixed = mixed.astype(BF).reshape(latents.shape)
    mixed, near = lax.optimization_barrier((mixed, near))
    terms = conv_terms(aturn, near, parts, owners, share)
    terms, dpre, dabove, dbelow = lax.optimization_barrier((terms, dpre, dabove, dbelow))
    terms = lax.all_to_all(terms, ("tm", "space"), 0, 0, tiled=True)
    grad_latents = make_grad_latents(dpre, dabove, dbelow, dres, x, spatial_weight).reshape(latents.shape)
    index = lax.axis_index("tm") * n_space + here
    which = (index < 9 * chans // (2 * share)).astype(jnp.int32).reshape(1)
    grad_weights = sum_terms(which, terms, norm, (n_time, n_space // GROUP, GROUP // 2))
    return (mixed, grad_latents, grad_weights)


def solution(mesh):
    placed = (P("tm", "space", None, None), P(), P(), P(), P(), P("tm", "space", None, None))
    return jax.shard_map(
        per_device,
        mesh=mesh,
        in_specs=placed,
        out_specs=(
            P("tm", "space", None, None),
            P("tm", "space", None, None),
            P(("tm", "space"), None),
        ),
        check_vma=False,
    )
```
